32 devices in a mesh: grp: 2 (over y), sp: 4 (over x, core), ch: 4 (over z).
Axes of the slice: x: 2, y: 2, z: 4, core: 2. Of those that a mesh axis runs over, the one named last changes fastest.
Arguments:
- features: bfloat16 [256, 8, 640], P('ch', ('grp', 'sp')), parts along dimension 1, may hold values from -6 to 6
- weights: bfloat16 [27, 256, 256], P(None, 'ch'), may hold values from -0.109375 to 0.109375
- cotangent: bfloat16 [256, 8, 640], P('ch', ('grp', 'sp')), parts along dimension 1, may hold values from -6 to 6
Outputs:
- output: float32 [256, 8, 640], P('ch', ('grp', 'sp')), parts along dimension 1
- input_grad: float32 [256, 8, 640], P('ch', ('grp', 'sp')), parts along dimension 1
- weight_grad: float32 [54, 256, 256], P('grp', 'ch', 'sp'), parts along dimension 0
The draws below stay inside these ranges and needn't reach their ends.
There are 2 independent parts, one for each index of `grp`. The reference program is written for one: setup_inputs(seed, part) draws one part's arguments, and reference() takes and returns one part's arrays. A program takes and returns all parts, laid end to end along the dimension named above; an argument that names none is the same for every part. Nothing has to cross between parts.
All inputs are finite; a program needn't handle non-finite values.
Results may differ from the reference program's by a relative error of at most 0.0003.
Values may be sent and summed in bfloat16 or wider, within the bound.
No kernel may reach another device: no remote copies, remote signals or barrier semaphores. Data moves between devices by JAX's collectives and lax.ppermute only.
A program may use at most 64 MiB of HBM per device.

```python
import math
import jax
import jax.numpy as jnp
from jax import lax

C = 256
NX = 64
NY = 10
NZ = 4


def with_spikes(entries, own_key, source, target, parts, factor):
    def block_of(dim):
        return (jnp.arange(entries.shape[dim]) // (entries.shape[dim] // parts)).reshape((-1,) + (1,) * (entries.ndim - 1 - dim))

    near = jax.random.permutation(own_key, parts)[block_of(target)]
    second = (block_of(target) + parts // 2) % parts
    return jnp.where((block_of(source) == near) | (block_of(source) == second), factor * entries, entries)


def shard_levels(stream_key, shape, shards, least, largest):
    gain, own = 1.0, jax.random.fold_in(stream_key, 6)
    for position, parts in shards:
        steps = jnp.exp(jax.random.uniform(jax.random.fold_in(own, position), (parts,), jnp.float32, least / len(shards), largest / len(shards)))
        gain = gain * jnp.repeat(steps, shape[position] // parts).reshape([-1 if axis == position else 1 for axis in range(len(shape))])
    return gain


def scatter_about(key, dims, scale, reach, shards=(), held_as=jnp.bfloat16):
    result = jax.random.normal(key, dims, jnp.float32) * scale
    if len(shards) > 0:
        result = shard_levels(key, dims, shards, -0.22, 0.18) * result
    return jnp.clip(result, min=-reach, max=reach).astype(held_as)


def bell_draw_with(stream_key, dims, spread, most, cuts, heavy, dtype=jnp.bfloat16):
    values = spread * jax.random.normal(stream_key, dims, jnp.float32)
    if cuts:
        values = values * shard_levels(stream_key, dims, cuts, -0.22, 0.18)
    return jnp.clip(with_spikes(values, jax.random.fold_in(stream_key, 3), *heavy), -most, most).astype(dtype)


def setup_inputs(seed: int = 0, part: int = 0) -> dict:
    arg_keys = jax.random.split(jax.random.key(seed), 4)
    own_keys = jax.random.split(jax.random.fold_in(arg_keys[3], part), 4)
    features = bell_draw_with(own_keys[0], (C, NZ, NY * NX), 1.0, 6.0, ((0, 4), (1, 4)), (1, 0, 4, 2.0))
    weights = bell_draw_with(arg_keys[1], (27, C, C), (27 * C) ** -0.5, 0.109375, ((1, 4),), (1, 2, 4, 2.0))
    cotangent = scatter_about(own_keys[2], (C, NZ, NY * NX), 1.0, 6.0, ((0, 4), (1, 4)))
    return dict(features=features, weights=weights, cotangent=cotangent)


def moved_field(padded, dz, dy, dx):
    count = padded.shape[0]
    part = padded[:, 1 + dz:1 + dz + NZ, 1 + dy:1 + dy + NY, 1 + dx:1 + dx + NX]
    return part.reshape(count, NZ * NY * NX)

def reference(features, weights, cotangent):
    chans = features.shape[0]
    pad_width = ((0, 0), (1, 1), (1, 1), (1, 1))
    padded_in = jnp.pad(features.reshape(chans, NZ, NY, NX), pad_width)
    padded_grad = jnp.pad(cotangent.reshape(chans, NZ, NY, NX), pad_width)
    flat_grad = cotangent.reshape(chans, NZ * NY * NX)
    total = jnp.zeros((chans, NZ * NY * NX), jnp.float32)
    back = jnp.zeros((chans, NZ * NY * NX), jnp.float32)
    filters = []
    for tap in range(27):
        dz = tap // 9 - 1
        dy = tap // 3 % 3 - 1
        dx = tap % 3 - 1
        moved = moved_field(padded_in, dz, dy, dx)
        total = total + jnp.dot(weights[tap], moved, preferred_element_type=jnp.float32)
        filters.append(lax.dot_general(flat_grad, moved, (((1,), (1,)), ((), ())), preferred_element_type=jnp.float32))
        opposite = moved_field(padded_grad, -dz, -dy, -dx)
        back = back + lax.dot_general(weights[tap], opposite, (((0,), (0,)), ((), ())), preferred_element_type=jnp.float32)
    factor = 1.0 / math.sqrt(NZ * NY * NX)
    output = total.reshape(chans, NZ, NY * NX)
    input_grad = back.reshape(chans, NZ, NY * NX)
    weight_grad = jnp.stack(filters) * factor
    return (output, input_grad, weight_grad)
```

```python
import functools
import math

import jax
import jax.numpy as jnp
from jax import lax
from jax.experimental import pallas as pl
from jax.experimental.pallas import tpu as pltpu
from jax.sharding import PartitionSpec as P

NX = 64
NY = 10
CELLS = NX * NY
F32 = jnp.float32
BF16 = jnp.bfloat16
VMEM_BYTES = 48 * 1024 * 1024


def cell_mask(rows, dy, dx):
    q = lax.broadcasted_iota(jnp.int32, (rows, CELLS), 1)
    x = q % NX + dx
    y = q // NX + dy
    return (x >= 0) & (x < NX) & (y >= 0) & (y < NY)


def shifted(value, dy, dx):
    if dy == 0 and dx == 0:
        return value
    moved = pltpu.roll(value, (-(dy * NX + dx)) % CELLS, 1)
    return jnp.where(cell_mask(value.shape[0], dy, dx), moved, 0.0)


def input_grad_kernel(nz, pos_ref, cot_all_ref, w_ref, part_ref, cols_ref):
    blocks = cot_all_ref.shape[1]
    s = pos_ref[0]
    for dz in (-1, 0, 1):
        source = s - dz
        inside = (source >= 0) & (source < nz)
        plane = cot_all_ref[jnp.clip(source, 0, nz - 1)].astype(F32)
        plane = jnp.where(inside, plane, 0.0)
        for dy in (-1, 0, 1):
            for dx in (-1, 0, 1):
                tap = 9 * (dz + 1) + 3 * (dy + 1) + dx + 1
                cols_ref[tap * blocks : (tap + 1) * blocks, :] = shifted(plane, -dy, -dx).astype(BF16)
    part_ref[...] = lax.dot_general(
        w_ref[...], cols_ref[...], (((0,), (0,)), ((), ())), preferred_element_type=F32
    )


def output_kernel(nz, scale, fm_ref, f0_ref, fp_ref, w_ref, cot_all_ref, fblk_ref, out_ref, wg_ref):
    blocks = cot_all_ref.shape[1]
    cols = fblk_ref.shape[1]
    taps = 9 * blocks
    acc = None
    for dz, ref in ((-1, fm_ref), (0, f0_ref), (1, fp_ref)):
        term = jnp.dot(
            w_ref[(dz + 1) * taps : (dz + 2) * taps, :], ref[...], preferred_element_type=F32
        )
        acc = term if acc is None else acc + term
    total = None
    for dx in (-1, 0, 1):
        for dy in (-1, 0, 1):
            at = (3 * (dy + 1) + dx + 1) * blocks
            term = shifted(acc[at : at + blocks], dy, dx)
            total = term if total is None else total + term
    out_ref[:, 0, :] = total

    cots = []
    feats = []
    for z in range(nz):
        plane = cot_all_ref[z].astype(F32)
        cots.append([shifted(plane, -dy, 0).astype(BF16) for dy in (-1, 0, 1)])
        field = fblk_ref[z].astype(F32)
        feats.append(jnp.concatenate([shifted(field, 0, dx).astype(BF16) for dx in (-1, 0, 1)], 0))
    for dz in (-1, 0, 1):
        sums = None
        for z in range(nz):
            if 0 <= z - dz < nz:
                term = lax.dot_general(
                    jnp.concatenate(cots[z - dz], 0),
                    feats[z],
                    (((1,), (1,)), ((), ())),
                    preferred_element_type=F32,
                )
                sums = term if sums is None else sums + term
        if sums is None:
            sums = jnp.zeros((3 * blocks, 3 * cols), F32)
        sums = sums * scale
        for dy in range(3):
            for dx in range(3):
                tap = 9 * (dz + 1) + 3 * dy + dx
                wg_ref[tap] = sums[dy * blocks : (dy + 1) * blocks, dx * cols : (dx + 1) * cols]


def per_device(features, weights, cotangent):
    blocks, depth, plane = features.shape
    channels = weights.shape[2]
    nz = lax.axis_size("sp")
    cols = channels // nz
    w2 = weights.reshape(27 * blocks, channels)
    feat = features.reshape(blocks, plane)
    cot = cotangent.reshape(blocks, plane)

    cot_all = lax.all_gather(cot, "sp", axis=0)
    f_all = lax.all_gather(feat, "ch", axis=0, tiled=True)
    pos = lax.axis_index("sp").astype(jnp.int32).reshape(1)

    vmem = pl.BlockSpec(memory_space=pltpu.VMEM)
    smem = pl.BlockSpec(memory_space=pltpu.SMEM)
    params = pltpu.CompilerParams(vmem_limit_bytes=VMEM_BYTES)
    part = pl.pallas_call(
        functools.partial(input_grad_kernel, nz),
        out_shape=jax.ShapeDtypeStruct((channels, plane), F32),
        in_specs=[smem, vmem, vmem],
        out_specs=vmem,
        scratch_shapes=[pltpu.VMEM((27 * blocks, plane), BF16)],
        compiler_params=params,
        cost_estimate=pl.CostEstimate(
            flops=2 * 27 * blocks * channels * plane, bytes_accessed=2000000, transcendentals=0
        ),
        name="input_grad",
    )(pos, cot_all, w2)
    back = lax.psum_scatter(part, "ch", scatter_dimension=0, tiled=True)

    up = [(i, i + 1) for i in range(nz - 1)]
    down = [(i + 1, i) for i in range(nz - 1)]
    before = lax.ppermute(f_all, "sp", up)
    after = lax.ppermute(f_all, "sp", down)
    fblk = lax.all_to_all(f_all.reshape(nz, cols, plane), "sp", 0, 0)

    scale = 1.0 / math.sqrt(nz * depth * plane)
    output, weight_grad = pl.pallas_call(
        functools.partial(output_kernel, nz, scale),
        out_shape=(
            jax.ShapeDtypeStruct((blocks, 1, plane), F32),
            jax.ShapeDtypeStruct((27, blocks, cols), F32),
        ),
        in_specs=[vmem] * 6,
        out_specs=(vmem, vmem),
        compiler_params=params,
        cost_estimate=pl.CostEstimate(
            flops=4 * 27 * blocks * channels * plane, bytes_accessed=4000000, transcendentals=0
        ),
        name="output_and_weight_grad",
    )(before, f_all, after, w2, cot_all, fblk)
    return (output, back.reshape(blocks, depth, plane), weight_grad)


def solution(mesh):
    return jax.shard_map(
        per_device,
        mesh=mesh,
        in_specs=(P("ch", ("grp", "sp"), None), P(None, "ch", None), P("ch", ("grp", "sp"), None)),
        out_specs=(
            P("ch", ("grp", "sp"), None),
            P("ch", ("grp", "sp"), None),
            P("grp", "ch", "sp"),
        ),
        check_vma=False,
    )
```

```python
import functools
import math

import jax
import jax.numpy as jnp
from jax import lax
from jax.experimental import pallas as pl
from jax.experimental.pallas import tpu as pltpu
from jax.sharding import PartitionSpec as P

NX = 64
NY = 10
CELLS = NX * NY
F32 = jnp.float32
BF16 = jnp.bfloat16
VMEM_BYTES = 48 * 1024 * 1024


def cell_mask(rows, dy, dx):
    q = lax.broadcasted_iota(jnp.int32, (rows, CELLS), 1)
    x = q % NX + dx
    y = q // NX + dy
    return (x >= 0) & (x < NX) & (y >= 0) & (y < NY)


def shifted(value, dy, dx):
    if dy == 0 and dx == 0:
        return value
    moved = pltpu.roll(value, (-(dy * NX + dx)) % CELLS, 1)
    return jnp.where(cell_mask(value.shape[0], dy, dx), moved, 0.0)


def gather_kernel(nz, nc, pos_ref, cot_ref, *refs):
    pieces = refs[:nc]
    f_ref = refs[nc]
    packs = refs[nc + 1 :]
    blocks = cot_ref.shape[0]
    cols = f_ref.shape[0] // nz
    s, c = pos_ref[0], pos_ref[1]
    for k in range(nc):
        owner = lax.rem(c + nc - k, nc)
        f_ref[pl.ds(pl.multiple_of(owner * blocks, blocks), blocks), :] = pieces[k][...]
    for k, pack in zip(range(2, nz), packs):
        goal = lax.rem(s + k, nz) if k < nz - 1 else nz - 1 - s
        goal = jnp.clip(goal, 0, nz - 1)
        pack[:cols, :] = f_ref[pl.ds(pl.multiple_of(goal * cols, cols), cols), :]
        pack[cols:, :] = cot_ref[...]


def input_grad_kernel(nc, pos_ref, before_ref, cot_ref, after_ref, w_ref, *refs):
    parts = refs[:nc]
    cols_ref, sum_ref = refs[nc:]
    blocks = cot_ref.shape[0]
    c = pos_ref[1]
    for dz, ref in ((-1, after_ref), (0, cot_ref), (1, before_ref)):
        plane = ref[...].astype(F32)
        for dy in (-1, 0, 1):
            for dx in (-1, 0, 1):
                tap = 9 * (dz + 1) + 3 * (dy + 1) + dx + 1
                cols_ref[tap * blocks : (tap + 1) * blocks, :] = shifted(plane, -dy, -dx).astype(BF16)
    sum_ref[...] = lax.dot_general(
        w_ref[...], cols_ref[...], (((0,), (0,)), ((), ())), preferred_element_type=F32
    )
    for k in range(nc):
        goal = lax.rem(c + k, nc)
        parts[k][...] = sum_ref[pl.ds(pl.multiple_of(goal * blocks, blocks), blocks), :]


def output_kernel(nz, scale, pos_ref, w_ref, cot_ref, cm_ref, cp_ref, f0_ref, fm_ref, fp_ref, *refs):
    packs = refs[: nz - 2]
    out_ref, wg_ref, c_ref, g_ref = refs[nz - 2 :]
    blocks = cot_ref.shape[0]
    cols = g_ref.shape[1]
    taps = 9 * blocks
    s = pos_ref[0]
    acc = None
    for dz, ref in ((-1, fm_ref), (0, f0_ref), (1, fp_ref)):
        term = jnp.dot(
            w_ref[(dz + 1) * taps : (dz + 2) * taps, :], ref[...], preferred_element_type=F32
        )
        acc = term if acc is None else acc + term
    total = None
    for dx in (-1, 0, 1):
        for dy in (-1, 0, 1):
            at = (3 * (dy + 1) + dx + 1) * blocks
            term = shifted(acc[at : at + blocks], dy, dx)
            total = term if total is None else total + term
    out_ref[:, 0, :] = total

    mine = pl.ds(pl.multiple_of(s * cols, cols), cols)
    c_ref[s] = cot_ref[...]
    g_ref[s] = f0_ref[mine, :]

    @pl.when(s > 0)
    def _():
        c_ref[s - 1] = cm_ref[...]
        g_ref[s - 1] = fm_ref[mine, :]

    @pl.when(s < nz - 1)
    def _():
        c_ref[s + 1] = cp_ref[...]
        g_ref[s + 1] = fp_ref[mine, :]

    for k, pack in zip(range(2, nz - 1), packs):
        source = lax.rem(s + nz - k, nz)
        c_ref[source] = pack[cols:, :]
        g_ref[source] = pack[:cols, :]

    @pl.when((s == 0) | (s == nz - 1))
    def _():
        source = nz - 1 - s
        c_ref[source] = packs[-1][cols:, :]
        g_ref[source] = packs[-1][:cols, :]

    cots = []
    feats = []
    for z in range(nz):
        plane = c_ref[z].astype(F32)
        cots.append([shifted(plane, -dy, 0).astype(BF16) for dy in (-1, 0, 1)])
        field = g_ref[z].astype(F32)
        feats.append(jnp.concatenate([shifted(field, 0, dx).astype(BF16) for dx in (-1, 0, 1)], 0))
    for dz in (-1, 0, 1):
        sums = None
        for z in range(nz):
            if 0 <= z - dz < nz:
                term = lax.dot_general(
                    jnp.concatenate(cots[z - dz], 0),
                    feats[z],
                    (((1,), (1,)), ((), ())),
                    preferred_element_type=F32,
                )
                sums = term if sums is None else sums + term
        sums = sums * scale
        for dy in range(3):
            for dx in range(3):
                tap = 9 * (dz + 1) + 3 * dy + dx
                wg_ref[tap] = sums[dy * blocks : (dy + 1) * blocks, dx * cols : (dx + 1) * cols]


def total_kernel(*refs):
    total = refs[0][...]
    for ref in refs[1:-1]:
        total = total + ref[...]
    refs[-1][:, 0, :] = total


VMEM = pl.BlockSpec(memory_space=pltpu.VMEM)
SMEM = pl.BlockSpec(memory_space=pltpu.SMEM)


def kernel_call(body, name, outs, args, scratch=(), flops=0):
    moved = sum(math.prod(a.shape) * a.dtype.itemsize for a in args + outs)
    return pl.pallas_call(
        body,
        out_shape=outs,
        in_specs=[SMEM if a.dtype == jnp.int32 else VMEM for a in args],
        out_specs=tuple(VMEM for _ in outs),
        scratch_shapes=list(scratch),
        compiler_params=pltpu.CompilerParams(vmem_limit_bytes=VMEM_BYTES),
        cost_estimate=pl.CostEstimate(flops=flops, bytes_accessed=moved, transcendentals=0),
        name=name,
    )(*args)


def per_device(features, weights, cotangent):
    blocks, depth, plane = features.shape
    channels = weights.shape[2]
    nz = lax.axis_size("sp")
    nc = lax.axis_size("ch")
    cols = channels // nz
    w2 = weights.reshape(27 * blocks, channels)
    feat = features.reshape(blocks, plane)
    cot = cotangent.reshape(blocks, plane)
    pos = jnp.stack([lax.axis_index("sp"), lax.axis_index("ch")]).astype(jnp.int32)

    def turn(count, k):
        return [(i, (i + k) % count) for i in range(count)]

    up = [(i, i + 1) for i in range(nz - 1)]
    down = [(i + 1, i) for i in range(nz - 1)]
    field = jax.ShapeDtypeStruct((blocks, plane), BF16)
    wide = jax.ShapeDtypeStruct((blocks, plane), F32)

    cot_before = lax.ppermute(cot, "sp", up)
    cot_after = lax.ppermute(cot, "sp", down)
    pieces = [feat] + [lax.ppermute(feat, "ch", turn(nc, k)) for k in range(1, nc)]

    parts = kernel_call(
        functools.partial(input_grad_kernel, nc),
        "input_grad",
        [wide] * nc,
        [pos, cot_before, cot, cot_after, w2],
        [pltpu.VMEM((27 * blocks, plane), BF16), pltpu.VMEM((channels, plane), F32)],
        2 * 27 * blocks * channels * plane,
    )
    terms = [parts[0]] + [lax.ppermute(parts[k], "ch", turn(nc, k)) for k in range(1, nc)]

    packed = jax.ShapeDtypeStruct((cols + blocks, plane), BF16)
    f_all, *packs = kernel_call(
        functools.partial(gather_kernel, nz, nc),
        "gather",
        [jax.ShapeDtypeStruct((channels, plane), BF16)] + [packed] * (nz - 2),
        [pos, cot] + pieces,
    )
    f_before = lax.ppermute(f_all, "sp", up)
    f_after = lax.ppermute(f_all, "sp", down)
    far = [lax.ppermute(packs[k - 2], "sp", turn(nz, k)) for k in range(2, nz - 1)]
    far.append(lax.ppermute(packs[-1], "sp", [(0, nz - 1), (nz - 1, 0)]))

    output, weight_grad = kernel_call(
        functools.partial(output_kernel, nz, 1.0 / math.sqrt(nz * depth * plane)),
        "output_and_weight_grad",
        [
            jax.ShapeDtypeStruct((blocks, 1, plane), F32),
            jax.ShapeDtypeStruct((27, blocks, cols), F32),
        ],
        [pos, w2, cot, cot_before, cot_after, f_all, f_before, f_after] + far,
        [pltpu.VMEM((nz, blocks, plane), BF16), pltpu.VMEM((nz, cols, plane), BF16)],
        4 * 27 * blocks * channels * plane,
    )
    (back,) = kernel_call(
        total_kernel, "total", [jax.ShapeDtypeStruct((blocks, 1, plane), F32)], terms
    )
    return (output, back, weight_grad)


def solution(mesh):
    return jax.shard_map(
        per_device,
        mesh=mesh,
        in_specs=(P("ch", ("grp", "sp"), None), P(None, "ch", None), P("ch", ("grp", "sp"), None)),
        out_specs=(
            P("ch", ("grp", "sp"), None),
            P("ch", ("grp", "sp"), None),
            P("grp", "ch", "sp"),
        ),
        check_vma=False,
    )
```

```python
import functools
import math

import jax
import jax.numpy as jnp
from jax import lax
from jax.experimental import pallas as pl
from jax.experimental.pallas import tpu as pltpu
from jax.sharding import PartitionSpec as P

NX = 64
NY = 10
CELLS = NX * NY
F32 = jnp.float32
BF16 = jnp.bfloat16
VMEM_BYTES = 48 * 1024 * 1024


def cell_mask(rows, dy, dx):
    q = lax.broadcasted_iota(jnp.int32, (rows, CELLS), 1)
    x = q % NX + dx
    y = q // NX + dy
    return (x >= 0) & (x < NX) & (y >= 0) & (y < NY)


def shifted(value, dy, dx):
    if dy == 0 and dx == 0:
        return value
    moved = pltpu.roll(value, (-(dy * NX + dx)) % CELLS, 1)
    return jnp.where(cell_mask(value.shape[0], dy, dx), moved, 0.0)


def gather_kernel(nz, nc, pos_ref, cot_ref, *refs):
    pieces = refs[:nc]
    f_ref = refs[nc]
    packs = refs[nc + 1 :]
    blocks = cot_ref.shape[0]
    cols = f_ref.shape[0] // nz
    s, c = pos_ref[0], pos_ref[1]
    for k in range(nc):
        owner = lax.rem(c + nc - k, nc)
        f_ref[pl.ds(pl.multiple_of(owner * blocks, blocks), blocks), :] = pieces[k][...]
    for k, pack in zip(range(2, nz - 1), packs):
        goal = lax.rem(s + k, nz)
        pack[:cols, :] = f_ref[pl.ds(pl.multiple_of(goal * cols, cols), cols), :]
        pack[cols:, :] = cot_ref[...]


def input_grad_kernel(nz, nc, pos_ref, before_ref, cot_ref, after_ref, w_ref, *refs):
    parts = refs[:nc]
    cols_ref, sum_ref = refs[nc:]
    blocks = cot_ref.shape[0]
    s, c = pos_ref[0], pos_ref[1]
    inside = {-1: s < nz - 1, 1: s > 0}
    for dz, ref in ((-1, after_ref), (0, cot_ref), (1, before_ref)):
        plane = ref[...].astype(F32)
        if dz:
            plane = jnp.where(inside[dz], plane, 0.0)
        for dy in (-1, 0, 1):
            for dx in (-1, 0, 1):
                tap = 9 * (dz + 1) + 3 * (dy + 1) + dx + 1
                cols_ref[tap * blocks : (tap + 1) * blocks, :] = shifted(plane, -dy, -dx).astype(BF16)
    sum_ref[...] = lax.dot_general(
        w_ref[...], cols_ref[...], (((0,), (0,)), ((), ())), preferred_element_type=F32
    )
    for k in range(nc):
        goal = lax.rem(c + k, nc)
        parts[k][...] = sum_ref[pl.ds(pl.multiple_of(goal * blocks, blocks), blocks), :]


def output_kernel(nz, scale, pos_ref, w_ref, cot_ref, cm_ref, cp_ref, f0_ref, fm_ref, fp_ref, *refs):
    packs = refs[: nz - 3]
    out_ref, wg_ref, c_ref, g_ref = refs[nz - 3 :]
    blocks = cot_ref.shape[0]
    cols = g_ref.shape[1]
    taps = 9 * blocks
    s = pos_ref[0]
    acc = None
    inside = {-1: s > 0, 1: s < nz - 1}
    for dz, ref in ((0, f0_ref), (-1, fm_ref), (1, fp_ref)):
        term = jnp.dot(
            w_ref[(dz + 1) * taps : (dz + 2) * taps, :], ref[...], preferred_element_type=F32
        )
        acc = term if acc is None else acc + jnp.where(inside[dz], term, 0.0)
    total = None
    for dx in (-1, 0, 1):
        for dy in (-1, 0, 1):
            at = (3 * (dy + 1) + dx + 1) * blocks
            term = shifted(acc[at : at + blocks], dy, dx)
            total = term if total is None else total + term
    out_ref[:, 0, :] = total

    mine = pl.ds(pl.multiple_of(s * cols, cols), cols)
    c_ref[s] = cot_ref[...]
    g_ref[s] = f0_ref[mine, :]

    for source, cot_near, f_near in (
        (lax.rem(s + nz - 1, nz), cm_ref, fm_ref),
        (lax.rem(s + 1, nz), cp_ref, fp_ref),
    ):
        c_ref[source] = cot_near[...]
        g_ref[source] = f_near[mine, :]
    for k, pack in zip(range(2, nz - 1), packs):
        source = lax.rem(s + nz - k, nz)
        c_ref[source] = pack[cols:, :]
        g_ref[source] = pack[:cols, :]

    cots = []
    feats = []
    for z in range(nz):
        plane = c_ref[z].astype(F32)
        cots.append([shifted(plane, -dy, 0).astype(BF16) for dy in (-1, 0, 1)])
        field = g_ref[z].astype(F32)
        feats.append(jnp.concatenate([shifted(field, 0, dx).astype(BF16) for dx in (-1, 0, 1)], 0))
    for dz in (-1, 0, 1):
        sums = None
        for z in range(nz):
            if 0 <= z - dz < nz:
                term = lax.dot_general(
                    jnp.concatenate(cots[z - dz], 0),
                    feats[z],
                    (((1,), (1,)), ((), ())),
                    preferred_element_type=F32,
                )
                sums = term if sums is None else sums + term
        sums = sums * scale
        for dy in range(3):
            for dx in range(3):
                tap = 9 * (dz + 1) + 3 * dy + dx
                wg_ref[tap] = sums[dy * blocks : (dy + 1) * blocks, dx * cols : (dx + 1) * cols]


def total_kernel(*refs):
    total = refs[0][...]
    for ref in refs[1:-1]:
        total = total + ref[...]
    refs[-1][:, 0, :] = total


VMEM = pl.BlockSpec(memory_space=pltpu.VMEM)
SMEM = pl.BlockSpec(memory_space=pltpu.SMEM)


def kernel_call(body, name, outs, args, scratch=(), flops=0):
    moved = sum(math.prod(a.shape) * a.dtype.itemsize for a in args + outs)
    return pl.pallas_call(
        body,
        out_shape=outs,
        in_specs=[SMEM if a.dtype == jnp.int32 else VMEM for a in args],
        out_specs=tuple(VMEM for _ in outs),
        scratch_shapes=list(scratch),
        compiler_params=pltpu.CompilerParams(vmem_limit_bytes=VMEM_BYTES),
        cost_estimate=pl.CostEstimate(flops=flops, bytes_accessed=moved, transcendentals=0),
        name=name,
    )(*args)


def per_device(features, weights, cotangent):
    blocks, depth, plane = features.shape
    channels = weights.shape[2]
    nz = lax.axis_size("sp")
    nc = lax.axis_size("ch")
    cols = channels // nz
    w2 = weights.reshape(27 * blocks, channels)
    feat = features.reshape(blocks, plane)
    cot = cotangent.reshape(blocks, plane)
    pos = jnp.stack([lax.axis_index("sp"), lax.axis_index("ch")]).astype(jnp.int32)

    def turn(count, k):
        return [(i, (i + k) % count) for i in range(count)]

    up, down = turn(nz, 1), turn(nz, nz - 1)
    field = jax.ShapeDtypeStruct((blocks, plane), BF16)
    wide = jax.ShapeDtypeStruct((blocks, plane), F32)

    cot_before = lax.ppermute(cot, "sp", up)
    cot_after = lax.ppermute(cot, "sp", down)
    pieces = [feat] + [lax.ppermute(feat, "ch", turn(nc, k)) for k in range(1, nc)]

    parts = kernel_call(
        functools.partial(input_grad_kernel, nz, nc),
        "input_grad",
        [wide] * nc,
        [pos, cot_before, cot, cot_after, w2],
        [pltpu.VMEM((27 * blocks, plane), BF16), pltpu.VMEM((channels, plane), F32)],
        2 * 27 * blocks * channels * plane,
    )
    terms = [parts[0]] + [lax.ppermute(parts[k], "ch", turn(nc, k)) for k in range(1, nc)]

    packed = jax.ShapeDtypeStruct((cols + blocks, plane), BF16)
    f_all, *packs = kernel_call(
        functools.partial(gather_kernel, nz, nc),
        "gather",
        [jax.ShapeDtypeStruct((channels, plane), BF16)] + [packed] * (nz - 3),
        [pos, cot] + pieces,
    )
    f_before = lax.ppermute(f_all, "sp", up)
    f_after = lax.ppermute(f_all, "sp", down)
    far = [lax.ppermute(packs[k - 2], "sp", turn(nz, k)) for k in range(2, nz - 1)]

    output, weight_grad = kernel_call(
        functools.partial(output_kernel, nz, 1.0 / math.sqrt(nz * depth * plane)),
        "output_and_weight_grad",
        [
            jax.ShapeDtypeStruct((blocks, 1, plane), F32),
            jax.ShapeDtypeStruct((27, blocks, cols), F32),
        ],
        [pos, w2, cot, cot_before, cot_after, f_all, f_before, f_after] + far,
        [pltpu.VMEM((nz, blocks, plane), BF16), pltpu.VMEM((nz, cols, plane), BF16)],
        4 * 27 * blocks * channels * plane,
    )
    (back,) = kernel_call(
        total_kernel, "total", [jax.ShapeDtypeStruct((blocks, 1, plane), F32)], terms
    )
    return (output, back, weight_grad)


def solution(mesh):
    return jax.shard_map(
        per_device,
        mesh=mesh,
        in_specs=(P("ch", ("grp", "sp"), None), P(None, "ch", None), P("ch", ("grp", "sp"), None)),
        out_specs=(
            P("ch", ("grp", "sp"), None),
            P("ch", ("grp", "sp"), None),
            P("grp", "ch", "sp"),
        ),
        check_vma=False,
    )
```

```python
import functools
import math

import jax
import jax.numpy as jnp
from jax import lax
from jax.experimental import pallas as pl
from jax.experimental.pallas import tpu as pltpu
from jax.sharding import PartitionSpec as P

NX = 64
NY = 10
CELLS = NX * NY
F32 = jnp.float32
BF16 = jnp.bfloat16
VMEM_BYTES = 32 * 1024 * 1024


def cell_mask(rows, dy, dx):
    q = lax.broadcasted_iota(jnp.int32, (rows, CELLS), 1)
    x = q % NX + dx
    y = q // NX + dy
    return (x >= 0) & (x < NX) & (y >= 0) & (y < NY)


def shifted(value, dy, dx):
    if dy == 0 and dx == 0:
        return value
    moved = pltpu.roll(value, (-(dy * NX + dx)) % CELLS, 1)
    return jnp.where(cell_mask(value.shape[0], dy, dx), moved, 0.0)


def gather_kernel(nz, nc, pos_ref, token_ref, cot_ref, *refs):
    pieces = refs[:nc]
    f_ref = refs[nc]
    packs = refs[nc + 1 :]
    blocks = cot_ref.shape[0]
    cols = f_ref.shape[0] // nz
    s, c = pos_ref[0], pos_ref[1]
    for k in range(nc):
        f_ref[pl.ds(pl.multiple_of((c ^ k) * blocks, blocks), blocks), :] = pieces[k][...]
    for k, pack in zip(range(2, nz), packs):
        goal = lax.rem(s + k, nz) if k < nz - 1 else nz - 1 - s
        pack[:cols, :] = f_ref[pl.ds(pl.multiple_of(goal * cols, cols), cols), :]
        pack[cols:, :] = cot_ref[...]


def columns(cols_ref, first, plane):
    blocks = plane.shape[0]
    for dy in (-1, 0, 1):
        for dx in (-1, 0, 1):
            tap = first + 3 * (dy + 1) + dx + 1
            cols_ref[tap * blocks : (tap + 1) * blocks, :] = shifted(plane, -dy, -dx).astype(BF16)


def own_plane_kernel(cot_ref, cols_ref):
    columns(cols_ref, 0, cot_ref[...].astype(F32))


def input_grad_kernel(nz, nc, pos_ref, own_ref, even_ref, odd_ref, w_ref, *refs):
    send_ref, keep_ref, token_ref, cols_ref, sum_ref = refs
    blocks = even_ref.shape[0]
    s, c = pos_ref[0], pos_ref[1]
    token_ref[...] = jnp.zeros(token_ref.shape, F32)
    even, odd = even_ref[...].astype(F32), odd_ref[...].astype(F32)
    first = s % 2 == 0
    columns(cols_ref, 0, jnp.where(s < nz - 1, jnp.where(first, even, odd), 0.0))
    columns(cols_ref, 9, jnp.where(s > 0, jnp.where(first, odd, even), 0.0))
    taps = 9 * blocks
    over_rows = (((0,), (0,)), ((), ()))
    near = lax.dot_general(
        w_ref[taps : 2 * taps, :], own_ref[...], over_rows, preferred_element_type=F32
    )
    low = lax.dot_general(
        w_ref[:taps, :], cols_ref[:taps, :], over_rows, preferred_element_type=F32
    )
    high = lax.dot_general(
        w_ref[2 * taps :, :], cols_ref[taps:, :], over_rows, preferred_element_type=F32
    )
    sum_ref[...] = near + low + high
    for k in range(nc):
        goal = c ^ k
        block = sum_ref[pl.ds(pl.multiple_of(goal * blocks, blocks), blocks), :]
        ref = send_ref if k % 2 else keep_ref
        ref[k // 2 * blocks : (k // 2 + 1) * blocks, :] = block


def fold_kernel(blocks, keep_ref, got_ref, send_ref, left_ref):
    for k in range(keep_ref.shape[0] // blocks):
        at = slice(k * blocks, (k + 1) * blocks)
        to = slice(k // 2 * blocks, (k // 2 + 1) * blocks)
        (send_ref if k % 2 else left_ref)[to, :] = keep_ref[at, :] + got_ref[at, :]


def output_kernel(nz, scale, pos_ref, w_ref, cot_ref, ce_ref, co_ref, f0_ref, fe_ref, fo_ref, *refs):
    packs = refs[: nz - 2]
    out_ref, wg_ref, token_ref, c_ref, g_ref = refs[nz - 2 :]
    blocks = cot_ref.shape[0]
    cols = g_ref.shape[1]
    taps = 9 * blocks
    s = pos_ref[0]
    first = s % 2 == 0
    even, odd = fe_ref[...].astype(F32), fo_ref[...].astype(F32)
    fields = {
        -1: jnp.where(s > 0, jnp.where(first, odd, even), 0.0).astype(BF16),
        0: f0_ref[...],
        1: jnp.where(s < nz - 1, jnp.where(first, even, odd), 0.0).astype(BF16),
    }
    acc = None
    for dz in (-1, 0, 1):
        term = jnp.dot(
            w_ref[(dz + 1) * taps : (dz + 2) * taps, :], fields[dz], preferred_element_type=F32
        )
        acc = term if acc is None else acc + term
    total = None
    for dx in (-1, 0, 1):
        for dy in (-1, 0, 1):
            at = (3 * (dy + 1) + dx + 1) * blocks
            term = shifted(acc[at : at + blocks], dy, dx)
            total = term if total is None else total + term
    out_ref[:, 0, :] = total
    token_ref[...] = jnp.zeros(token_ref.shape, F32)

    mine = pl.ds(pl.multiple_of(s * cols, cols), cols)
    odd_source = jnp.clip(jnp.where(first, s - 1, s + 1), 0, nz - 1)
    c_ref[odd_source] = co_ref[...]
    g_ref[odd_source] = fo_ref[mine, :]
    even_source = s ^ 1
    c_ref[even_source] = ce_ref[...]
    g_ref[even_source] = fe_ref[mine, :]
    c_ref[s] = cot_ref[...]
    g_ref[s] = f0_ref[mine, :]
    for k, pack in zip(range(2, nz - 1), packs):
        source = lax.rem(s + nz - k, nz)
        c_ref[source] = pack[cols:, :]
        g_ref[source] = pack[:cols, :]

    @pl.when((s == 0) | (s == nz - 1))
    def _():
        source = nz - 1 - s
        c_ref[source] = packs[-1][cols:, :]
        g_ref[source] = packs[-1][:cols, :]

    cots = []
    feats = []
    for z in range(nz):
        plane = c_ref[z].astype(F32)
        cots.append([shifted(plane, -dy, 0).astype(BF16) for dy in (-1, 0, 1)])
        field = g_ref[z].astype(F32)
        feats.append(jnp.concatenate([shifted(field, 0, dx).astype(BF16) for dx in (-1, 0, 1)], 0))
    for dz in (-1, 0, 1):
        sums = None
        for z in range(nz):
            if 0 <= z - dz < nz:
                term = lax.dot_general(
                    jnp.concatenate(cots[z - dz], 0),
                    feats[z],
                    (((1,), (1,)), ((), ())),
                    preferred_element_type=F32,
                )
                sums = term if sums is None else sums + term
        sums = sums * scale
        for dy in range(3):
            for dx in range(3):
                tap = 9 * (dz + 1) + 3 * dy + dx
                wg_ref[tap] = sums[dy * blocks : (dy + 1) * blocks, dx * cols : (dx + 1) * cols]


def total_kernel(token_ref, keep_ref, got_ref, out_ref):
    out_ref[:, 0, :] = keep_ref[...] + got_ref[...]


VMEM = pl.BlockSpec(memory_space=pltpu.VMEM)
SMEM = pl.BlockSpec(memory_space=pltpu.SMEM)


def kernel_call(body, name, outs, args, scratch=(), flops=0):
    moved = sum(math.prod(a.shape) * a.dtype.itemsize for a in args + outs)
    return pl.pallas_call(
        body,
        out_shape=outs,
        in_specs=[SMEM if a.dtype == jnp.int32 else VMEM for a in args],
        out_specs=tuple(VMEM for _ in outs),
        scratch_shapes=list(scratch),
        compiler_params=pltpu.CompilerParams(vmem_limit_bytes=VMEM_BYTES),
        cost_estimate=pl.CostEstimate(flops=flops, bytes_accessed=moved, transcendentals=0),
        name=name,
    )(*args)


def per_device(features, weights, cotangent):
    blocks, depth, plane = features.shape
    channels = weights.shape[2]
    nz = lax.axis_size("sp")
    nc = lax.axis_size("ch")
    cols = channels // nz
    w2 = weights.reshape(27 * blocks, channels)
    feat = features.reshape(blocks, plane)
    cot = cotangent.reshape(blocks, plane)
    pos = jnp.stack([lax.axis_index("sp"), lax.axis_index("ch")]).astype(jnp.int32)

    even_pairs = [(i, i ^ 1) for i in range(nz)]
    odd_pairs = [(i, min(max(((i + 1) ^ 1) - 1, 0), nz - 1)) for i in range(nz)]
    ends = [(i, nz - 1 - i if i in (0, nz - 1) else i) for i in range(nz)]

    def mixed(k):
        return [(i, i ^ k) for i in range(nc)]

    def of(rows, dtype):
        return jax.ShapeDtypeStruct((rows, plane), dtype)

    small = jax.ShapeDtypeStruct((8, 128), F32)
    work = 2 * 27 * blocks * channels * plane

    cot_even = lax.ppermute(cot, "sp", even_pairs)
    cot_odd = lax.ppermute(cot, "sp", odd_pairs)
    (own,) = kernel_call(own_plane_kernel, "own_plane", [of(9 * blocks, BF16)], [cot], flops=work)
    feat, cot_even = lax.optimization_barrier((feat, cot_even))
    pieces = [feat] + [lax.ppermute(feat, "ch", mixed(k)) for k in range(1, nc)]

    send, keep, token = kernel_call(
        functools.partial(input_grad_kernel, nz, nc),
        "input_grad",
        [of(channels // 2, F32), of(channels // 2, F32), small],
        [pos, own, cot_even, cot_odd, w2],
        [pltpu.VMEM((18 * blocks, plane), BF16), pltpu.VMEM((channels, plane), F32)],
        work,
    )
    step = 1
    got = lax.ppermute(send, "ch", mixed(step))
    while 2 * step < nc:
        step *= 2
        rows = channels // (2 * step)
        send, keep = kernel_call(
            functools.partial(fold_kernel, blocks), "fold", [of(rows, F32)] * 2, [keep, got]
        )
        got = lax.ppermute(send, "ch", mixed(step))

    f_all, *packs = kernel_call(
        functools.partial(gather_kernel, nz, nc),
        "gather",
        [of(channels, BF16)] + [of(cols + blocks, BF16)] * (nz - 2),
        [pos, token, cot] + pieces,
    )
    f_even = lax.ppermute(f_all, "sp", even_pairs)
    f_odd = lax.ppermute(f_all, "sp", odd_pairs)
    far = [
        lax.ppermute(packs[k - 2], "sp", [(i, (i + k) % nz) for i in range(nz)])
        for k in range(2, nz - 1)
    ]
    far.append(lax.ppermute(packs[-1], "sp", ends))

    output, weight_grad, last = kernel_call(
        functools.partial(output_kernel, nz, 1.0 / math.sqrt(nz * depth * plane)),
        "output_and_weight_grad",
        [
            jax.ShapeDtypeStruct((blocks, 1, plane), F32),
            jax.ShapeDtypeStruct((27, blocks, cols), F32),
            small,
        ],
        [pos, w2, cot, cot_even, cot_odd, f_all, f_even, f_odd] + far,
        [pltpu.VMEM((nz, blocks, plane), BF16), pltpu.VMEM((nz, cols, plane), BF16)],
        4 * work,
    )
    (back,) = kernel_call(
        total_kernel, "total", [jax.ShapeDtypeStruct((blocks, 1, plane), F32)], [last, keep, got]
    )
    return (output, back, weight_grad)


def solution(mesh):
    return jax.shard_map(
        per_device,
        mesh=mesh,
        in_specs=(P("ch", ("grp", "sp"), None), P(None, "ch", None), P("ch", ("grp", "sp"), None)),
        out_specs=(
            P("ch", ("grp", "sp"), None),
            P("ch", ("grp", "sp"), None),
            P("grp", "ch", "sp"),
        ),
        check_vma=False,
    )
```

```python
import functools
import math

import jax
import jax.numpy as jnp
from jax import lax
from jax.experimental import pallas as pl
from jax.experimental.pallas import tpu as pltpu
from jax.sharding import PartitionSpec as P

NX = 64
NY = 10
CELLS = NX * NY
F32 = jnp.float32
BF16 = jnp.bfloat16
W_BEGIN, W_GRAD, W_TOTAL, W_OUT = 8, 1, 4, 0
PARTS = 1
VMEM_BYTES = 32 * 1024 * 1024


def cell_mask(rows, dy, dx):
    q = lax.broadcasted_iota(jnp.int32, (rows, CELLS), 1)
    x = q % NX + dx
    y = q // NX + dy
    return (x >= 0) & (x < NX) & (y >= 0) & (y < NY)


def shifted(value, dy, dx):
    if dy == 0 and dx == 0:
        return value
    moved = pltpu.roll(value, (-(dy * NX + dx)) % CELLS, 1)
    return jnp.where(cell_mask(value.shape[0], dy, dx), moved, 0.0)


def gather_kernel(nz, nc, pos_ref, token_ref, cot_ref, *refs):
    pieces = refs[:nc]
    parts = refs[nc : nc + PARTS]
    packs = refs[nc + PARTS : -1]
    f_ref = refs[-1]
    blocks = cot_ref.shape[0]
    cols = f_ref.shape[0] // nz
    some = f_ref.shape[0] // PARTS
    s, c = pos_ref[0], pos_ref[1]
    for k in range(nc):
        f_ref[pl.ds(pl.multiple_of((c ^ k) * blocks, blocks), blocks), :] = pieces[k][...]
    for i, part in enumerate(parts):
        part[...] = f_ref[i * some : (i + 1) * some, :]
    for k, pack in zip(range(2, nz - 1), packs):
        goal = lax.rem(s + k, nz)
        pack[:cols, :] = f_ref[pl.ds(pl.multiple_of(goal * cols, cols), cols), :]
        pack[cols:, :] = cot_ref[...]


def columns(cols_ref, first, plane):
    blocks = plane.shape[0]
    for dy in (-1, 0, 1):
        for dx in (-1, 0, 1):
            tap = first + 3 * (dy + 1) + dx + 1
            cols_ref[tap * blocks : (tap + 1) * blocks, :] = shifted(plane, -dy, -dx).astype(BF16)


def token_kernel(token_ref):
    token_ref[...] = jnp.zeros(token_ref.shape, F32)


def input_grad_kernel(nz, nc, pos_ref, begin_ref, cot_ref, even_ref, odd_ref, w_ref, *refs):
    parts = refs[:nc]
    token_ref, cols_ref, sum_ref = refs[nc:]
    blocks = even_ref.shape[0]
    s, c = pos_ref[0], pos_ref[1]
    token_ref[...] = jnp.zeros(token_ref.shape, F32)
    even, odd = even_ref[...].astype(F32), odd_ref[...].astype(F32)
    first = s % 2 == 0
    columns(cols_ref, 0, jnp.where(s < nz - 1, jnp.where(first, even, odd), 0.0))
    columns(cols_ref, 9, cot_ref[...].astype(F32))
    columns(cols_ref, 18, jnp.where(s > 0, jnp.where(first, odd, even), 0.0))
    sum_ref[...] = lax.dot_general(
        w_ref[...], cols_ref[...], (((0,), (0,)), ((), ())), preferred_element_type=F32
    )
    for k in range(nc):
        parts[k][...] = sum_ref[pl.ds(pl.multiple_of((c ^ k) * blocks, blocks), blocks), :]


def output_kernel(nz, scale, pos_ref, last_ref, w_ref, cot_ref, ce_ref, co_ref, *refs):
    f_parts = [refs[i * PARTS : (i + 1) * PARTS] for i in range(3)]
    packs = refs[3 * PARTS : 3 * PARTS + nz - 3]
    out_ref, wg_ref, c_ref, g_ref, f_ref = refs[3 * PARTS + nz - 3 :]
    blocks = cot_ref.shape[0]
    cols = g_ref.shape[1]
    some = f_ref.shape[1] // PARTS
    taps = 9 * blocks
    s = pos_ref[0]
    even_at = 1 + s % 2
    for i in range(PARTS):
        rows = slice(i * some, (i + 1) * some)
        f_ref[0, rows, :] = f_parts[0][i][...]
        f_ref[even_at, rows, :] = f_parts[1][i][...]
        f_ref[3 - even_at, rows, :] = f_parts[2][i][...]
    inside = {-1: s > 0, 1: s < nz - 1}
    acc = None
    for dz in (0, 1, -1):
        term = jnp.dot(
            w_ref[(dz + 1) * taps : (dz + 2) * taps, :], f_ref[dz % 3], preferred_element_type=F32
        )
        acc = term if acc is None else acc + jnp.where(inside[dz], term, 0.0)
    total = None
    for dx in (-1, 0, 1):
        for dy in (-1, 0, 1):
            at = (3 * (dy + 1) + dx + 1) * blocks
            term = shifted(acc[at : at + blocks], dy, dx)
            total = term if total is None else total + term
    out_ref[:, 0, :] = total

    mine = pl.ds(pl.multiple_of(s * cols, cols), cols)
    odd_source = lax.rem(((s + 1) ^ 1) + nz - 1, nz)
    c_ref[odd_source] = co_ref[...]
    g_ref[odd_source] = f_ref[3 - even_at, mine, :]
    even_source = s ^ 1
    c_ref[even_source] = ce_ref[...]
    g_ref[even_source] = f_ref[even_at, mine, :]
    c_ref[s] = cot_ref[...]
    g_ref[s] = f_ref[0, mine, :]
    for k, pack in zip(range(2, nz - 1), packs):
        source = lax.rem(s + nz - k, nz)
        c_ref[source] = pack[cols:, :]
        g_ref[source] = pack[:cols, :]

    cots = []
    feats = []
    for z in range(nz):
        plane = c_ref[z].astype(F32)
        cots.append([shifted(plane, -dy, 0).astype(BF16) for dy in (-1, 0, 1)])
        field = g_ref[z].astype(F32)
        feats.append(jnp.concatenate([shifted(field, 0, dx).astype(BF16) for dx in (-1, 0, 1)], 0))
    for dz in (-1, 0, 1):
        sums = None
        for z in range(nz):
            if 0 <= z - dz < nz:
                term = lax.dot_general(
                    jnp.concatenate(cots[z - dz], 0),
                    feats[z],
                    (((1,), (1,)), ((), ())),
                    preferred_element_type=F32,
                )
                sums = term if sums is None else sums + term
        sums = sums * scale
        for dy in range(3):
            for dx in range(3):
                tap = 9 * (dz + 1) + 3 * dy + dx
                wg_ref[tap] = sums[dy * blocks : (dy + 1) * blocks, dx * cols : (dx + 1) * cols]


def total_kernel(*refs):
    total = refs[0][...]
    for ref in refs[1:-2]:
        total = total + ref[...]
    refs[-2][:, 0, :] = total
    refs[-1][...] = jnp.zeros(refs[-1].shape, F32)


VMEM = pl.BlockSpec(memory_space=pltpu.VMEM)
SMEM = pl.BlockSpec(memory_space=pltpu.SMEM)


def kernel_call(body, name, outs, args, scratch=(), weight=0):
    return pl.pallas_call(
        body,
        out_shape=outs,
        in_specs=[SMEM if a.dtype == jnp.int32 else VMEM for a in args],
        out_specs=tuple(VMEM for _ in outs),
        scratch_shapes=list(scratch),
        compiler_params=pltpu.CompilerParams(vmem_limit_bytes=VMEM_BYTES),
        cost_estimate=pl.CostEstimate(flops=weight, bytes_accessed=0, transcendentals=0),
        name=name,
    )(*args)


def per_device(features, weights, cotangent):
    blocks, depth, plane = features.shape
    channels = weights.shape[2]
    nz = lax.axis_size("sp")
    nc = lax.axis_size("ch")
    cols = channels // nz
    w2 = weights.reshape(27 * blocks, channels)
    feat = features.reshape(blocks, plane)
    cot = cotangent.reshape(blocks, plane)
    pos = jnp.stack([lax.axis_index("sp"), lax.axis_index("ch")]).astype(jnp.int32)

    even_pairs = [(i, i ^ 1) for i in range(nz)]
    odd_pairs = [(i, (((i + 1) ^ 1) - 1) % nz) for i in range(nz)]

    def mixed(k):
        return [(i, i ^ k) for i in range(nc)]

    def of(rows, dtype):
        return jax.ShapeDtypeStruct((rows, plane), dtype)

    small = jax.ShapeDtypeStruct((8, 128), F32)
    work = 2 * 27 * blocks * channels * plane

    (begin,) = kernel_call(token_kernel, "begin", [small], [], weight=W_BEGIN * work)
    cot_sent, begin = lax.optimization_barrier((cot, begin))
    cot_even = lax.ppermute(cot_sent, "sp", even_pairs)
    cot_odd = lax.ppermute(cot_sent, "sp", odd_pairs)
    feat, cot_even = lax.optimization_barrier((feat, cot_even))
    pieces = [feat] + [lax.ppermute(feat, "ch", mixed(k)) for k in range(1, nc)]

    *parts, token = kernel_call(
        functools.partial(input_grad_kernel, nz, nc),
        "input_grad",
        [of(blocks, F32)] * nc + [small],
        [pos, begin, cot, cot_even, cot_odd, w2],
        [pltpu.VMEM((27 * blocks, plane), BF16), pltpu.VMEM((channels, plane), F32)],
        W_GRAD * work,
    )
    terms = [parts[0]] + [lax.ppermute(parts[k], "ch", mixed(k)) for k in range(1, nc)]

    f_parts = kernel_call(
        functools.partial(gather_kernel, nz, nc),
        "gather",
        [of(channels // PARTS, BF16)] * PARTS + [of(cols + blocks, BF16)] * (nz - 3),
        [pos, token, cot] + pieces,
        [pltpu.VMEM((channels, plane), BF16)],
    )
    f_parts, packs = f_parts[:PARTS], f_parts[PARTS:]
    f_even = [lax.ppermute(part, "sp", even_pairs) for part in f_parts]
    f_odd = [lax.ppermute(part, "sp", odd_pairs) for part in f_parts]
    far = [
        lax.ppermute(packs[k - 2], "sp", [(i, (i + k) % nz) for i in range(nz)])
        for k in range(2, nz - 1)
    ]

    back, last = kernel_call(
        total_kernel,
        "total",
        [jax.ShapeDtypeStruct((blocks, 1, plane), F32), small],
        terms,
        weight=W_TOTAL * work,
    )
    output, weight_grad = kernel_call(
        functools.partial(output_kernel, nz, 1.0 / math.sqrt(nz * depth * plane)),
        "output_and_weight_grad",
        [
            jax.ShapeDtypeStruct((blocks, 1, plane), F32),
            jax.ShapeDtypeStruct((27, blocks, cols), F32),
        ],
        [pos, last, w2, cot, cot_even, cot_odd, *f_parts, *f_even, *f_odd, *far],
        [
            pltpu.VMEM((nz, blocks, plane), BF16),
            pltpu.VMEM((nz, cols, plane), BF16),
            pltpu.VMEM((3, channels, plane), BF16),
        ],
        W_OUT * work,
    )
    return (output, back, weight_grad)


def solution(mesh):
    return jax.shard_map(
        per_device,
        mesh=mesh,
        in_specs=(P("ch", ("grp", "sp"), None), P(None, "ch", None), P("ch", ("grp", "sp"), None)),
        out_specs=(
            P("ch", ("grp", "sp"), None),
            P("ch", ("grp", "sp"), None),
            P("grp", "ch", "sp"),
        ),
        check_vma=False,
    )
```

```python
import functools
import math

import jax
import jax.numpy as jnp
from jax import lax
from jax.experimental import pallas as pl
from jax.experimental.pallas import tpu as pltpu
from jax.sharding import PartitionSpec as P

NX = 64
NY = 10
CELLS = NX * NY
F32 = jnp.float32
BF16 = jnp.bfloat16
W_BEGIN, W_GRAD, W_TOTAL, W_OUT = 8, 1, 4, 0
VMEM_BYTES = 32 * 1024 * 1024


def cell_mask(rows, dy, dx):
    q = lax.broadcasted_iota(jnp.int32, (rows, CELLS), 1)
    x = q % NX + dx
    y = q // NX + dy
    return (x >= 0) & (x < NX) & (y >= 0) & (y < NY)


def shifted(value, dy, dx):
    if dy == 0 and dx == 0:
        return value
    moved = pltpu.roll(value, (-(dy * NX + dx)) % CELLS, 1)
    return jnp.where(cell_mask(value.shape[0], dy, dx), moved, 0.0)


def odd_partner(s, nz):
    return lax.rem(((s + 1) ^ 1) + nz - 1, nz)


def gather_kernel(nz, nc, pos_ref, token_ref, cot_ref, *refs):
    pieces, f_ref, packs = refs[:nc], refs[nc], refs[nc + 1 :]
    blocks = cot_ref.shape[0]
    cols = f_ref.shape[0] // nz
    s, c = pos_ref[0], pos_ref[1]
    for k in range(nc):
        f_ref[pl.ds(pl.multiple_of((c ^ k) * blocks, blocks), blocks), :] = pieces[k][...]
    for k, pack in zip(range(2, nz - 1), packs):
        goal = lax.rem(s + k, nz)
        pack[:cols, :] = f_ref[pl.ds(pl.multiple_of(goal * cols, cols), cols), :]
        pack[cols:, :] = cot_ref[...]


def columns(cols_ref, first, plane):
    blocks = plane.shape[0]
    for dy in (-1, 0, 1):
        for dx in (-1, 0, 1):
            tap = first + 3 * (dy + 1) + dx + 1
            cols_ref[tap * blocks : (tap + 1) * blocks, :] = shifted(plane, -dy, -dx).astype(BF16)


def hold_kernel(*refs):
    refs[-1][...] = jnp.zeros(refs[-1].shape, F32)


def token_kernel(token_ref):
    token_ref[...] = jnp.zeros(token_ref.shape, F32)


def input_grad_kernel(nz, nc, pos_ref, begin_ref, cot_ref, even_ref, odd_ref, w_ref, *refs):
    parts = refs[:nc]
    token_ref, cols_ref, sum_ref = refs[nc:]
    blocks = even_ref.shape[0]
    s, c = pos_ref[0], pos_ref[1]
    token_ref[...] = jnp.zeros(token_ref.shape, F32)
    even, odd = even_ref[...].astype(F32), odd_ref[...].astype(F32)
    first = s % 2 == 0
    columns(cols_ref, 0, jnp.where(s < nz - 1, jnp.where(first, even, odd), 0.0))
    columns(cols_ref, 9, cot_ref[...].astype(F32))
    columns(cols_ref, 18, jnp.where(s > 0, jnp.where(first, odd, even), 0.0))
    sum_ref[...] = lax.dot_general(
        w_ref[...], cols_ref[...], (((0,), (0,)), ((), ())), preferred_element_type=F32
    )
    for k in range(nc):
        parts[k][...] = sum_ref[pl.ds(pl.multiple_of((c ^ k) * blocks, blocks), blocks), :]


def conv_part(w_ref, field, dz):
    taps = w_ref.shape[0] // 3
    return jnp.dot(
        w_ref[(dz + 1) * taps : (dz + 2) * taps, :], field, preferred_element_type=F32
    )


def output_kernel(nz, nc, scale, pos_ref, last_ref, w_ref, *refs):
    terms = refs[:nc]
    cot_ref, ce_ref, co_ref, f_ref, fe_ref, fo_ref = refs[nc : nc + 6]
    packs = refs[nc + 6 : -5]
    out_ref, back_ref, wg_ref, c_ref, g_ref = refs[-5:]
    total = terms[0][...]
    for term in terms[1:]:
        total = total + term[...]
    back_ref[:, 0, :] = total

    blocks = cot_ref.shape[0]
    cols = g_ref.shape[1]
    s = pos_ref[0]
    first = s % 2 == 0
    even, odd = fe_ref[...], fo_ref[...]
    acc = conv_part(w_ref, f_ref[...], 0)
    acc = acc + jnp.where(s < nz - 1, conv_part(w_ref, jnp.where(first, even, odd), 1), 0.0)
    acc = acc + jnp.where(s > 0, conv_part(w_ref, jnp.where(first, odd, even), -1), 0.0)
    total = None
    for dx in (-1, 0, 1):
        for dy in (-1, 0, 1):
            at = (3 * (dy + 1) + dx + 1) * blocks
            term = shifted(acc[at : at + blocks], dy, dx)
            total = term if total is None else total + term
    out_ref[:, 0, :] = total

    mine = pl.ds(pl.multiple_of(s * cols, cols), cols)
    for source, cot, field in (
        (s, cot_ref, f_ref),
        (s ^ 1, ce_ref, fe_ref),
        (odd_partner(s, nz), co_ref, fo_ref),
    ):
        c_ref[source] = cot[...]
        g_ref[source] = field[mine, :]
    for k, pack in zip(range(2, nz - 1), packs):
        source = lax.rem(s + nz - k, nz)
        c_ref[source] = pack[cols:, :]
        g_ref[source] = pack[:cols, :]

    cots = []
    feats = []
    for z in range(nz):
        plane = c_ref[z].astype(F32)
        cots.append([shifted(plane, -dy, 0).astype(BF16) for dy in (-1, 0, 1)])
        field = g_ref[z].astype(F32)
        feats.append(jnp.concatenate([shifted(field, 0, dx).astype(BF16) for dx in (-1, 0, 1)], 0))
    for dz in (-1, 0, 1):
        sums = None
        for z in range(nz):
            if 0 <= z - dz < nz:
                term = lax.dot_general(
                    jnp.concatenate(cots[z - dz], 0),
                    feats[z],
                    (((1,), (1,)), ((), ())),
                    preferred_element_type=F32,
                )
                sums = term if sums is None else sums + term
        sums = sums * scale
        for dy in range(3):
            for dx in range(3):
                tap = 9 * (dz + 1) + 3 * dy + dx
                wg_ref[tap] = sums[dy * blocks : (dy + 1) * blocks, dx * cols : (dx + 1) * cols]


VMEM = pl.BlockSpec(memory_space=pltpu.VMEM)
SMEM = pl.BlockSpec(memory_space=pltpu.SMEM)


def kernel_call(body, name, outs, args, scratch=(), weight=0):
    return pl.pallas_call(
        body,
        out_shape=outs,
        in_specs=[SMEM if a.dtype == jnp.int32 else VMEM for a in args],
        out_specs=tuple(VMEM for _ in outs),
        scratch_shapes=list(scratch),
        compiler_params=pltpu.CompilerParams(vmem_limit_bytes=VMEM_BYTES),
        cost_estimate=pl.CostEstimate(flops=int(weight), bytes_accessed=0, transcendentals=0),
        name=name,
    )(*args)


def per_device(features, weights, cotangent):
    blocks, depth, plane = features.shape
    channels = weights.shape[2]
    nz = lax.axis_size("sp")
    nc = lax.axis_size("ch")
    cols = channels // nz
    w2 = weights.reshape(27 * blocks, channels)
    feat = features.reshape(blocks, plane)
    cot = cotangent.reshape(blocks, plane)
    pos = jnp.stack([lax.axis_index("sp"), lax.axis_index("ch")]).astype(jnp.int32)

    even_pairs = [(i, i ^ 1) for i in range(nz)]
    odd_pairs = [(i, (((i + 1) ^ 1) - 1) % nz) for i in range(nz)]

    def mixed(k):
        return [(i, i ^ k) for i in range(nc)]

    def of(rows, dtype):
        return jax.ShapeDtypeStruct((rows, plane), dtype)

    small = jax.ShapeDtypeStruct((8, 128), F32)
    work = 2 * 27 * blocks * channels * plane

    cot_even = lax.ppermute(cot, "sp", even_pairs)
    cot_odd = lax.ppermute(cot, "sp", odd_pairs)
    (begin,) = kernel_call(token_kernel, "begin", [small], [], weight=W_BEGIN * work)
    pieces = [feat] + [lax.ppermute(feat, "ch", mixed(k)) for k in range(1, nc)]

    *parts, token = kernel_call(
        functools.partial(input_grad_kernel, nz, nc),
        "input_grad",
        [of(blocks, F32)] * nc + [small],
        [pos, begin, cot, cot_even, cot_odd, w2],
        [pltpu.VMEM((27 * blocks, plane), BF16), pltpu.VMEM((channels, plane), F32)],
        W_GRAD * work,
    )
    terms = [parts[0]] + [lax.ppermute(parts[k], "ch", mixed(k)) for k in range(1, nc)]

    f_all, *packs = kernel_call(
        functools.partial(gather_kernel, nz, nc),
        "gather",
        [of(channels, BF16)] + [of(cols + blocks, BF16)] * (nz - 3),
        [pos, token, cot] + pieces,
    )
    f_odd = lax.ppermute(f_all, "sp", odd_pairs)
    far = [
        lax.ppermute(packs[k - 2], "sp", [(i, (i + k) % nz) for i in range(nz)])
        for k in range(2, nz - 1)
    ]
    f_even = lax.ppermute(f_all, "sp", even_pairs)

    block = jax.ShapeDtypeStruct((blocks, 1, plane), F32)
    (last,) = kernel_call(hold_kernel, "hold", [small], terms, weight=W_TOTAL * work)
    output, back, weight_grad = kernel_call(
        functools.partial(output_kernel, nz, nc, 1.0 / math.sqrt(nz * depth * plane)),
        "outputs",
        [block, block, jax.ShapeDtypeStruct((27, blocks, cols), F32)],
        [pos, last, w2, *terms, cot, cot_even, cot_odd, f_all, f_even, f_odd, *far],
        [pltpu.VMEM((nz, blocks, plane), BF16), pltpu.VMEM((nz, cols, plane), BF16)],
        W_OUT * work,
    )
    return (output, back, weight_grad)


def solution(mesh):
    return jax.shard_map(
        per_device,
        mesh=mesh,
        in_specs=(P("ch", ("grp", "sp"), None), P(None, "ch", None), P("ch", ("grp", "sp"), None)),
        out_specs=(
            P("ch", ("grp", "sp"), None),
            P("ch", ("grp", "sp"), None),
            P("grp", "ch", "sp"),
        ),
        check_vma=False,
    )
```

```python
import functools
import math

import jax
import jax.numpy as jnp
from jax import lax
from jax.experimental import pallas as pl
from jax.experimental.pallas import tpu as pltpu
from jax.sharding import PartitionSpec as P

NX = 64
NY = 10
CELLS = NX * NY
F32 = jnp.float32
BF16 = jnp.bfloat16
W_BEGIN, W_GRAD, W_TOTAL, W_OUT = 8, 1, 5, 0
VMEM_BYTES = 32 * 1024 * 1024


def cell_mask(rows, dy, dx):
    q = lax.broadcasted_iota(jnp.int32, (rows, CELLS), 1)
    x = q % NX + dx
    y = q // NX + dy
    return (x >= 0) & (x < NX) & (y >= 0) & (y < NY)


def shifted(value, dy, dx):
    if dy == 0 and dx == 0:
        return value
    moved = pltpu.roll(value, (-(dy * NX + dx)) % CELLS, 1)
    return jnp.where(cell_mask(value.shape[0], dy, dx), moved, 0.0)


def odd_partner(s, nz):
    return lax.rem(((s + 1) ^ 1) + nz - 1, nz)


def gather_kernel(nz, nc, pos_ref, token_ref, cot_ref, near_ref, *refs):
    pieces, f_ref, packs = refs[:nc], refs[nc], refs[nc + 1 :]
    blocks = cot_ref.shape[0]
    channels = nc * blocks
    cols = channels // nz
    s, c = pos_ref[0], pos_ref[1]
    for k in range(nc):
        f_ref[pl.ds(pl.multiple_of((c ^ k) * blocks, blocks), blocks), :] = pieces[k][...]
    f_ref[channels:, :] = near_ref[...]
    for k, pack in zip(range(2, nz - 1), packs):
        goal = lax.rem(s + k, nz)
        pack[:cols, :] = f_ref[pl.ds(pl.multiple_of(goal * cols, cols), cols), :]
        if nz > 4:
            pack[cols:, :] = cot_ref[...]


def columns(cols_ref, first, plane):
    blocks = plane.shape[0]
    for dy in (-1, 0, 1):
        for dx in (-1, 0, 1):
            tap = first + 3 * (dy + 1) + dx + 1
            cols_ref[tap * blocks : (tap + 1) * blocks, :] = shifted(plane, -dy, -dx).astype(BF16)


def hold_kernel(*refs):
    refs[-1][...] = jnp.zeros(refs[-1].shape, F32)


def token_kernel(token_ref):
    token_ref[...] = jnp.zeros(token_ref.shape, F32)


def input_grad_kernel(nz, nc, pos_ref, begin_ref, cot_ref, even_ref, odd_ref, w_ref, *refs):
    parts = refs[:nc]
    token_ref, cols_ref, sum_ref = refs[nc:]
    blocks = even_ref.shape[0]
    s, c = pos_ref[0], pos_ref[1]
    token_ref[...] = jnp.zeros(token_ref.shape, F32)
    even, odd = even_ref[...].astype(F32), odd_ref[...].astype(F32)
    first = s % 2 == 0
    columns(cols_ref, 0, jnp.where(s < nz - 1, jnp.where(first, even, odd), 0.0))
    columns(cols_ref, 9, cot_ref[...].astype(F32))
    columns(cols_ref, 18, jnp.where(s > 0, jnp.where(first, odd, even), 0.0))
    sum_ref[...] = lax.dot_general(
        w_ref[...], cols_ref[...], (((0,), (0,)), ((), ())), preferred_element_type=F32
    )
    for k in range(nc):
        parts[k][...] = sum_ref[pl.ds(pl.multiple_of((c ^ k) * blocks, blocks), blocks), :]


def conv_part(w_ref, field, dz):
    taps = w_ref.shape[0] // 3
    return jnp.dot(
        w_ref[(dz + 1) * taps : (dz + 2) * taps, :], field, preferred_element_type=F32
    )


def conv_part(w_ref, field, dz):
    taps = w_ref.shape[0] // 3
    return jnp.dot(
        w_ref[(dz + 1) * taps : (dz + 2) * taps, :], field, preferred_element_type=F32
    )


def moved_sum(acc):
    blocks = acc.shape[0] // 9
    total = None
    for dx in (-1, 0, 1):
        for dy in (-1, 0, 1):
            at = (3 * (dy + 1) + dx + 1) * blocks
            term = shifted(acc[at : at + blocks], dy, dx)
            total = term if total is None else total + term
    return total


def moved_rows(plane):
    plane = plane.astype(F32)
    return jnp.concatenate([shifted(plane, -dy, 0).astype(BF16) for dy in (-1, 0, 1)], 0)


def early_kernel(pos_ref, w_ref, f_ref, cot_ref, ce_ref, co_ref, out_ref, moved_ref, token_ref):
    channels = w_ref.shape[1]
    token_ref[...] = jnp.zeros(token_ref.shape, F32)
    out_ref[...] = moved_sum(conv_part(w_ref, f_ref[:channels, :], 0))
    for i, ref in enumerate((cot_ref, ce_ref, co_ref)):
        moved_ref[i] = moved_rows(ref[...])


def output_kernel(nz, nc, scale, pos_ref, last_ref, w_ref, *refs):
    terms = refs[:nc]
    own_ref, moved_ref, f_ref, fe_ref, fo_ref = refs[nc : nc + 5]
    packs = refs[nc + 5 : -5]
    out_ref, back_ref, wg_ref, c_ref, g_ref = refs[-5:]
    total = terms[0][...]
    for term in terms[1:]:
        total = total + term[...]
    back_ref[:, 0, :] = total

    channels = w_ref.shape[1]
    blocks = own_ref.shape[0]
    cols = g_ref.shape[1]
    s = pos_ref[0]
    first = s % 2 == 0
    even, odd = fe_ref[:channels, :], fo_ref[...]
    after = conv_part(w_ref, jnp.where(first, even, odd), 1)
    before = conv_part(w_ref, jnp.where(first, odd, even), -1)
    acc = jnp.where(s < nz - 1, after, 0.0) + jnp.where(s > 0, before, 0.0)
    out_ref[:, 0, :] = own_ref[...] + moved_sum(acc)

    mine = pl.ds(pl.multiple_of(s * cols, cols), cols)
    sources = (s, s ^ 1, odd_partner(s, nz))
    for i, (source, field) in enumerate(zip(sources, (f_ref, fe_ref, fo_ref))):
        c_ref[source] = moved_ref[i]
        g_ref[source] = field[mine, :]
    for k, pack in zip(range(2, nz - 1), packs):
        source = lax.rem(s + nz - k, nz)
        g_ref[source] = pack[:cols, :]
        c_ref[source] = moved_rows(pack[cols:, :] if nz > 4 else fe_ref[channels:, :])

    feats = []
    for z in range(nz):
        field = g_ref[z].astype(F32)
        feats.append(jnp.concatenate([shifted(field, 0, dx).astype(BF16) for dx in (-1, 0, 1)], 0))
    for dz in (-1, 0, 1):
        sums = None
        for z in range(nz):
            if 0 <= z - dz < nz:
                term = lax.dot_general(
                    c_ref[z - dz], feats[z], (((1,), (1,)), ((), ())), preferred_element_type=F32
                )
                sums = term if sums is None else sums + term
        sums = sums * scale
        for dy in range(3):
            for dx in range(3):
                tap = 9 * (dz + 1) + 3 * dy + dx
                wg_ref[tap] = sums[dy * blocks : (dy + 1) * blocks, dx * cols : (dx + 1) * cols]


VMEM = pl.BlockSpec(memory_space=pltpu.VMEM)
SMEM = pl.BlockSpec(memory_space=pltpu.SMEM)


def kernel_call(body, name, outs, args, scratch=(), weight=0):
    return pl.pallas_call(
        body,
        out_shape=outs,
        in_specs=[SMEM if a.dtype == jnp.int32 else VMEM for a in args],
        out_specs=tuple(VMEM for _ in outs),
        scratch_shapes=list(scratch),
        compiler_params=pltpu.CompilerParams(vmem_limit_bytes=VMEM_BYTES),
        cost_estimate=pl.CostEstimate(flops=int(weight), bytes_accessed=0, transcendentals=0),
        name=name,
    )(*args)


def per_device(features, weights, cotangent):
    blocks, depth, plane = features.shape
    channels = weights.shape[2]
    nz = lax.axis_size("sp")
    nc = lax.axis_size("ch")
    cols = channels // nz
    w2 = weights.reshape(27 * blocks, channels)
    feat = features.reshape(blocks, plane)
    cot = cotangent.reshape(blocks, plane)
    pos = jnp.stack([lax.axis_index("sp"), lax.axis_index("ch")]).astype(jnp.int32)

    even_pairs = [(i, i ^ 1) for i in range(nz)]
    odd_pairs = [(i, (((i + 1) ^ 1) - 1) % nz) for i in range(nz)]

    def mixed(k):
        return [(i, i ^ k) for i in range(nc)]

    def of(rows, dtype):
        return jax.ShapeDtypeStruct((rows, plane), dtype)

    small = jax.ShapeDtypeStruct((8, 128), F32)
    work = 2 * 27 * blocks * channels * plane

    cot_even = lax.ppermute(cot, "sp", even_pairs)
    cot_odd = lax.ppermute(cot, "sp", odd_pairs)
    (begin,) = kernel_call(token_kernel, "begin", [small], [], weight=W_BEGIN * work)
    feat, cot_even = lax.optimization_barrier((feat, cot_even))
    pieces = [feat] + [lax.ppermute(feat, "ch", mixed(k)) for k in range(1, nc)]

    *parts, token = kernel_call(
        functools.partial(input_grad_kernel, nz, nc),
        "input_grad",
        [of(blocks, F32)] * nc + [small],
        [pos, begin, cot, cot_even, cot_odd, w2],
        [pltpu.VMEM((27 * blocks, plane), BF16), pltpu.VMEM((channels, plane), F32)],
        W_GRAD * work,
    )
    terms = [parts[0]] + [lax.ppermute(parts[k], "ch", mixed(k)) for k in range(1, nc)]

    far_rows = cols if nz == 4 else cols + blocks
    f_all, *packs = kernel_call(
        functools.partial(gather_kernel, nz, nc),
        "gather",
        [of(channels + blocks, BF16)] + [of(far_rows, BF16)] * (nz - 3),
        [pos, token, cot, cot_odd] + pieces,
    )
    f_odd = lax.ppermute(f_all[:channels], "sp", odd_pairs)
    f_even = lax.ppermute(f_all, "sp", even_pairs)
    far = [
        lax.ppermute(packs[k - 2], "sp", [(i, (i + k) % nz) for i in range(nz)])
        for k in range(2, nz - 1)
    ]
    out_own, moved, done = kernel_call(
        early_kernel,
        "early",
        [of(blocks, F32), jax.ShapeDtypeStruct((3, 3 * blocks, plane), BF16), small],
        [pos, w2, f_all, cot, cot_even, cot_odd],
    )

    block = jax.ShapeDtypeStruct((blocks, 1, plane), F32)
    (last,) = kernel_call(hold_kernel, "hold", [small], [done] + terms, weight=W_TOTAL * work)
    output, back, weight_grad = kernel_call(
        functools.partial(output_kernel, nz, nc, 1.0 / math.sqrt(nz * depth * plane)),
        "outputs",
        [block, block, jax.ShapeDtypeStruct((27, blocks, cols), F32)],
        [pos, last, w2, *terms, out_own, moved, f_all, f_even, f_odd, *far],
        [pltpu.VMEM((nz, 3 * blocks, plane), BF16), pltpu.VMEM((nz, cols, plane), BF16)],
        W_OUT * work,
    )
    return (output, back, weight_grad)


def solution(mesh):
    return jax.shard_map(
        per_device,
        mesh=mesh,
        in_specs=(P("ch", ("grp", "sp"), None), P(None, "ch", None), P("ch", ("grp", "sp"), None)),
        out_specs=(
            P("ch", ("grp", "sp"), None),
            P("ch", ("grp", "sp"), None),
            P("grp", "ch", "sp"),
        ),
        check_vma=False,
    )
```

```python
import functools
import math

import jax
import jax.numpy as jnp
from jax import lax
from jax.experimental import pallas as pl
from jax.experimental.pallas import tpu as pltpu
from jax.sharding import PartitionSpec as P

NX = 64
NY = 10
CELLS = NX * NY
F32 = jnp.float32
BF16 = jnp.bfloat16
W_BEGIN, W_GRAD, W_TOTAL, W_OUT = 8, 1, 0, 4
VMEM_BYTES = 32 * 1024 * 1024


def cell_mask(rows, dy, dx):
    q = lax.broadcasted_iota(jnp.int32, (rows, CELLS), 1)
    x = q % NX + dx
    y = q // NX + dy
    return (x >= 0) & (x < NX) & (y >= 0) & (y < NY)


def shifted(value, dy, dx):
    if dy == 0 and dx == 0:
        return value
    moved = pltpu.roll(value, (-(dy * NX + dx)) % CELLS, 1)
    return jnp.where(cell_mask(value.shape[0], dy, dx), moved, 0.0)


def odd_partner(s, nz):
    return lax.rem(((s + 1) ^ 1) + nz - 1, nz)


def gather_kernel(nz, nc, pos_ref, token_ref, cot_ref, near_ref, *refs):
    pieces, f_ref, packs = refs[:nc], refs[nc], refs[nc + 1 :]
    blocks = cot_ref.shape[0]
    channels = nc * blocks
    cols = channels // nz
    s, c = pos_ref[0], pos_ref[1]
    for k in range(nc):
        f_ref[pl.ds(pl.multiple_of((c ^ k) * blocks, blocks), blocks), :] = pieces[k][...]
    f_ref[channels:, :] = near_ref[...]
    for k, pack in zip(range(2, nz - 1), packs):
        goal = lax.rem(s + k, nz)
        pack[:cols, :] = f_ref[pl.ds(pl.multiple_of(goal * cols, cols), cols), :]
        if nz > 4:
            pack[cols:, :] = cot_ref[...]


def columns(cols_ref, first, plane):
    blocks = plane.shape[0]
    for dy in (-1, 0, 1):
        for dx in (-1, 0, 1):
            tap = first + 3 * (dy + 1) + dx + 1
            cols_ref[tap * blocks : (tap + 1) * blocks, :] = shifted(plane, -dy, -dx).astype(BF16)


def token_kernel(token_ref):
    token_ref[...] = jnp.zeros(token_ref.shape, F32)


def input_grad_kernel(nz, nc, pos_ref, begin_ref, cot_ref, even_ref, odd_ref, w_ref, *refs):
    parts = refs[:nc]
    token_ref, cols_ref, sum_ref = refs[nc:]
    blocks = even_ref.shape[0]
    s, c = pos_ref[0], pos_ref[1]
    token_ref[...] = jnp.zeros(token_ref.shape, F32)
    even, odd = even_ref[...].astype(F32), odd_ref[...].astype(F32)
    first = s % 2 == 0
    columns(cols_ref, 0, jnp.where(s < nz - 1, jnp.where(first, even, odd), 0.0))
    columns(cols_ref, 9, cot_ref[...].astype(F32))
    columns(cols_ref, 18, jnp.where(s > 0, jnp.where(first, odd, even), 0.0))
    sum_ref[...] = lax.dot_general(
        w_ref[...], cols_ref[...], (((0,), (0,)), ((), ())), preferred_element_type=F32
    )
    for k in range(nc):
        parts[k][...] = sum_ref[pl.ds(pl.multiple_of((c ^ k) * blocks, blocks), blocks), :]


def conv_part(w_ref, field, dz):
    taps = w_ref.shape[0] // 3
    return jnp.dot(
        w_ref[(dz + 1) * taps : (dz + 2) * taps, :], field, preferred_element_type=F32
    )


def conv_part(w_ref, field, dz):
    taps = w_ref.shape[0] // 3
    return jnp.dot(
        w_ref[(dz + 1) * taps : (dz + 2) * taps, :], field, preferred_element_type=F32
    )


def moved_sum(acc):
    blocks = acc.shape[0] // 9
    total = None
    for dx in (-1, 0, 1):
        for dy in (-1, 0, 1):
            at = (3 * (dy + 1) + dx + 1) * blocks
            term = shifted(acc[at : at + blocks], dy, dx)
            total = term if total is None else total + term
    return total


def moved_rows(plane):
    plane = plane.astype(F32)
    return jnp.concatenate([shifted(plane, -dy, 0).astype(BF16) for dy in (-1, 0, 1)], 0)


def early_kernel(w_ref, f_ref, cot_ref, ce_ref, co_ref, out_ref, moved_ref):
    channels = w_ref.shape[1]
    out_ref[...] = moved_sum(conv_part(w_ref, f_ref[:channels, :], 0))
    for i, ref in enumerate((cot_ref, ce_ref, co_ref)):
        moved_ref[i] = moved_rows(ref[...])


def output_kernel(nz, scale, pos_ref, w_ref, own_ref, moved_ref, f_ref, fe_ref, fo_ref, *refs):
    packs = refs[:-5]
    out_ref, wg_ref, token_ref, c_ref, g_ref = refs[-5:]
    token_ref[...] = jnp.zeros(token_ref.shape, F32)
    channels = w_ref.shape[1]
    blocks = own_ref.shape[0]
    cols = g_ref.shape[1]
    s = pos_ref[0]
    first = s % 2 == 0
    even, odd = fe_ref[:channels, :], fo_ref[...]
    after = conv_part(w_ref, jnp.where(first, even, odd), 1)
    before = conv_part(w_ref, jnp.where(first, odd, even), -1)
    acc = jnp.where(s < nz - 1, after, 0.0) + jnp.where(s > 0, before, 0.0)
    out_ref[:, 0, :] = own_ref[...] + moved_sum(acc)

    mine = pl.ds(pl.multiple_of(s * cols, cols), cols)
    sources = (s, s ^ 1, odd_partner(s, nz))
    for i, (source, field) in enumerate(zip(sources, (f_ref, fe_ref, fo_ref))):
        c_ref[source] = moved_ref[i]
        g_ref[source] = field[mine, :]
    for k, pack in zip(range(2, nz - 1), packs):
        source = lax.rem(s + nz - k, nz)
        g_ref[source] = pack[:cols, :]
        c_ref[source] = moved_rows(pack[cols:, :] if nz > 4 else fe_ref[channels:, :])

    feats = []
    for z in range(nz):
        field = g_ref[z].astype(F32)
        feats.append(jnp.concatenate([shifted(field, 0, dx).astype(BF16) for dx in (-1, 0, 1)], 0))
    for dz in (-1, 0, 1):
        sums = None
        for z in range(nz):
            if 0 <= z - dz < nz:
                term = lax.dot_general(
                    c_ref[z - dz], feats[z], (((1,), (1,)), ((), ())), preferred_element_type=F32
                )
                sums = term if sums is None else sums + term
        sums = sums * scale
        for dy in range(3):
            for dx in range(3):
                tap = 9 * (dz + 1) + 3 * dy + dx
                wg_ref[tap] = sums[dy * blocks : (dy + 1) * blocks, dx * cols : (dx + 1) * cols]


def total_kernel(token_ref, *refs):
    total = refs[0][...]
    for ref in refs[1:-1]:
        total = total + ref[...]
    refs[-1][:, 0, :] = total


VMEM = pl.BlockSpec(memory_space=pltpu.VMEM)
SMEM = pl.BlockSpec(memory_space=pltpu.SMEM)


def kernel_call(body, name, outs, args, scratch=(), weight=0):
    return pl.pallas_call(
        body,
        out_shape=outs,
        in_specs=[SMEM if a.dtype == jnp.int32 else VMEM for a in args],
        out_specs=tuple(VMEM for _ in outs),
        scratch_shapes=list(scratch),
        compiler_params=pltpu.CompilerParams(vmem_limit_bytes=VMEM_BYTES),
        cost_estimate=pl.CostEstimate(flops=int(weight), bytes_accessed=0, transcendentals=0),
        name=name,
    )(*args)


def per_device(features, weights, cotangent):
    blocks, depth, plane = features.shape
    channels = weights.shape[2]
    nz = lax.axis_size("sp")
    nc = lax.axis_size("ch")
    cols = channels // nz
    w2 = weights.reshape(27 * blocks, channels)
    feat = features.reshape(blocks, plane)
    cot = cotangent.reshape(blocks, plane)
    pos = jnp.stack([lax.axis_index("sp"), lax.axis_index("ch")]).astype(jnp.int32)

    even_pairs = [(i, i ^ 1) for i in range(nz)]
    odd_pairs = [(i, (((i + 1) ^ 1) - 1) % nz) for i in range(nz)]

    def mixed(k):
        return [(i, i ^ k) for i in range(nc)]

    def of(rows, dtype):
        return jax.ShapeDtypeStruct((rows, plane), dtype)

    small = jax.ShapeDtypeStruct((8, 128), F32)
    work = 2 * 27 * blocks * channels * plane

    cot_even = lax.ppermute(cot, "sp", even_pairs)
    cot_odd = lax.ppermute(cot, "sp", odd_pairs)
    (begin,) = kernel_call(token_kernel, "begin", [small], [], weight=W_BEGIN * work)
    feat, cot_even = lax.optimization_barrier((feat, cot_even))
    pieces = [feat] + [lax.ppermute(feat, "ch", mixed(k)) for k in range(1, nc)]

    *parts, token = kernel_call(
        functools.partial(input_grad_kernel, nz, nc),
        "input_grad",
        [of(blocks, F32)] * nc + [small],
        [pos, begin, cot, cot_even, cot_odd, w2],
        [pltpu.VMEM((27 * blocks, plane), BF16), pltpu.VMEM((channels, plane), F32)],
        W_GRAD * work,
    )
    terms = [parts[0]] + [lax.ppermute(parts[k], "ch", mixed(k)) for k in range(1, nc)]

    far_rows = cols if nz == 4 else cols + blocks
    f_all, *packs = kernel_call(
        functools.partial(gather_kernel, nz, nc),
        "gather",
        [of(channels + blocks, BF16)] + [of(far_rows, BF16)] * (nz - 3),
        [pos, token, cot, cot_odd] + pieces,
    )
    f_odd = lax.ppermute(f_all[:channels], "sp", odd_pairs)
    f_even = lax.ppermute(f_all, "sp", even_pairs)
    far = [
        lax.ppermute(packs[k - 2], "sp", [(i, (i + k) % nz) for i in range(nz)])
        for k in range(2, nz - 1)
    ]
    out_own, moved = kernel_call(
        early_kernel,
        "early",
        [of(blocks, F32), jax.ShapeDtypeStruct((3, 3 * blocks, plane), BF16)],
        [w2, f_all, cot, cot_even, cot_odd],
    )

    block = jax.ShapeDtypeStruct((blocks, 1, plane), F32)
    output, weight_grad, last = kernel_call(
        functools.partial(output_kernel, nz, 1.0 / math.sqrt(nz * depth * plane)),
        "outputs",
        [block, jax.ShapeDtypeStruct((27, blocks, cols), F32), small],
        [pos, w2, out_own, moved, f_all, f_even, f_odd, *far],
        [pltpu.VMEM((nz, 3 * blocks, plane), BF16), pltpu.VMEM((nz, cols, plane), BF16)],
        W_OUT * work,
    )
    (back,) = kernel_call(total_kernel, "total", [block], [last] + terms, weight=W_TOTAL * work)
    return (output, back, weight_grad)


def solution(mesh):
    return jax.shard_map(
        per_device,
        mesh=mesh,
        in_specs=(P("ch", ("grp", "sp"), None), P(None, "ch", None), P("ch", ("grp", "sp"), None)),
        out_specs=(
            P("ch", ("grp", "sp"), None),
            P("ch", ("grp", "sp"), None),
            P("grp", "ch", "sp"),
        ),
        check_vma=False,
    )
```

```python
import functools
import math

import jax
import jax.numpy as jnp
from jax import lax
from jax.experimental import pallas as pl
from jax.experimental.pallas import tpu as pltpu
from jax.sharding import PartitionSpec as P

NX = 64
NY = 10
CELLS = NX * NY
F32 = jnp.float32
BF16 = jnp.bfloat16
W_BEGIN, W_GRAD, W_EARLY, W_TOTAL, W_OUT = 8, 1, 4, 0, 0
VMEM_BYTES = 32 * 1024 * 1024


def cell_mask(dy, dx):
    q = lax.broadcasted_iota(jnp.int32, (1, CELLS), 1)
    x = lax.rem(q, NX) + dx
    at = q + NX * dy
    return ((x >= 0) & (x < NX) & (at >= 0) & (at < CELLS)).astype(F32)


def shifted(value, dy, dx):
    if dy == 0 and dx == 0:
        return value
    return pltpu.roll(value, (-(dy * NX + dx)) % CELLS, 1) * cell_mask(dy, dx)


def odd_partner(s, nz):
    return lax.rem(((s + 1) ^ 1) + nz - 1, nz)


def gather_kernel(nz, nc, pos_ref, token_ref, cot_ref, near_ref, *refs):
    pieces, (f_ref, even_ref, odd_ref), packs = refs[:nc], refs[nc : nc + 3], refs[nc + 3 :]
    blocks = cot_ref.shape[0]
    cols = f_ref.shape[0] // nz
    s, c = pos_ref[0], pos_ref[1]

    def block_for(goal):
        return f_ref[pl.ds(pl.multiple_of(goal * cols, cols), cols), :]

    for k in range(nc):
        f_ref[pl.ds(pl.multiple_of((c ^ k) * blocks, blocks), blocks), :] = pieces[k][...]
    even_ref[:cols, :] = block_for(s ^ 1)
    even_ref[cols:, :] = near_ref[...]
    odd_ref[...] = block_for(odd_partner(s, nz))
    for k, pack in zip(range(2, nz - 1), packs):
        pack[:cols, :] = block_for(lax.rem(s + k, nz))
        if nz > 4:
            pack[cols:, :] = cot_ref[...]


def columns(cols_ref, first, plane):
    blocks = plane.shape[0]
    for dy in (-1, 0, 1):
        for dx in (-1, 0, 1):
            tap = first + 3 * (dy + 1) + dx + 1
            cols_ref[tap * blocks : (tap + 1) * blocks, :] = shifted(plane, -dy, -dx).astype(BF16)


def token_kernel(token_ref):
    token_ref[...] = jnp.zeros(token_ref.shape, F32)


def input_grad_kernel(nz, nc, pos_ref, begin_ref, cot_ref, even_ref, odd_ref, w_ref, *refs):
    parts = refs[:nc]
    token_ref, cols_ref, sum_ref = refs[nc:]
    blocks = even_ref.shape[0]
    s, c = pos_ref[0], pos_ref[1]
    token_ref[...] = jnp.zeros(token_ref.shape, F32)
    even, odd = even_ref[...].astype(F32), odd_ref[...].astype(F32)
    first = s % 2 == 0
    columns(cols_ref, 0, jnp.where(s < nz - 1, jnp.where(first, even, odd), 0.0))
    columns(cols_ref, 9, cot_ref[...].astype(F32))
    columns(cols_ref, 18, jnp.where(s > 0, jnp.where(first, odd, even), 0.0))
    sum_ref[...] = lax.dot_general(
        w_ref[...], cols_ref[...], (((0,), (0,)), ((), ())), preferred_element_type=F32
    )
    for k in range(nc):
        parts[k][...] = sum_ref[pl.ds(pl.multiple_of((c ^ k) * blocks, blocks), blocks), :]


def conv_part(w_ref, field, dz):
    taps = w_ref.shape[0] // 3
    rows = pl.ds(pl.multiple_of((dz + 1) * taps, taps), taps)
    return jnp.dot(w_ref[rows, :], field, preferred_element_type=F32)


def moved_sum(acc):
    blocks = acc.shape[0] // 9
    total = None
    for dx in (-1, 0, 1):
        for dy in (-1, 0, 1):
            at = (3 * (dy + 1) + dx + 1) * blocks
            term = shifted(acc[at : at + blocks], dy, dx)
            total = term if total is None else total + term
    return total


def moved_rows(plane):
    plane = plane.astype(F32)
    return jnp.concatenate([shifted(plane, -dy, 0).astype(BF16) for dy in (-1, 0, 1)], 0)


def early_kernel(pos_ref, w_ref, f_ref, cot_ref, ce_ref, co_ref, own_ref, even_ref, odd_ref, moved_ref):
    side = 1 - 2 * lax.rem(pos_ref[0], 2)
    for ref, dz in ((odd_ref, side), (even_ref, -side), (own_ref, 0)):
        ref[...] = moved_sum(conv_part(w_ref, f_ref[...], dz))
    for i, ref in enumerate((cot_ref, ce_ref, co_ref)):
        moved_ref[i] = moved_rows(ref[...])


def weight_grad_kernel(nz, scale, pos_ref, moved_ref, f_ref, ge_ref, go_ref, *refs):
    packs = refs[:-4]
    wg_ref, token_ref, c_ref, g_ref = refs[-4:]
    token_ref[...] = jnp.zeros(token_ref.shape, F32)
    blocks = c_ref.shape[1] // 3
    cols = go_ref.shape[0]
    s = pos_ref[0]

    empty = jnp.zeros(c_ref.shape[1:], BF16)
    c_ref[0] = empty
    c_ref[nz + 1] = empty
    mine = pl.ds(pl.multiple_of(s * cols, cols), cols)
    sources = (s, s ^ 1, odd_partner(s, nz))
    for i, (source, field) in enumerate(zip(sources, (f_ref[mine, :], ge_ref[:cols, :], go_ref[...]))):
        c_ref[source + 1] = moved_ref[i]
        g_ref[source] = field
    for k, pack in zip(range(2, nz - 1), packs):
        source = lax.rem(s + nz - k, nz)
        g_ref[source] = pack[:cols, :]
        c_ref[source + 1] = moved_rows(pack[cols:, :] if nz > 4 else ge_ref[cols:, :])

    sums = None
    for z in range(nz):
        field = g_ref[z].astype(F32)
        fields = jnp.concatenate([shifted(field, 0, dx).astype(BF16) for dx in (-1, 0, 1)], 0)
        term = lax.dot_general(
            c_ref[z : z + 3].reshape(9 * blocks, CELLS),
            fields,
            (((1,), (1,)), ((), ())),
            preferred_element_type=F32,
        )
        sums = term if sums is None else sums + term
    sums = sums * scale
    for tap in range(27):
        dz, dy, dx = tap // 9, tap // 3 % 3, tap % 3
        at = ((2 - dz) * 3 + dy) * blocks
        wg_ref[tap] = sums[at : at + blocks, dx * cols : (dx + 1) * cols]


def total_kernel(nz, pos_ref, token_ref, *refs):
    terms, (own_ref, even_ref, odd_ref, out_ref, back_ref) = refs[:-5], refs[-5:]
    s = pos_ref[0]
    inner = ((s > 0) & (s < nz - 1)).astype(F32)
    out_ref[:, 0, :] = own_ref[...] + even_ref[...] + inner * odd_ref[...]
    total = terms[0][...]
    for term in terms[1:]:
        total = total + term[...]
    back_ref[:, 0, :] = total


VMEM = pl.BlockSpec(memory_space=pltpu.VMEM)
SMEM = pl.BlockSpec(memory_space=pltpu.SMEM)


def kernel_call(body, name, outs, args, scratch=(), weight=0):
    return pl.pallas_call(
        body,
        out_shape=outs,
        in_specs=[SMEM if a.dtype == jnp.int32 else VMEM for a in args],
        out_specs=tuple(VMEM for _ in outs),
        scratch_shapes=list(scratch),
        compiler_params=pltpu.CompilerParams(vmem_limit_bytes=VMEM_BYTES),
        cost_estimate=pl.CostEstimate(flops=int(weight), bytes_accessed=0, transcendentals=0),
        name=name,
    )(*args)


def per_device(features, weights, cotangent):
    blocks, depth, plane = features.shape
    channels = weights.shape[2]
    nz = lax.axis_size("sp")
    nc = lax.axis_size("ch")
    cols = channels // nz
    w2 = weights.reshape(27 * blocks, channels)
    feat = features.reshape(blocks, plane)
    cot = cotangent.reshape(blocks, plane)
    pos = jnp.stack([lax.axis_index("sp"), lax.axis_index("ch")]).astype(jnp.int32)

    even_pairs = [(i, i ^ 1) for i in range(nz)]
    odd_pairs = [(i, (((i + 1) ^ 1) - 1) % nz) for i in range(nz)]

    def mixed(k):
        return [(i, i ^ k) for i in range(nc)]

    def of(rows, dtype):
        return jax.ShapeDtypeStruct((rows, plane), dtype)

    small = jax.ShapeDtypeStruct((8, 128), F32)
    work = 2 * 27 * blocks * channels * plane

    cot_even = lax.ppermute(cot, "sp", even_pairs)
    cot_odd = lax.ppermute(cot, "sp", odd_pairs)
    (begin,) = kernel_call(token_kernel, "begin", [small], [], weight=W_BEGIN * work)
    feat, cot_even = lax.optimization_barrier((feat, cot_even))
    pieces = [feat] + [lax.ppermute(feat, "ch", mixed(k)) for k in range(1, nc)]

    *parts, token = kernel_call(
        functools.partial(input_grad_kernel, nz, nc),
        "input_grad",
        [of(blocks, F32)] * nc + [small],
        [pos, begin, cot, cot_even, cot_odd, w2],
        [pltpu.VMEM((27 * blocks, plane), BF16), pltpu.VMEM((channels, plane), F32)],
        W_GRAD * work,
    )
    terms = [parts[0]] + [lax.ppermute(parts[k], "ch", mixed(k)) for k in (*range(2, nc), 1)]

    far_rows = cols if nz == 4 else cols + blocks
    f_all, to_even, to_odd, *packs = kernel_call(
        functools.partial(gather_kernel, nz, nc),
        "gather",
        [of(channels, BF16), of(cols + blocks, BF16), of(cols, BF16)]
        + [of(far_rows, BF16)] * (nz - 3),
        [pos, token, cot, cot_odd] + pieces,
    )
    g_odd = lax.ppermute(to_odd, "sp", odd_pairs)
    far = [
        lax.ppermute(packs[k - 2], "sp", [(i, (i + k) % nz) for i in range(nz)])
        for k in range(2, nz - 1)
    ]
    g_even = lax.ppermute(to_even, "sp", even_pairs)
    out_own, out_even, out_odd, moved = kernel_call(
        early_kernel,
        "early",
        [of(blocks, F32)] * 3 + [jax.ShapeDtypeStruct((3, 3 * blocks, plane), BF16)],
        [pos, w2, f_all, cot, cot_even, cot_odd],
        weight=W_EARLY * work,
    )
    out_odd = lax.ppermute(out_odd, "sp", odd_pairs)
    out_even = lax.ppermute(out_even, "sp", even_pairs)

    weight_grad, last = kernel_call(
        functools.partial(weight_grad_kernel, nz, 1.0 / math.sqrt(nz * depth * plane)),
        "weight_grad",
        [jax.ShapeDtypeStruct((27, blocks, cols), F32), small],
        [pos, moved, f_all, g_even, g_odd, *far],
        [pltpu.VMEM((nz + 2, 3 * blocks, plane), BF16), pltpu.VMEM((nz, cols, plane), BF16)],
        W_OUT * work,
    )
    block = jax.ShapeDtypeStruct((blocks, 1, plane), F32)
    output, back = kernel_call(
        functools.partial(total_kernel, nz),
        "total",
        [block, block],
        [pos, last, *terms, out_own, out_even, out_odd],
        weight=W_TOTAL * work,
    )
    return (output, back, weight_grad)


def solution(mesh):
    return jax.shard_map(
        per_device,
        mesh=mesh,
        in_specs=(P("ch", ("grp", "sp"), None), P(None, "ch", None), P("ch", ("grp", "sp"), None)),
        out_specs=(
            P("ch", ("grp", "sp"), None),
            P("ch", ("grp", "sp"), None),
            P("grp", "ch", "sp"),
        ),
        check_vma=False,
    )
```

```python
import functools
import math

import jax
import jax.numpy as jnp
from jax import lax
from jax.experimental import pallas as pl
from jax.experimental.pallas import tpu as pltpu
from jax.sharding import PartitionSpec as P

NX = 64
NY = 10
CELLS = NX * NY
F32 = jnp.float32
BF16 = jnp.bfloat16
W_BEGIN, W_GRAD, W_TOTAL, W_OUT = 8, 1, 5, 0
VMEM_BYTES = 32 * 1024 * 1024


def cell_mask(dy, dx):
    q = lax.broadcasted_iota(jnp.int32, (1, CELLS), 1)
    x = lax.rem(q, NX) + dx
    at = q + NX * dy
    return ((x >= 0) & (x < NX) & (at >= 0) & (at < CELLS)).astype(F32)


def shifted(value, dy, dx):
    if dy == 0 and dx == 0:
        return value
    return pltpu.roll(value, (-(dy * NX + dx)) % CELLS, 1) * cell_mask(dy, dx)


def odd_partner(s, nz):
    return lax.rem(((s + 1) ^ 1) + nz - 1, nz)


def gather_kernel(nz, nc, pos_ref, token_ref, cot_ref, near_ref, *refs):
    pieces, f_ref, packs = refs[:nc], refs[nc], refs[nc + 1 :]
    blocks = cot_ref.shape[0]
    channels = nc * blocks
    cols = channels // nz
    s, c = pos_ref[0], pos_ref[1]
    for k in range(nc):
        f_ref[pl.ds(pl.multiple_of((c ^ k) * blocks, blocks), blocks), :] = pieces[k][...]
    f_ref[channels:, :] = near_ref[...]
    for k, pack in zip(range(2, nz - 1), packs):
        goal = lax.rem(s + k, nz)
        pack[:cols, :] = f_ref[pl.ds(pl.multiple_of(goal * cols, cols), cols), :]
        if nz > 4:
            pack[cols:, :] = cot_ref[...]


def columns(cols_ref, first, plane):
    blocks = plane.shape[0]
    for dy in (-1, 0, 1):
        for dx in (-1, 0, 1):
            tap = first + 3 * (dy + 1) + dx + 1
            cols_ref[tap * blocks : (tap + 1) * blocks, :] = shifted(plane, -dy, -dx).astype(BF16)


def hold_kernel(*refs):
    refs[-1][...] = jnp.zeros(refs[-1].shape, F32)


def token_kernel(token_ref):
    token_ref[...] = jnp.zeros(token_ref.shape, F32)


def input_grad_kernel(nz, nc, pos_ref, begin_ref, cot_ref, even_ref, odd_ref, w_ref, *refs):
    parts = refs[:nc]
    token_ref, cols_ref, sum_ref = refs[nc:]
    blocks = even_ref.shape[0]
    s, c = pos_ref[0], pos_ref[1]
    token_ref[...] = jnp.zeros(token_ref.shape, F32)
    even, odd = even_ref[...].astype(F32), odd_ref[...].astype(F32)
    first = s % 2 == 0
    columns(cols_ref, 0, jnp.where(s < nz - 1, jnp.where(first, even, odd), 0.0))
    columns(cols_ref, 9, cot_ref[...].astype(F32))
    columns(cols_ref, 18, jnp.where(s > 0, jnp.where(first, odd, even), 0.0))
    sum_ref[...] = lax.dot_general(
        w_ref[...], cols_ref[...], (((0,), (0,)), ((), ())), preferred_element_type=F32
    )
    for k in range(nc):
        parts[k][...] = sum_ref[pl.ds(pl.multiple_of((c ^ k) * blocks, blocks), blocks), :]


def conv_part(w_ref, field, dz):
    taps = w_ref.shape[0] // 3
    return jnp.dot(
        w_ref[(dz + 1) * taps : (dz + 2) * taps, :], field, preferred_element_type=F32
    )


def conv_part(w_ref, field, dz):
    taps = w_ref.shape[0] // 3
    return jnp.dot(
        w_ref[(dz + 1) * taps : (dz + 2) * taps, :], field, preferred_element_type=F32
    )


def moved_sum(acc):
    blocks = acc.shape[0] // 9
    total = None
    for dx in (-1, 0, 1):
        for dy in (-1, 0, 1):
            at = (3 * (dy + 1) + dx + 1) * blocks
            term = shifted(acc[at : at + blocks], dy, dx)
            total = term if total is None else total + term
    return total


def moved_rows(plane):
    plane = plane.astype(F32)
    return jnp.concatenate([shifted(plane, -dy, 0).astype(BF16) for dy in (-1, 0, 1)], 0)


def early_kernel(pos_ref, w_ref, f_ref, cot_ref, ce_ref, co_ref, out_ref, moved_ref, token_ref):
    channels = w_ref.shape[1]
    token_ref[...] = jnp.zeros(token_ref.shape, F32)
    out_ref[...] = moved_sum(conv_part(w_ref, f_ref[:channels, :], 0))
    for i, ref in enumerate((cot_ref, ce_ref, co_ref)):
        moved_ref[i] = moved_rows(ref[...])


def block_of(ref, goal, cols):
    return ref[pl.ds(pl.multiple_of(goal * cols, cols), cols), :]


def output_kernel(nz, nc, scale, pos_ref, last_ref, w_ref, *refs):
    terms = refs[:nc]
    own_ref, moved_ref, f_ref, fe_ref, fo_ref = refs[nc : nc + 5]
    packs = refs[nc + 5 : -9]
    out_hbm, back_hbm, wg_hbm, out_ref, back_ref, wg_ref, c_ref, g_ref, sems = refs[-9:]
    total = terms[0][...]
    for term in terms[1:]:
        total = total + term[...]
    back_ref[:, 0, :] = total
    copies = [pltpu.make_async_copy(back_ref, back_hbm, sems.at[0])]
    copies[0].start()

    channels = w_ref.shape[1]
    blocks = own_ref.shape[0]
    cols = g_ref.shape[1]
    s = pos_ref[0]

    empty = jnp.zeros(c_ref.shape[1:], BF16)
    c_ref[0] = empty
    c_ref[nz + 1] = empty
    even, odd = s ^ 1, odd_partner(s, nz)
    for i, (source, field) in enumerate(((s, f_ref), (even, fe_ref), (odd, fo_ref))):
        c_ref[source + 1] = moved_ref[i]
        g_ref[source] = block_of(field, s, cols)
    for k, pack in zip(range(2, nz - 1), packs):
        source = lax.rem(s + nz - k, nz)
        g_ref[source] = pack[:cols, :]
        c_ref[source + 1] = moved_rows(pack[cols:, :] if nz > 4 else fe_ref[channels:, :])

    sums = None
    for z in range(nz):
        field = g_ref[z].astype(F32)
        fields = jnp.concatenate([shifted(field, 0, dx).astype(BF16) for dx in (-1, 0, 1)], 0)
        term = lax.dot_general(
            c_ref[z : z + 3].reshape(9 * blocks, CELLS),
            fields,
            (((1,), (1,)), ((), ())),
            preferred_element_type=F32,
        )
        sums = term if sums is None else sums + term
    sums = sums * scale
    for dz in range(3):
        for dy in range(3):
            at = ((2 - dz) * 3 + dy) * blocks
            for dx in range(3):
                wg_ref[9 * dz + 3 * dy + dx] = sums[at : at + blocks, dx * cols : (dx + 1) * cols]
        taps = pl.ds(9 * dz, 9)
        copies.append(pltpu.make_async_copy(wg_ref.at[taps], wg_hbm.at[taps], sems.at[dz + 1]))
        copies[-1].start()

    first = s % 2 == 0
    even, odd = fe_ref[:channels, :], fo_ref[...]
    after = conv_part(w_ref, jnp.where(first, even, odd), 1)
    before = conv_part(w_ref, jnp.where(first, odd, even), -1)
    acc = jnp.where(s < nz - 1, after, 0.0) + jnp.where(s > 0, before, 0.0)
    out_ref[:, 0, :] = own_ref[...] + moved_sum(acc)
    copies.append(pltpu.make_async_copy(out_ref, out_hbm, sems.at[4]))
    copies[-1].start()
    for copy in copies:
        copy.wait()


VMEM = pl.BlockSpec(memory_space=pltpu.VMEM)
SMEM = pl.BlockSpec(memory_space=pltpu.SMEM)
ANY = pl.BlockSpec(memory_space=pl.ANY)


def kernel_call(body, name, outs, args, scratch=(), weight=0, far_outs=()):
    return pl.pallas_call(
        body,
        out_shape=outs,
        in_specs=[SMEM if a.dtype == jnp.int32 else VMEM for a in args],
        out_specs=tuple(ANY if i in far_outs else VMEM for i in range(len(outs))),
        scratch_shapes=list(scratch),
        compiler_params=pltpu.CompilerParams(vmem_limit_bytes=VMEM_BYTES),
        cost_estimate=pl.CostEstimate(flops=weight, bytes_accessed=0, transcendentals=0),
        name=name,
    )(*args)


def per_device(features, weights, cotangent):
    blocks, depth, plane = features.shape
    channels = weights.shape[2]
    nz = lax.axis_size("sp")
    nc = lax.axis_size("ch")
    cols = channels // nz
    w2 = weights.reshape(27 * blocks, channels)
    feat = features.reshape(blocks, plane)
    cot = cotangent.reshape(blocks, plane)
    pos = jnp.stack([lax.axis_index("sp"), lax.axis_index("ch")]).astype(jnp.int32)

    even_pairs = [(i, i ^ 1) for i in range(nz)]
    odd_pairs = [(i, (((i + 1) ^ 1) - 1) % nz) for i in range(nz)]

    def mixed(k):
        return [(i, i ^ k) for i in range(nc)]

    def of(rows, dtype):
        return jax.ShapeDtypeStruct((rows, plane), dtype)

    small = jax.ShapeDtypeStruct((8, 128), F32)
    work = 2 * 27 * blocks * channels * plane

    cot_even = lax.ppermute(cot, "sp", even_pairs)
    cot_odd = lax.ppermute(cot, "sp", odd_pairs)
    (begin,) = kernel_call(token_kernel, "begin", [small], [], weight=W_BEGIN * work)
    feat, cot_even = lax.optimization_barrier((feat, cot_even))
    pieces = [feat] + [lax.ppermute(feat, "ch", mixed(k)) for k in range(1, nc)]

    *parts, token = kernel_call(
        functools.partial(input_grad_kernel, nz, nc),
        "input_grad",
        [of(blocks, F32)] * nc + [small],
        [pos, begin, cot, cot_even, cot_odd, w2],
        [pltpu.VMEM((27 * blocks, plane), BF16), pltpu.VMEM((channels, plane), F32)],
        W_GRAD * work,
    )
    terms = [parts[0]] + [lax.ppermute(parts[k], "ch", mixed(k)) for k in range(1, nc)]

    far_rows = cols if nz == 4 else cols + blocks
    f_all, *packs = kernel_call(
        functools.partial(gather_kernel, nz, nc),
        "gather",
        [of(channels + blocks, BF16)] + [of(far_rows, BF16)] * (nz - 3),
        [pos, token, cot, cot_odd] + pieces,
    )
    f_odd = lax.ppermute(f_all[:channels], "sp", odd_pairs)
    f_even = lax.ppermute(f_all, "sp", even_pairs)
    far = [
        lax.ppermute(packs[k - 2], "sp", [(i, (i + k) % nz) for i in range(nz)])
        for k in range(2, nz - 1)
    ]
    out_own, moved, done = kernel_call(
        early_kernel,
        "early",
        [of(blocks, F32), jax.ShapeDtypeStruct((3, 3 * blocks, plane), BF16), small],
        [pos, w2, f_all, cot, cot_even, cot_odd],
    )

    block = jax.ShapeDtypeStruct((blocks, 1, plane), F32)
    (last,) = kernel_call(hold_kernel, "hold", [small], [done] + terms, weight=W_TOTAL * work)
    output, back, weight_grad = kernel_call(
        functools.partial(output_kernel, nz, nc, 1.0 / math.sqrt(nz * depth * plane)),
        "outputs",
        [block, block, jax.ShapeDtypeStruct((27, blocks, cols), F32)],
        [pos, last, w2, *terms, out_own, moved, f_all, f_even, f_odd, *far],
        [
            pltpu.VMEM((blocks, 1, plane), F32),
            pltpu.VMEM((blocks, 1, plane), F32),
            pltpu.VMEM((27, blocks, cols), F32),
            pltpu.VMEM((nz + 2, 3 * blocks, plane), BF16),
            pltpu.VMEM((nz, cols, plane), BF16),
            pltpu.SemaphoreType.DMA((5,)),
        ],
        W_OUT * work,
        (0, 1, 2),
    )
    return (output, back, weight_grad)


def solution(mesh):
    return jax.shard_map(
        per_device,
        mesh=mesh,
        in_specs=(P("ch", ("grp", "sp"), None), P(None, "ch", None), P("ch", ("grp", "sp"), None)),
        out_specs=(
            P("ch", ("grp", "sp"), None),
            P("ch", ("grp", "sp"), None),
            P("grp", "ch", "sp"),
        ),
        check_vma=False,
    )
```

```python
import functools
import math

import jax
import jax.numpy as jnp
from jax import lax
from jax.experimental import pallas as pl
from jax.experimental.pallas import tpu as pltpu
from jax.sharding import PartitionSpec as P

NX = 64
NY = 10
CELLS = NX * NY
F32 = jnp.float32
BF16 = jnp.bfloat16
W_GATHER, W_EARLY, W_BEGIN, W_GRAD, W_FOLD, W_TOTAL, W_OUT = 2, 0, 8, 1, 0, 3, 0
VMEM_BYTES = 32 * 1024 * 1024


def cell_mask(dy, dx):
    q = lax.broadcasted_iota(jnp.int32, (1, CELLS), 1)
    x = lax.rem(q, NX) + dx
    at = q + NX * dy
    return ((x >= 0) & (x < NX) & (at >= 0) & (at < CELLS)).astype(F32)


def shifted(value, dy, dx):
    if dy == 0 and dx == 0:
        return value
    return pltpu.roll(value, (-(dy * NX + dx)) % CELLS, 1) * cell_mask(dy, dx)


def odd_partner(s, nz):
    return lax.rem(((s + 1) ^ 1) + nz - 1, nz)


def gather_kernel(nz, nc, pos_ref, token_ref, cot_ref, near_ref, *refs):
    pieces, (f_ref, even_ref), packs = refs[:nc], refs[nc : nc + 2], refs[nc + 2 :]
    blocks = cot_ref.shape[0]
    channels = nc * blocks
    cols = channels // nz
    s, c = pos_ref[0], pos_ref[1]
    for k in range(nc):
        f_ref[pl.ds(pl.multiple_of((c ^ k) * blocks, blocks), blocks), :] = pieces[k][...]
    even_ref[:cols, :] = f_ref[pl.ds(pl.multiple_of((s ^ 1) * cols, cols), cols), :]
    even_ref[cols:, :] = near_ref[...]
    for k, pack in zip(range(2, nz - 1), packs):
        goal = lax.rem(s + k, nz)
        pack[:cols, :] = f_ref[pl.ds(pl.multiple_of(goal * cols, cols), cols), :]
        if nz > 4:
            pack[cols:, :] = cot_ref[...]


def columns(cols_ref, first, plane):
    blocks = plane.shape[0]
    for dy in (-1, 0, 1):
        for dx in (-1, 0, 1):
            tap = first + 3 * (dy + 1) + dx + 1
            cols_ref[tap * blocks : (tap + 1) * blocks, :] = shifted(plane, -dy, -dx).astype(BF16)


def fold_kernel(own_ref, got_ref, both_ref):
    both_ref[...] = own_ref[...] + got_ref[...]


def hold_kernel(*refs):
    refs[-1][...] = jnp.zeros(refs[-1].shape, F32)


def token_kernel(token_ref):
    token_ref[...] = jnp.zeros(token_ref.shape, F32)


def input_grad_kernel(nz, nc, pos_ref, begin_ref, cot_ref, even_ref, odd_ref, w_ref, *refs):
    parts = refs[:nc]
    token_ref, cols_ref, sum_ref = refs[nc:]
    blocks = even_ref.shape[0]
    s, c = pos_ref[0], pos_ref[1]
    token_ref[...] = jnp.zeros(token_ref.shape, F32)
    even, odd = even_ref[...].astype(F32), odd_ref[...].astype(F32)
    first = s % 2 == 0
    columns(cols_ref, 0, jnp.where(s < nz - 1, jnp.where(first, even, odd), 0.0))
    columns(cols_ref, 9, cot_ref[...].astype(F32))
    columns(cols_ref, 18, jnp.where(s > 0, jnp.where(first, odd, even), 0.0))
    sum_ref[...] = lax.dot_general(
        w_ref[...], cols_ref[...], (((0,), (0,)), ((), ())), preferred_element_type=F32
    )
    for k in range(nc):
        parts[k][...] = sum_ref[pl.ds(pl.multiple_of((c ^ k) * blocks, blocks), blocks), :]


def conv_part(w_ref, field, dz):
    taps = w_ref.shape[0] // 3
    rows = pl.ds(pl.multiple_of((dz + 1) * taps, taps), taps)
    return jnp.dot(w_ref[rows, :], field, preferred_element_type=F32)


def moved_sum(acc):
    blocks = acc.shape[0] // 9
    total = None
    for dx in (-1, 0, 1):
        for dy in (-1, 0, 1):
            at = (3 * (dy + 1) + dx + 1) * blocks
            term = shifted(acc[at : at + blocks], dy, dx)
            total = term if total is None else total + term
    return total


def moved_rows(plane):
    plane = plane.astype(F32)
    return jnp.concatenate([shifted(plane, -dy, 0).astype(BF16) for dy in (-1, 0, 1)], 0)


def side_of(s):
    return 1 - 2 * lax.rem(s, 2)


def early_kernel(pos_ref, w_ref, f_ref, cot_ref, ce_ref, co_ref, own_ref, even_ref, moved_ref, token_ref):
    token_ref[...] = jnp.zeros(token_ref.shape, F32)
    even_ref[...] = moved_sum(conv_part(w_ref, f_ref[...], -side_of(pos_ref[0])))
    own_ref[...] = moved_sum(conv_part(w_ref, f_ref[...], 0))
    for i, ref in enumerate((cot_ref, ce_ref, co_ref)):
        moved_ref[i] = moved_rows(ref[...])


def output_kernel(nz, count, scale, pos_ref, last_ref, w_ref, *refs):
    terms = refs[:count]
    own_ref, part_ref, moved_ref, f_ref, ge_ref, fo_ref = refs[count : count + 6]
    packs = refs[count + 6 : -5]
    out_ref, back_ref, wg_ref, c_ref, g_ref = refs[-5:]
    total = terms[0][...]
    for term in terms[1:]:
        total = total + term[...]
    back_ref[:, 0, :] = total

    blocks = own_ref.shape[0]
    cols = g_ref.shape[1]
    s = pos_ref[0]
    inner = ((s > 0) & (s < nz - 1)).astype(F32)
    beyond = moved_sum(conv_part(w_ref, fo_ref[...], -side_of(s)))
    out_ref[:, 0, :] = own_ref[...] + part_ref[...] + inner * beyond

    mine = pl.ds(pl.multiple_of(s * cols, cols), cols)
    sources = (s, s ^ 1, odd_partner(s, nz))
    for i, (source, field) in enumerate(zip(sources, (f_ref[mine, :], ge_ref[:cols, :], fo_ref[mine, :]))):
        c_ref[source] = moved_ref[i]
        g_ref[source] = field
    for k, pack in zip(range(2, nz - 1), packs):
        source = lax.rem(s + nz - k, nz)
        g_ref[source] = pack[:cols, :]
        c_ref[source] = moved_rows(pack[cols:, :] if nz > 4 else ge_ref[cols:, :])

    feats = []
    for z in range(nz):
        field = g_ref[z].astype(F32)
        feats.append(jnp.concatenate([shifted(field, 0, dx).astype(BF16) for dx in (-1, 0, 1)], 0))
    for dz in (-1, 0, 1):
        sums = None
        for z in range(nz):
            if 0 <= z - dz < nz:
                term = lax.dot_general(
                    c_ref[z - dz], feats[z], (((1,), (1,)), ((), ())), preferred_element_type=F32
                )
                sums = term if sums is None else sums + term
        sums = sums * scale
        for dy in range(3):
            for dx in range(3):
                tap = 9 * (dz + 1) + 3 * dy + dx
                wg_ref[tap] = sums[dy * blocks : (dy + 1) * blocks, dx * cols : (dx + 1) * cols]


VMEM = pl.BlockSpec(memory_space=pltpu.VMEM)
SMEM = pl.BlockSpec(memory_space=pltpu.SMEM)


def kernel_call(body, name, outs, args, scratch=(), weight=0):
    return pl.pallas_call(
        body,
        out_shape=outs,
        in_specs=[SMEM if a.dtype == jnp.int32 else VMEM for a in args],
        out_specs=tuple(VMEM for _ in outs),
        scratch_shapes=list(scratch),
        compiler_params=pltpu.CompilerParams(vmem_limit_bytes=VMEM_BYTES),
        cost_estimate=pl.CostEstimate(flops=int(weight), bytes_accessed=0, transcendentals=0),
        name=name,
    )(*args)


def per_device(features, weights, cotangent):
    blocks, depth, plane = features.shape
    channels = weights.shape[2]
    nz = lax.axis_size("sp")
    nc = lax.axis_size("ch")
    cols = channels // nz
    w2 = weights.reshape(27 * blocks, channels)
    feat = features.reshape(blocks, plane)
    cot = cotangent.reshape(blocks, plane)
    pos = jnp.stack([lax.axis_index("sp"), lax.axis_index("ch")]).astype(jnp.int32)

    even_pairs = [(i, i ^ 1) for i in range(nz)]
    odd_pairs = [(i, (((i + 1) ^ 1) - 1) % nz) for i in range(nz)]

    def mixed(k):
        return [(i, i ^ k) for i in range(nc)]

    def of(rows, dtype):
        return jax.ShapeDtypeStruct((rows, plane), dtype)

    small = jax.ShapeDtypeStruct((8, 128), F32)
    work = 2 * 27 * blocks * channels * plane

    cot_even = lax.ppermute(cot, "sp", even_pairs)
    cot_odd = lax.ppermute(cot, "sp", odd_pairs)
    (begin,) = kernel_call(token_kernel, "begin", [small], [], weight=W_BEGIN * work)
    feat, cot_even = lax.optimization_barrier((feat, cot_even))
    pieces = [feat] + [lax.ppermute(feat, "ch", mixed(k)) for k in range(1, nc)]

    *parts, token = kernel_call(
        functools.partial(input_grad_kernel, nz, nc),
        "input_grad",
        [of(blocks, F32)] * nc + [small],
        [pos, begin, cot, cot_even, cot_odd, w2],
        [pltpu.VMEM((27 * blocks, plane), BF16), pltpu.VMEM((channels, plane), F32)],
        W_GRAD * work,
    )
    terms = [parts[0]]
    for k in range(2, nc, 2):
        got = lax.ppermute(parts[k + 1], "ch", mixed(1))
        (both,) = kernel_call(fold_kernel, "fold", [of(blocks, F32)], [parts[k], got], weight=W_FOLD * work)
        terms.append(lax.ppermute(both, "ch", mixed(k)))
    terms.append(lax.ppermute(parts[1], "ch", mixed(1)))

    far_rows = cols if nz == 4 else cols + blocks
    f_all, to_even, *packs = kernel_call(
        functools.partial(gather_kernel, nz, nc),
        "gather",
        [of(channels, BF16), of(cols + blocks, BF16)] + [of(far_rows, BF16)] * (nz - 3),
        [pos, token, cot, cot_odd] + pieces,
        weight=W_GATHER * work,
    )
    f_odd = lax.ppermute(f_all, "sp", odd_pairs)
    g_even = lax.ppermute(to_even, "sp", even_pairs)
    far = [
        lax.ppermute(packs[k - 2], "sp", [(i, (i + k) % nz) for i in range(nz)])
        for k in range(2, nz - 1)
    ]
    out_own, out_even, moved, done = kernel_call(
        early_kernel,
        "early",
        [of(blocks, F32)] * 2 + [jax.ShapeDtypeStruct((3, 3 * blocks, plane), BF16), small],
        [pos, w2, f_all, cot, cot_even, cot_odd],
        weight=W_EARLY * work,
    )
    out_even = lax.ppermute(out_even, "sp", even_pairs)

    block = jax.ShapeDtypeStruct((blocks, 1, plane), F32)
    (last,) = kernel_call(hold_kernel, "hold", [small], [done] + terms, weight=W_TOTAL * work)
    output, back, weight_grad = kernel_call(
        functools.partial(output_kernel, nz, len(terms), 1.0 / math.sqrt(nz * depth * plane)),
        "outputs",
        [block, block, jax.ShapeDtypeStruct((27, blocks, cols), F32)],
        [pos, last, w2, *terms, out_own, out_even, moved, f_all, g_even, f_odd, *far],
        [pltpu.VMEM((nz, 3 * blocks, plane), BF16), pltpu.VMEM((nz, cols, plane), BF16)],
        W_OUT * work,
    )
    return (output, back, weight_grad)


def solution(mesh):
    return jax.shard_map(
        per_device,
        mesh=mesh,
        in_specs=(P("ch", ("grp", "sp"), None), P(None, "ch", None), P("ch", ("grp", "sp"), None)),
        out_specs=(
            P("ch", ("grp", "sp"), None),
            P("ch", ("grp", "sp"), None),
            P("grp", "ch", "sp"),
        ),
        check_vma=False,
    )
```

```python
import functools
import math

import jax
import jax.numpy as jnp
from jax import lax
from jax.experimental import pallas as pl
from jax.experimental.pallas import tpu as pltpu
from jax.sharding import PartitionSpec as P

NX = 64
NY = 10
CELLS = NX * NY
F32 = jnp.float32
BF16 = jnp.bfloat16
W_GATHER, W_EARLY, W_BEGIN, W_GRAD, W_FOLD, W_TOTAL, W_OUT = 2, 0, 8, 1, 0, 1, 0
VMEM_BYTES = 32 * 1024 * 1024


def cell_mask(dy, dx):
    q = lax.broadcasted_iota(jnp.int32, (1, CELLS), 1)
    x = lax.rem(q, NX) + dx
    at = q + NX * dy
    return ((x >= 0) & (x < NX) & (at >= 0) & (at < CELLS)).astype(F32)


def shifted(value, dy, dx):
    if dy == 0 and dx == 0:
        return value
    return pltpu.roll(value, (-(dy * NX + dx)) % CELLS, 1) * cell_mask(dy, dx)


def odd_partner(s, nz):
    return lax.rem(((s + 1) ^ 1) + nz - 1, nz)


def gather_kernel(nz, nc, pos_ref, token_ref, cot_ref, near_ref, *refs):
    pieces, (f_ref, even_ref, odd_ref), packs = refs[:nc], refs[nc : nc + 3], refs[nc + 3 :]
    blocks = cot_ref.shape[0]
    cols = f_ref.shape[0] // nz
    s, c = pos_ref[0], pos_ref[1]

    def block_for(goal):
        return f_ref[pl.ds(pl.multiple_of(goal * cols, cols), cols), :]

    for k in range(nc):
        f_ref[pl.ds(pl.multiple_of((c ^ k) * blocks, blocks), blocks), :] = pieces[k][...]
    even_ref[:cols, :] = block_for(s ^ 1)
    even_ref[cols:, :] = near_ref[...]
    odd_ref[...] = block_for(odd_partner(s, nz))
    for k, pack in zip(range(2, nz - 1), packs):
        pack[:cols, :] = block_for(lax.rem(s + k, nz))
        if nz > 4:
            pack[cols:, :] = cot_ref[...]


def columns(cols_ref, first, plane):
    blocks = plane.shape[0]
    for dy in (-1, 0, 1):
        for dx in (-1, 0, 1):
            tap = first + 3 * (dy + 1) + dx + 1
            cols_ref[tap * blocks : (tap + 1) * blocks, :] = shifted(plane, -dy, -dx).astype(BF16)


def token_kernel(token_ref):
    token_ref[...] = jnp.zeros(token_ref.shape, F32)


def input_grad_kernel(nz, nc, pos_ref, begin_ref, cot_ref, even_ref, odd_ref, w_ref, *refs):
    parts = refs[:nc]
    token_ref, cols_ref, sum_ref = refs[nc:]
    blocks = even_ref.shape[0]
    s, c = pos_ref[0], pos_ref[1]
    token_ref[...] = jnp.zeros(token_ref.shape, F32)
    even, odd = even_ref[...].astype(F32), odd_ref[...].astype(F32)
    first = s % 2 == 0
    columns(cols_ref, 0, jnp.where(s < nz - 1, jnp.where(first, even, odd), 0.0))
    columns(cols_ref, 9, cot_ref[...].astype(F32))
    columns(cols_ref, 18, jnp.where(s > 0, jnp.where(first, odd, even), 0.0))
    sum_ref[...] = lax.dot_general(
        w_ref[...], cols_ref[...], (((0,), (0,)), ((), ())), preferred_element_type=F32
    )
    for k in range(nc):
        parts[k][...] = sum_ref[pl.ds(pl.multiple_of((c ^ k) * blocks, blocks), blocks), :]


def conv_part(w_ref, field, dz):
    taps = w_ref.shape[0] // 3
    rows = pl.ds(pl.multiple_of((dz + 1) * taps, taps), taps)
    return jnp.dot(w_ref[rows, :], field, preferred_element_type=F32)


def moved_sum(acc):
    blocks = acc.shape[0] // 9
    total = None
    for dx in (-1, 0, 1):
        for dy in (-1, 0, 1):
            at = (3 * (dy + 1) + dx + 1) * blocks
            term = shifted(acc[at : at + blocks], dy, dx)
            total = term if total is None else total + term
    return total


def moved_rows(plane):
    plane = plane.astype(F32)
    return jnp.concatenate([shifted(plane, -dy, 0).astype(BF16) for dy in (-1, 0, 1)], 0)


def early_kernel(pos_ref, w_ref, f_ref, cot_ref, ce_ref, co_ref, own_ref, even_ref, odd_ref, moved_ref):
    side = 1 - 2 * lax.rem(pos_ref[0], 2)
    for ref, dz in ((odd_ref, side), (even_ref, -side), (own_ref, 0)):
        ref[...] = moved_sum(conv_part(w_ref, f_ref[...], dz))
    for i, ref in enumerate((cot_ref, ce_ref, co_ref)):
        moved_ref[i] = moved_rows(ref[...])


def weight_grad_kernel(nz, scale, pos_ref, moved_ref, f_ref, ge_ref, go_ref, *refs):
    packs = refs[:-4]
    wg_ref, token_ref, c_ref, g_ref = refs[-4:]
    token_ref[...] = jnp.zeros(token_ref.shape, F32)
    blocks = c_ref.shape[1] // 3
    cols = go_ref.shape[0]
    s = pos_ref[0]

    empty = jnp.zeros(c_ref.shape[1:], BF16)
    c_ref[0] = empty
    c_ref[nz + 1] = empty
    mine = pl.ds(pl.multiple_of(s * cols, cols), cols)
    sources = (s, s ^ 1, odd_partner(s, nz))
    for i, (source, field) in enumerate(zip(sources, (f_ref[mine, :], ge_ref[:cols, :], go_ref[...]))):
        c_ref[source + 1] = moved_ref[i]
        g_ref[source] = field
    for k, pack in zip(range(2, nz - 1), packs):
        source = lax.rem(s + nz - k, nz)
        g_ref[source] = pack[:cols, :]
        c_ref[source + 1] = moved_rows(pack[cols:, :] if nz > 4 else ge_ref[cols:, :])

    sums = None
    for z in range(nz):
        field = g_ref[z].astype(F32)
        fields = jnp.concatenate([shifted(field, 0, dx).astype(BF16) for dx in (-1, 0, 1)], 0)
        term = lax.dot_general(
            c_ref[z : z + 3].reshape(9 * blocks, CELLS),
            fields,
            (((1,), (1,)), ((), ())),
            preferred_element_type=F32,
        )
        sums = term if sums is None else sums + term
    sums = sums * scale
    for tap in range(27):
        dz, dy, dx = tap // 9, tap // 3 % 3, tap % 3
        at = ((2 - dz) * 3 + dy) * blocks
        wg_ref[tap] = sums[at : at + blocks, dx * cols : (dx + 1) * cols]


def fold_kernel(own_ref, got_ref, both_ref):
    both_ref[...] = own_ref[...] + got_ref[...]


def input_total_kernel(token_ref, *refs):
    terms, back_ref, done_ref = refs[:-2], refs[-2], refs[-1]
    done_ref[...] = jnp.zeros(done_ref.shape, F32)
    total = terms[0][...]
    for term in terms[1:]:
        total = total + term[...]
    back_ref[:, 0, :] = total


def output_total_kernel(nz, pos_ref, token_ref, own_ref, odd_ref, even_ref, out_ref):
    s = pos_ref[0]
    inner = ((s > 0) & (s < nz - 1)).astype(F32)
    out_ref[:, 0, :] = own_ref[...] + even_ref[...] + inner * odd_ref[...]


VMEM = pl.BlockSpec(memory_space=pltpu.VMEM)
SMEM = pl.BlockSpec(memory_space=pltpu.SMEM)


def kernel_call(body, name, outs, args, scratch=(), weight=0):
    return pl.pallas_call(
        body,
        out_shape=outs,
        in_specs=[SMEM if a.dtype == jnp.int32 else VMEM for a in args],
        out_specs=tuple(VMEM for _ in outs),
        scratch_shapes=list(scratch),
        compiler_params=pltpu.CompilerParams(vmem_limit_bytes=VMEM_BYTES),
        cost_estimate=pl.CostEstimate(flops=int(weight), bytes_accessed=0, transcendentals=0),
        name=name,
    )(*args)


def per_device(features, weights, cotangent):
    blocks, depth, plane = features.shape
    channels = weights.shape[2]
    nz = lax.axis_size("sp")
    nc = lax.axis_size("ch")
    cols = channels // nz
    w2 = weights.reshape(27 * blocks, channels)
    feat = features.reshape(blocks, plane)
    cot = cotangent.reshape(blocks, plane)
    pos = jnp.stack([lax.axis_index("sp"), lax.axis_index("ch")]).astype(jnp.int32)

    even_pairs = [(i, i ^ 1) for i in range(nz)]
    odd_pairs = [(i, (((i + 1) ^ 1) - 1) % nz) for i in range(nz)]

    def mixed(k):
        return [(i, i ^ k) for i in range(nc)]

    def of(rows, dtype):
        return jax.ShapeDtypeStruct((rows, plane), dtype)

    small = jax.ShapeDtypeStruct((8, 128), F32)
    work = 2 * 27 * blocks * channels * plane

    cot_even = lax.ppermute(cot, "sp", even_pairs)
    cot_odd = lax.ppermute(cot, "sp", odd_pairs)
    (begin,) = kernel_call(token_kernel, "begin", [small], [], weight=W_BEGIN * work)
    feat, cot_even = lax.optimization_barrier((feat, cot_even))
    pieces = [feat] + [lax.ppermute(feat, "ch", mixed(k)) for k in range(1, nc)]

    *parts, token = kernel_call(
        functools.partial(input_grad_kernel, nz, nc),
        "input_grad",
        [of(blocks, F32)] * nc + [small],
        [pos, begin, cot, cot_even, cot_odd, w2],
        [pltpu.VMEM((27 * blocks, plane), BF16), pltpu.VMEM((channels, plane), F32)],
        W_GRAD * work,
    )
    terms = [parts[0]]
    for k in range(2, nc, 2):
        got = lax.ppermute(parts[k + 1], "ch", mixed(1))
        (both,) = kernel_call(fold_kernel, "fold", [of(blocks, F32)], [parts[k], got], weight=W_FOLD * work)
        terms.append(lax.ppermute(both, "ch", mixed(k)))
    terms.append(lax.ppermute(parts[1], "ch", mixed(1)))

    far_rows = cols if nz == 4 else cols + blocks
    f_all, to_even, to_odd, *packs = kernel_call(
        functools.partial(gather_kernel, nz, nc),
        "gather",
        [of(channels, BF16), of(cols + blocks, BF16), of(cols, BF16)]
        + [of(far_rows, BF16)] * (nz - 3),
        [pos, token, cot, cot_odd] + pieces,
        weight=W_GATHER * work,
    )
    g_odd = lax.ppermute(to_odd, "sp", odd_pairs)
    far = [
        lax.ppermute(packs[k - 2], "sp", [(i, (i + k) % nz) for i in range(nz)])
        for k in range(2, nz - 1)
    ]
    g_even = lax.ppermute(to_even, "sp", even_pairs)
    out_own, out_even, out_odd, moved = kernel_call(
        early_kernel,
        "early",
        [of(blocks, F32)] * 3 + [jax.ShapeDtypeStruct((3, 3 * blocks, plane), BF16)],
        [pos, w2, f_all, cot, cot_even, cot_odd],
        weight=W_EARLY * work,
    )
    out_odd = lax.ppermute(out_odd, "sp", odd_pairs)
    out_even = lax.ppermute(out_even, "sp", even_pairs)

    weight_grad, last = kernel_call(
        functools.partial(weight_grad_kernel, nz, 1.0 / math.sqrt(nz * depth * plane)),
        "weight_grad",
        [jax.ShapeDtypeStruct((27, blocks, cols), F32), small],
        [pos, moved, f_all, g_even, g_odd, *far],
        [pltpu.VMEM((nz + 2, 3 * blocks, plane), BF16), pltpu.VMEM((nz, cols, plane), BF16)],
        W_OUT * work,
    )
    block = jax.ShapeDtypeStruct((blocks, 1, plane), F32)
    back, done = kernel_call(
        input_total_kernel, "input_total", [block, small], [last] + terms, weight=W_TOTAL * work
    )
    (output,) = kernel_call(
        functools.partial(output_total_kernel, nz),
        "output_total",
        [block],
        [pos, done, out_own, out_odd, out_even],
    )
    return (output, back, weight_grad)


def solution(mesh):
    return jax.shard_map(
        per_device,
        mesh=mesh,
        in_specs=(P("ch", ("grp", "sp"), None), P(None, "ch", None), P("ch", ("grp", "sp"), None)),
        out_specs=(
            P("ch", ("grp", "sp"), None),
            P("ch", ("grp", "sp"), None),
            P("grp", "ch", "sp"),
        ),
        check_vma=False,
    )
```

```python
import functools
import math

import jax
import jax.numpy as jnp
from jax import lax
from jax.experimental import pallas as pl
from jax.experimental.pallas import tpu as pltpu
from jax.sharding import PartitionSpec as P

NX = 64
NY = 10
CELLS = NX * NY
F32 = jnp.float32
BF16 = jnp.bfloat16
W_GATHER, W_EARLY, W_BEGIN, W_GRAD, W_FOLD, W_TOTAL, W_OUT = 2, 0, 8, 1, 0, 1, 0
VMEM_BYTES = 32 * 1024 * 1024


def cell_mask(dy, dx):
    q = lax.broadcasted_iota(jnp.int32, (1, CELLS), 1)
    x = lax.rem(q, NX) + dx
    at = q + NX * dy
    return ((x >= 0) & (x < NX) & (at >= 0) & (at < CELLS)).astype(F32)


def shifted(value, dy, dx):
    if dy == 0 and dx == 0:
        return value
    return pltpu.roll(value, (-(dy * NX + dx)) % CELLS, 1) * cell_mask(dy, dx)


def odd_partner(s, nz):
    return lax.rem(((s + 1) ^ 1) + nz - 1, nz)


def gather_kernel(nz, nc, token_ref, cot_ref, near_ref, *refs):
    pieces, (f_ref, even_ref, odd_ref), packs = refs[:nc], refs[nc : nc + 3], refs[nc + 3 :]
    blocks = cot_ref.shape[0]
    cols = f_ref.shape[0] // nz
    s, c = lax.axis_index("sp"), lax.axis_index("ch")

    def block_for(goal):
        return f_ref[pl.ds(pl.multiple_of(goal * cols, cols), cols), :]

    for k in range(nc):
        f_ref[pl.ds(pl.multiple_of((c ^ k) * blocks, blocks), blocks), :] = pieces[k][...]
    even_ref[:cols, :] = block_for(s ^ 1)
    even_ref[cols:, :] = near_ref[...]
    odd_ref[...] = block_for(odd_partner(s, nz))
    for k, pack in zip(range(2, nz - 1), packs):
        pack[:cols, :] = block_for(lax.rem(s + k, nz))
        if nz > 4:
            pack[cols:, :] = cot_ref[...]


def columns(cols_ref, first, plane):
    blocks = plane.shape[0]
    for dy in (-1, 0, 1):
        for dx in (-1, 0, 1):
            tap = first + 3 * (dy + 1) + dx + 1
            cols_ref[tap * blocks : (tap + 1) * blocks, :] = shifted(plane, -dy, -dx).astype(BF16)


def token_kernel(token_ref):
    token_ref[...] = jnp.zeros(token_ref.shape, F32)


def input_grad_kernel(nz, nc, begin_ref, cot_ref, even_ref, odd_ref, w_ref, *refs):
    parts = refs[:nc]
    token_ref, cols_ref, sum_ref = refs[nc:]
    blocks = even_ref.shape[0]
    s, c = lax.axis_index("sp"), lax.axis_index("ch")
    token_ref[...] = jnp.zeros(token_ref.shape, F32)
    even, odd = even_ref[...].astype(F32), odd_ref[...].astype(F32)
    first = s % 2 == 0
    columns(cols_ref, 0, jnp.where(s < nz - 1, jnp.where(first, even, odd), 0.0))
    columns(cols_ref, 9, cot_ref[...].astype(F32))
    columns(cols_ref, 18, jnp.where(s > 0, jnp.where(first, odd, even), 0.0))
    sum_ref[...] = lax.dot_general(
        w_ref[...], cols_ref[...], (((0,), (0,)), ((), ())), preferred_element_type=F32
    )
    for k in range(nc):
        parts[k][...] = sum_ref[pl.ds(pl.multiple_of((c ^ k) * blocks, blocks), blocks), :]


def conv_part(w_ref, field, dz):
    taps = w_ref.shape[0] // 3
    rows = pl.ds(pl.multiple_of((dz + 1) * taps, taps), taps)
    return jnp.dot(w_ref[rows, :], field, preferred_element_type=F32)


def moved_sum(acc):
    blocks = acc.shape[0] // 9
    total = None
    for dx in (-1, 0, 1):
        for dy in (-1, 0, 1):
            at = (3 * (dy + 1) + dx + 1) * blocks
            term = shifted(acc[at : at + blocks], dy, dx)
            total = term if total is None else total + term
    return total


def moved_rows(plane):
    plane = plane.astype(F32)
    return jnp.concatenate([shifted(plane, -dy, 0).astype(BF16) for dy in (-1, 0, 1)], 0)


def early_kernel(w_ref, f_ref, cot_ref, ce_ref, co_ref, own_ref, even_ref, odd_ref, moved_ref):
    side = 1 - 2 * lax.rem(lax.axis_index("sp"), 2)
    for ref, dz in ((odd_ref, side), (even_ref, -side), (own_ref, 0)):
        ref[...] = moved_sum(conv_part(w_ref, f_ref[...], dz))
    for i, ref in enumerate((cot_ref, ce_ref, co_ref)):
        moved_ref[i] = moved_rows(ref[...])


def weight_grad_kernel(nz, scale, moved_ref, f_ref, ge_ref, go_ref, *refs):
    packs = refs[:-4]
    wg_ref, token_ref, c_ref, g_ref = refs[-4:]
    token_ref[...] = jnp.zeros(token_ref.shape, F32)
    blocks = c_ref.shape[1] // 3
    cols = go_ref.shape[0]
    s = lax.axis_index("sp")

    empty = jnp.zeros(c_ref.shape[1:], BF16)
    c_ref[0] = empty
    c_ref[nz + 1] = empty
    mine = pl.ds(pl.multiple_of(s * cols, cols), cols)
    sources = (s, s ^ 1, odd_partner(s, nz))
    for i, (source, field) in enumerate(zip(sources, (f_ref[mine, :], ge_ref[:cols, :], go_ref[...]))):
        c_ref[source + 1] = moved_ref[i]
        g_ref[source] = field
    for k, pack in zip(range(2, nz - 1), packs):
        source = lax.rem(s + nz - k, nz)
        g_ref[source] = pack[:cols, :]
        c_ref[source + 1] = moved_rows(pack[cols:, :] if nz > 4 else ge_ref[cols:, :])

    sums = None
    for z in range(nz):
        field = g_ref[z].astype(F32)
        fields = jnp.concatenate([shifted(field, 0, dx).astype(BF16) for dx in (-1, 0, 1)], 0)
        term = lax.dot_general(
            c_ref[z : z + 3].reshape(9 * blocks, CELLS),
            fields,
            (((1,), (1,)), ((), ())),
            preferred_element_type=F32,
        )
        sums = term if sums is None else sums + term
    sums = sums * scale
    for tap in range(27):
        dz, dy, dx = tap // 9, tap // 3 % 3, tap % 3
        at = ((2 - dz) * 3 + dy) * blocks
        wg_ref[tap] = sums[at : at + blocks, dx * cols : (dx + 1) * cols]


def fold_kernel(own_ref, got_ref, both_ref):
    both_ref[...] = own_ref[...] + got_ref[...]


def input_total_kernel(token_ref, *refs):
    terms, back_ref, done_ref = refs[:-2], refs[-2], refs[-1]
    done_ref[...] = jnp.zeros(done_ref.shape, F32)
    total = terms[0][...]
    for term in terms[1:]:
        total = total + term[...]
    back_ref[:, 0, :] = total


def output_total_kernel(nz, token_ref, own_ref, odd_ref, even_ref, out_ref):
    s = lax.axis_index("sp")
    inner = ((s > 0) & (s < nz - 1)).astype(F32)
    out_ref[:, 0, :] = own_ref[...] + even_ref[...] + inner * odd_ref[...]


VMEM = pl.BlockSpec(memory_space=pltpu.VMEM)
SMEM = pl.BlockSpec(memory_space=pltpu.SMEM)


def kernel_call(body, name, outs, args, scratch=(), weight=0):
    return pl.pallas_call(
        body,
        out_shape=outs,
        in_specs=[SMEM if a.dtype == jnp.int32 else VMEM for a in args],
        out_specs=tuple(VMEM for _ in outs),
        scratch_shapes=list(scratch),
        compiler_params=pltpu.CompilerParams(vmem_limit_bytes=VMEM_BYTES),
        cost_estimate=pl.CostEstimate(flops=int(weight), bytes_accessed=0, transcendentals=0),
        name=name,
    )(*args)


def per_device(features, weights, cotangent):
    blocks, depth, plane = features.shape
    channels = weights.shape[2]
    nz = lax.axis_size("sp")
    nc = lax.axis_size("ch")
    cols = channels // nz
    w2 = weights.reshape(27 * blocks, channels)
    feat = features.reshape(blocks, plane)
    cot = cotangent.reshape(blocks, plane)

    even_pairs = [(i, i ^ 1) for i in range(nz)]
    odd_pairs = [(i, (((i + 1) ^ 1) - 1) % nz) for i in range(nz)]

    def mixed(k):
        return [(i, i ^ k) for i in range(nc)]

    def of(rows, dtype):
        return jax.ShapeDtypeStruct((rows, plane), dtype)

    small = jax.ShapeDtypeStruct((8, 128), F32)
    work = 2 * 27 * blocks * channels * plane

    cot_even = lax.ppermute(cot, "sp", even_pairs)
    cot_odd = lax.ppermute(cot, "sp", odd_pairs)
    (begin,) = kernel_call(token_kernel, "begin", [small], [], weight=W_BEGIN * work)
    feat, cot_even = lax.optimization_barrier((feat, cot_even))
    pieces = [feat] + [lax.ppermute(feat, "ch", mixed(k)) for k in range(1, nc)]

    *parts, token = kernel_call(
        functools.partial(input_grad_kernel, nz, nc),
        "input_grad",
        [of(blocks, F32)] * nc + [small],
        [begin, cot, cot_even, cot_odd, w2],
        [pltpu.VMEM((27 * blocks, plane), BF16), pltpu.VMEM((channels, plane), F32)],
        W_GRAD * work,
    )
    terms = [parts[0]]
    for k in range(2, nc, 2):
        got = lax.ppermute(parts[k + 1], "ch", mixed(1))
        (both,) = kernel_call(fold_kernel, "fold", [of(blocks, F32)], [parts[k], got], weight=W_FOLD * work)
        terms.append(lax.ppermute(both, "ch", mixed(k)))
    terms.append(lax.ppermute(parts[1], "ch", mixed(1)))

    far_rows = cols if nz == 4 else cols + blocks
    f_all, to_even, to_odd, *packs = kernel_call(
        functools.partial(gather_kernel, nz, nc),
        "gather",
        [of(channels, BF16), of(cols + blocks, BF16), of(cols, BF16)]
        + [of(far_rows, BF16)] * (nz - 3),
        [token, cot, cot_odd] + pieces,
        weight=W_GATHER * work,
    )
    g_odd = lax.ppermute(to_odd, "sp", odd_pairs)
    far = [
        lax.ppermute(packs[k - 2], "sp", [(i, (i + k) % nz) for i in range(nz)])
        for k in range(2, nz - 1)
    ]
    g_even = lax.ppermute(to_even, "sp", even_pairs)
    out_own, out_even, out_odd, moved = kernel_call(
        early_kernel,
        "early",
        [of(blocks, F32)] * 3 + [jax.ShapeDtypeStruct((3, 3 * blocks, plane), BF16)],
        [w2, f_all, cot, cot_even, cot_odd],
        weight=W_EARLY * work,
    )
    out_odd = lax.ppermute(out_odd, "sp", odd_pairs)
    out_even = lax.ppermute(out_even, "sp", even_pairs)

    weight_grad, last = kernel_call(
        functools.partial(weight_grad_kernel, nz, 1.0 / math.sqrt(nz * depth * plane)),
        "weight_grad",
        [jax.ShapeDtypeStruct((27, blocks, cols), F32), small],
        [moved, f_all, g_even, g_odd, *far],
        [pltpu.VMEM((nz + 2, 3 * blocks, plane), BF16), pltpu.VMEM((nz, cols, plane), BF16)],
        W_OUT * work,
    )
    block = jax.ShapeDtypeStruct((blocks, 1, plane), F32)
    back, done = kernel_call(
        input_total_kernel, "input_total", [block, small], [last] + terms, weight=W_TOTAL * work
    )
    (output,) = kernel_call(
        functools.partial(output_total_kernel, nz),
        "output_total",
        [block],
        [done, out_own, out_odd, out_even],
    )
    return (output, back, weight_grad)


def solution(mesh):
    return jax.shard_map(
        per_device,
        mesh=mesh,
        in_specs=(P("ch", ("grp", "sp"), None), P(None, "ch", None), P("ch", ("grp", "sp"), None)),
        out_specs=(
            P("ch", ("grp", "sp"), None),
            P("ch", ("grp", "sp"), None),
            P("grp", "ch", "sp"),
        ),
        check_vma=False,
    )
```

```python
import functools
import math

import jax
import jax.numpy as jnp
from jax import lax
from jax.experimental import pallas as pl
from jax.experimental.pallas import tpu as pltpu
from jax.sharding import PartitionSpec as P

NX = 64
NY = 10
CELLS = NX * NY
F32 = jnp.float32
BF16 = jnp.bfloat16
W_GATHER, W_EARLY, W_BEGIN, W_GRAD, W_FOLD, W_TOTAL, W_OUT = 2, 0, 8, 1, 0, 2, 0
VMEM_BYTES = 32 * 1024 * 1024


def cell_mask(dy, dx):
    q = lax.broadcasted_iota(jnp.int32, (1, CELLS), 1)
    x = lax.rem(q, NX) + dx
    at = q + NX * dy
    return ((x >= 0) & (x < NX) & (at >= 0) & (at < CELLS)).astype(F32)


def shifted(value, dy, dx):
    if dy == 0 and dx == 0:
        return value
    return pltpu.roll(value, (-(dy * NX + dx)) % CELLS, 1) * cell_mask(dy, dx)


def odd_partner(s, nz):
    return lax.rem(((s + 1) ^ 1) + nz - 1, nz)


def gather_kernel(nz, nc, token_ref, cot_ref, near_ref, *refs):
    pieces, (f_ref, even_ref, odd_ref), packs = refs[:nc], refs[nc : nc + 3], refs[nc + 3 :]
    blocks = cot_ref.shape[0]
    cols = f_ref.shape[0] // nz
    s, c = lax.axis_index("sp"), lax.axis_index("ch")

    def block_for(goal):
        return f_ref[pl.ds(pl.multiple_of(goal * cols, cols), cols), :]

    for k in range(nc):
        f_ref[pl.ds(pl.multiple_of((c ^ k) * blocks, blocks), blocks), :] = pieces[k][...]
    even_ref[:cols, :] = block_for(s ^ 1)
    even_ref[cols:, :] = near_ref[...]
    odd_ref[...] = block_for(odd_partner(s, nz))
    for k, pack in zip(range(2, nz - 1), packs):
        pack[:cols, :] = block_for(lax.rem(s + k, nz))
        if nz > 4:
            pack[cols:, :] = cot_ref[...]


def columns(cols_ref, first, plane):
    blocks = plane.shape[0]
    for dy in (-1, 0, 1):
        for dx in (-1, 0, 1):
            tap = first + 3 * (dy + 1) + dx + 1
            cols_ref[tap * blocks : (tap + 1) * blocks, :] = shifted(plane, -dy, -dx).astype(BF16)


def token_kernel(token_ref):
    token_ref[...] = jnp.zeros(token_ref.shape, F32)


def input_grad_kernel(nz, nc, begin_ref, cot_ref, even_ref, odd_ref, w_ref, *refs):
    parts = refs[:nc]
    token_ref, cols_ref, sum_ref = refs[nc:]
    blocks = even_ref.shape[0]
    s, c = lax.axis_index("sp"), lax.axis_index("ch")
    token_ref[...] = jnp.zeros(token_ref.shape, F32)
    even, odd = even_ref[...].astype(F32), odd_ref[...].astype(F32)
    first = s % 2 == 0
    columns(cols_ref, 0, jnp.where(s < nz - 1, jnp.where(first, even, odd), 0.0))
    columns(cols_ref, 9, cot_ref[...].astype(F32))
    columns(cols_ref, 18, jnp.where(s > 0, jnp.where(first, odd, even), 0.0))
    sum_ref[...] = lax.dot_general(
        w_ref[...], cols_ref[...], (((0,), (0,)), ((), ())), preferred_element_type=F32
    )
    for k in range(nc):
        parts[k][...] = sum_ref[pl.ds(pl.multiple_of((c ^ k) * blocks, blocks), blocks), :]


def conv_part(w_ref, field, dz):
    taps = w_ref.shape[0] // 3
    rows = pl.ds(pl.multiple_of((dz + 1) * taps, taps), taps)
    return jnp.dot(w_ref[rows, :], field, preferred_element_type=F32)


def moved_sum(acc):
    blocks = acc.shape[0] // 9
    total = None
    for dx in (-1, 0, 1):
        for dy in (-1, 0, 1):
            at = (3 * (dy + 1) + dx + 1) * blocks
            term = shifted(acc[at : at + blocks], dy, dx)
            total = term if total is None else total + term
    return total


def moved_rows(plane):
    plane = plane.astype(F32)
    return jnp.concatenate([shifted(plane, -dy, 0).astype(BF16) for dy in (-1, 0, 1)], 0)


def early_kernel(w_ref, f_ref, cot_ref, ce_ref, co_ref, own_ref, even_ref, odd_ref, moved_ref):
    side = 1 - 2 * lax.rem(lax.axis_index("sp"), 2)
    for ref, dz in ((odd_ref, side), (even_ref, -side), (own_ref, 0)):
        ref[...] = moved_sum(conv_part(w_ref, f_ref[...], dz))
    for i, ref in enumerate((cot_ref, ce_ref, co_ref)):
        moved_ref[i] = moved_rows(ref[...])


def weight_grad_kernel(nz, scale, moved_ref, f_ref, ge_ref, go_ref, *refs):
    packs = refs[:-4]
    wg_ref, token_ref, c_ref, g_ref = refs[-4:]
    token_ref[...] = jnp.zeros(token_ref.shape, F32)
    blocks = c_ref.shape[1] // 3
    cols = go_ref.shape[0]
    s = lax.axis_index("sp")

    empty = jnp.zeros(c_ref.shape[1:], BF16)
    c_ref[0] = empty
    c_ref[nz + 1] = empty
    mine = pl.ds(pl.multiple_of(s * cols, cols), cols)
    sources = (s, s ^ 1, odd_partner(s, nz))
    for i, (source, field) in enumerate(zip(sources, (f_ref[mine, :], ge_ref[:cols, :], go_ref[...]))):
        c_ref[source + 1] = moved_ref[i]
        g_ref[source] = field
    for k, pack in zip(range(2, nz - 1), packs):
        source = lax.rem(s + nz - k, nz)
        g_ref[source] = pack[:cols, :]
        c_ref[source + 1] = moved_rows(pack[cols:, :] if nz > 4 else ge_ref[cols:, :])

    sums = None
    for z in range(nz):
        field = g_ref[z].astype(F32)
        fields = jnp.concatenate([shifted(field, 0, dx).astype(BF16) for dx in (-1, 0, 1)], 0)
        term = lax.dot_general(
            c_ref[z : z + 3].reshape(9 * blocks, CELLS),
            fields,
            (((1,), (1,)), ((), ())),
            preferred_element_type=F32,
        )
        sums = term if sums is None else sums + term
    sums = sums * scale
    for tap in range(27):
        dz, dy, dx = tap // 9, tap // 3 % 3, tap % 3
        at = ((2 - dz) * 3 + dy) * blocks
        wg_ref[tap] = sums[at : at + blocks, dx * cols : (dx + 1) * cols]


def fold_kernel(own_ref, got_ref, both_ref):
    both_ref[...] = own_ref[...] + got_ref[...]


def input_total_kernel(token_ref, *refs):
    terms, back_ref, done_ref = refs[:-2], refs[-2], refs[-1]
    done_ref[...] = jnp.zeros(done_ref.shape, F32)
    total = terms[0][...]
    for term in terms[1:]:
        total = total + term[...]
    back_ref[:, 0, :] = total


def output_total_kernel(nz, token_ref, own_ref, odd_ref, even_ref, out_ref):
    s = lax.axis_index("sp")
    inner = ((s > 0) & (s < nz - 1)).astype(F32)
    out_ref[:, 0, :] = own_ref[...] + even_ref[...] + inner * odd_ref[...]


VMEM = pl.BlockSpec(memory_space=pltpu.VMEM)
SMEM = pl.BlockSpec(memory_space=pltpu.SMEM)


def kernel_call(body, name, outs, args, scratch=(), weight=0):
    return pl.pallas_call(
        body,
        out_shape=outs,
        in_specs=[SMEM if a.dtype == jnp.int32 else VMEM for a in args],
        out_specs=tuple(VMEM for _ in outs),
        scratch_shapes=list(scratch),
        compiler_params=pltpu.CompilerParams(vmem_limit_bytes=VMEM_BYTES),
        cost_estimate=pl.CostEstimate(flops=int(weight), bytes_accessed=0, transcendentals=0),
        name=name,
    )(*args)


def per_device(features, weights, cotangent):
    blocks, depth, plane = features.shape
    channels = weights.shape[2]
    nz = lax.axis_size("sp")
    nc = lax.axis_size("ch")
    cols = channels // nz
    w2 = weights.reshape(27 * blocks, channels)
    feat = features.reshape(blocks, plane)
    cot = cotangent.reshape(blocks, plane)

    even_pairs = [(i, i ^ 1) for i in range(nz)]
    odd_pairs = [(i, (((i + 1) ^ 1) - 1) % nz) for i in range(nz)]

    def mixed(k):
        return [(i, i ^ k) for i in range(nc)]

    def of(rows, dtype):
        return jax.ShapeDtypeStruct((rows, plane), dtype)

    small = jax.ShapeDtypeStruct((8, 128), F32)
    work = 2 * 27 * blocks * channels * plane

    cot_even = lax.ppermute(cot, "sp", even_pairs)
    cot_odd = lax.ppermute(cot, "sp", odd_pairs)
    (begin,) = kernel_call(token_kernel, "begin", [small], [], weight=W_BEGIN * work)
    feat, cot_even = lax.optimization_barrier((feat, cot_even))
    pieces = [feat] + [lax.ppermute(feat, "ch", mixed(k)) for k in range(1, nc)]

    *parts, token = kernel_call(
        functools.partial(input_grad_kernel, nz, nc),
        "input_grad",
        [of(blocks, F32)] * nc + [small],
        [begin, cot, cot_even, cot_odd, w2],
        [pltpu.VMEM((27 * blocks, plane), BF16), pltpu.VMEM((channels, plane), F32)],
        W_GRAD * work,
    )
    terms = [parts[0]]
    for k in range(2, nc, 2):
        got = lax.ppermute(parts[k + 1], "ch", mixed(1))
        (both,) = kernel_call(fold_kernel, "fold", [of(blocks, F32)], [parts[k], got], weight=W_FOLD * work)
        terms.append(lax.ppermute(both, "ch", mixed(k)))
    terms.append(lax.ppermute(parts[1], "ch", mixed(1)))

    far_rows = cols if nz == 4 else cols + blocks
    f_all, to_even, to_odd, *packs = kernel_call(
        functools.partial(gather_kernel, nz, nc),
        "gather",
        [of(channels, BF16), of(cols + blocks, BF16), of(cols, BF16)]
        + [of(far_rows, BF16)] * (nz - 3),
        [token, cot, cot_odd] + pieces,
        weight=W_GATHER * work,
    )
    g_odd = lax.ppermute(to_odd, "sp", odd_pairs)
    far = [
        lax.ppermute(packs[k - 2], "sp", [(i, (i + k) % nz) for i in range(nz)])
        for k in range(2, nz - 1)
    ]
    g_even = lax.ppermute(to_even, "sp", even_pairs)
    out_own, out_even, out_odd, moved = kernel_call(
        early_kernel,
        "early",
        [of(blocks, F32)] * 3 + [jax.ShapeDtypeStruct((3, 3 * blocks, plane), BF16)],
        [w2, f_all, cot, cot_even, cot_odd],
        weight=W_EARLY * work,
    )
    out_odd = lax.ppermute(out_odd, "sp", odd_pairs)
    out_even = lax.ppermute(out_even, "sp", even_pairs)

    weight_grad, last = kernel_call(
        functools.partial(weight_grad_kernel, nz, 1.0 / math.sqrt(nz * depth * plane)),
        "weight_grad",
        [jax.ShapeDtypeStruct((27, blocks, cols), F32), small],
        [moved, f_all, g_even, g_odd, *far],
        [pltpu.VMEM((nz + 2, 3 * blocks, plane), BF16), pltpu.VMEM((nz, cols, plane), BF16)],
        W_OUT * work,
    )
    block = jax.ShapeDtypeStruct((blocks, 1, plane), F32)
    back, done = kernel_call(
        input_total_kernel, "input_total", [block, small], [last] + terms, weight=W_TOTAL * work
    )
    (output,) = kernel_call(
        functools.partial(output_total_kernel, nz),
        "output_total",
        [block],
        [done, out_own, out_odd, out_even],
    )
    return (output, back, weight_grad)


def solution(mesh):
    return jax.shard_map(
        per_device,
        mesh=mesh,
        in_specs=(P("ch", ("grp", "sp"), None), P(None, "ch", None), P("ch", ("grp", "sp"), None)),
        out_specs=(
            P("ch", ("grp", "sp"), None),
            P("ch", ("grp", "sp"), None),
            P("grp", "ch", "sp"),
        ),
        check_vma=False,
    )
```

```python
import functools
import math

import jax
import jax.numpy as jnp
from jax import lax
from jax.experimental import pallas as pl
from jax.experimental.pallas import tpu as pltpu
from jax.sharding import PartitionSpec as P

NX = 64
NY = 10
CELLS = NX * NY
F32 = jnp.float32
BF16 = jnp.bfloat16
W_GATHER, W_EARLY, W_BEGIN, W_GRAD, W_FOLD, W_TOTAL, W_OUT = 2, 0, 8, 1, 0, 1, 0
VMEM_BYTES = 32 * 1024 * 1024


def cell_mask(dy, dx):
    q = lax.broadcasted_iota(jnp.int32, (1, CELLS), 1)
    x = lax.rem(q, NX) + dx
    at = q + NX * dy
    return ((x >= 0) & (x < NX) & (at >= 0) & (at < CELLS)).astype(F32)


def shifted(value, dy, dx):
    if dy == 0 and dx == 0:
        return value
    return pltpu.roll(value, (-(dy * NX + dx)) % CELLS, 1) * cell_mask(dy, dx)


def odd_partner(s, nz):
    return lax.rem(((s + 1) ^ 1) + nz - 1, nz)


def gather_kernel(nz, nc, token_ref, cot_ref, near_ref, *refs):
    pieces, (f_ref, even_ref, odd_ref), packs = refs[:nc], refs[nc : nc + 3], refs[nc + 3 :]
    blocks = cot_ref.shape[0]
    cols = f_ref.shape[0] // nz
    s, c = lax.axis_index("sp"), lax.axis_index("ch")

    def block_for(goal):
        return f_ref[pl.ds(pl.multiple_of(goal * cols, cols), cols), :]

    for k in range(nc):
        f_ref[pl.ds(pl.multiple_of((c ^ k) * blocks, blocks), blocks), :] = pieces[k][...]
    even_ref[:cols, :] = block_for(s ^ 1)
    even_ref[cols:, :] = near_ref[...]
    odd_ref[...] = block_for(odd_partner(s, nz))
    for k, pack in zip(range(2, nz - 1), packs):
        pack[:cols, :] = block_for(lax.rem(s + k, nz))
        if nz > 4:
            pack[cols:, :] = cot_ref[...]


def columns(cols_ref, first, plane):
    blocks = plane.shape[0]
    for dy in (-1, 0, 1):
        for dx in (-1, 0, 1):
            tap = first + 3 * (dy + 1) + dx + 1
            cols_ref[tap * blocks : (tap + 1) * blocks, :] = shifted(plane, -dy, -dx).astype(BF16)


def token_kernel(token_ref):
    token_ref[...] = jnp.zeros(token_ref.shape, F32)


def input_grad_kernel(nz, nc, begin_ref, cot_ref, even_ref, odd_ref, w_ref, *refs):
    parts = refs[:nc]
    token_ref, cols_ref, sum_ref = refs[nc:]
    blocks = even_ref.shape[0]
    s, c = lax.axis_index("sp"), lax.axis_index("ch")
    token_ref[...] = jnp.zeros(token_ref.shape, F32)
    even, odd = even_ref[...].astype(F32), odd_ref[...].astype(F32)
    first = s % 2 == 0
    columns(cols_ref, 0, jnp.where(s < nz - 1, jnp.where(first, even, odd), 0.0))
    columns(cols_ref, 9, cot_ref[...].astype(F32))
    columns(cols_ref, 18, jnp.where(s > 0, jnp.where(first, odd, even), 0.0))
    sum_ref[...] = lax.dot_general(
        w_ref[...], cols_ref[...], (((0,), (0,)), ((), ())), preferred_element_type=F32
    )
    for k in range(nc):
        parts[k][...] = sum_ref[pl.ds(pl.multiple_of((c ^ k) * blocks, blocks), blocks), :]


def conv_part(w_ref, field, dz):
    taps = w_ref.shape[0] // 3
    rows = pl.ds(pl.multiple_of((dz + 1) * taps, taps), taps)
    return jnp.dot(w_ref[rows, :], field, preferred_element_type=F32)


def moved_sum(acc):
    blocks = acc.shape[0] // 9
    total = None
    for dx in (-1, 0, 1):
        for dy in (-1, 0, 1):
            at = (3 * (dy + 1) + dx + 1) * blocks
            term = shifted(acc[at : at + blocks], dy, dx)
            total = term if total is None else total + term
    return total


def moved_rows(plane):
    plane = plane.astype(F32)
    return jnp.concatenate([shifted(plane, -dy, 0).astype(BF16) for dy in (-1, 0, 1)], 0)


def early_kernel(token_ref, w_ref, f_ref, cot_ref, ce_ref, co_ref, own_ref, even_ref, odd_ref, moved_ref):
    side = 1 - 2 * lax.rem(lax.axis_index("sp"), 2)
    for ref, dz in ((odd_ref, side), (even_ref, -side), (own_ref, 0)):
        ref[...] = moved_sum(conv_part(w_ref, f_ref[...], dz))
    for i, ref in enumerate((cot_ref, ce_ref, co_ref)):
        moved_ref[i] = moved_rows(ref[...])


def weight_grad_kernel(nz, scale, moved_ref, f_ref, ge_ref, go_ref, *refs):
    packs = refs[:-4]
    wg_ref, token_ref, c_ref, g_ref = refs[-4:]
    token_ref[...] = jnp.zeros(token_ref.shape, F32)
    blocks = c_ref.shape[1] // 3
    cols = go_ref.shape[0]
    s = lax.axis_index("sp")

    empty = jnp.zeros(c_ref.shape[1:], BF16)
    c_ref[0] = empty
    c_ref[nz + 1] = empty
    mine = pl.ds(pl.multiple_of(s * cols, cols), cols)
    sources = (s, s ^ 1, odd_partner(s, nz))
    for i, (source, field) in enumerate(zip(sources, (f_ref[mine, :], ge_ref[:cols, :], go_ref[...]))):
        c_ref[source + 1] = moved_ref[i]
        g_ref[source] = field
    for k, pack in zip(range(2, nz - 1), packs):
        source = lax.rem(s + nz - k, nz)
        g_ref[source] = pack[:cols, :]
        c_ref[source + 1] = moved_rows(pack[cols:, :] if nz > 4 else ge_ref[cols:, :])

    sums = None
    for z in range(nz):
        field = g_ref[z].astype(F32)
        fields = jnp.concatenate([shifted(field, 0, dx).astype(BF16) for dx in (-1, 0, 1)], 0)
        term = lax.dot_general(
            c_ref[z : z + 3].reshape(9 * blocks, CELLS),
            fields,
            (((1,), (1,)), ((), ())),
            preferred_element_type=F32,
        )
        sums = term if sums is None else sums + term
    sums = sums * scale
    for tap in range(27):
        dz, dy, dx = tap // 9, tap // 3 % 3, tap % 3
        at = ((2 - dz) * 3 + dy) * blocks
        wg_ref[tap] = sums[at : at + blocks, dx * cols : (dx + 1) * cols]


def fold_kernel(own_ref, got_ref, both_ref):
    both_ref[...] = own_ref[...] + got_ref[...]


def input_total_kernel(token_ref, *refs):
    terms, back_ref, done_ref = refs[:-2], refs[-2], refs[-1]
    done_ref[...] = jnp.zeros(done_ref.shape, F32)
    total = terms[0][...]
    for term in terms[1:]:
        total = total + term[...]
    back_ref[:, 0, :] = total


def output_total_kernel(nz, token_ref, own_ref, odd_ref, even_ref, out_ref):
    s = lax.axis_index("sp")
    inner = ((s > 0) & (s < nz - 1)).astype(F32)
    out_ref[:, 0, :] = own_ref[...] + even_ref[...] + inner * odd_ref[...]


VMEM = pl.BlockSpec(memory_space=pltpu.VMEM)
SMEM = pl.BlockSpec(memory_space=pltpu.SMEM)


def kernel_call(body, name, outs, args, scratch=(), weight=0):
    return pl.pallas_call(
        body,
        out_shape=outs,
        in_specs=[SMEM if a.dtype == jnp.int32 else VMEM for a in args],
        out_specs=tuple(VMEM for _ in outs),
        scratch_shapes=list(scratch),
        compiler_params=pltpu.CompilerParams(vmem_limit_bytes=VMEM_BYTES),
        cost_estimate=pl.CostEstimate(flops=int(weight), bytes_accessed=0, transcendentals=0),
        name=name,
    )(*args)


def per_device(features, weights, cotangent):
    blocks, depth, plane = features.shape
    channels = weights.shape[2]
    nz = lax.axis_size("sp")
    nc = lax.axis_size("ch")
    cols = channels // nz
    w2 = weights.reshape(27 * blocks, channels)
    feat = features.reshape(blocks, plane)
    cot = cotangent.reshape(blocks, plane)

    even_pairs = [(i, i ^ 1) for i in range(nz)]
    odd_pairs = [(i, (((i + 1) ^ 1) - 1) % nz) for i in range(nz)]

    def mixed(k):
        return [(i, i ^ k) for i in range(nc)]

    def of(rows, dtype):
        return jax.ShapeDtypeStruct((rows, plane), dtype)

    small = jax.ShapeDtypeStruct((8, 128), F32)
    work = 2 * 27 * blocks * channels * plane

    cot_even = lax.ppermute(cot, "sp", even_pairs)
    cot_odd = lax.ppermute(cot, "sp", odd_pairs)
    (begin,) = kernel_call(token_kernel, "begin", [small], [], weight=W_BEGIN * work)
    feat, cot_even = lax.optimization_barrier((feat, cot_even))
    pieces = [feat] + [lax.ppermute(feat, "ch", mixed(k)) for k in range(1, nc)]

    *parts, token = kernel_call(
        functools.partial(input_grad_kernel, nz, nc),
        "input_grad",
        [of(blocks, F32)] * nc + [small],
        [begin, cot, cot_even, cot_odd, w2],
        [pltpu.VMEM((27 * blocks, plane), BF16), pltpu.VMEM((channels, plane), F32)],
        W_GRAD * work,
    )
    terms = [parts[0]]
    for k in range(2, nc, 2):
        got = lax.ppermute(parts[k + 1], "ch", mixed(1))
        (both,) = kernel_call(fold_kernel, "fold", [of(blocks, F32)], [parts[k], got], weight=W_FOLD * work)
        terms.append(lax.ppermute(both, "ch", mixed(k)))

    far_rows = cols if nz == 4 else cols + blocks
    f_all, to_even, to_odd, *packs = kernel_call(
        functools.partial(gather_kernel, nz, nc),
        "gather",
        [of(channels, BF16), of(cols + blocks, BF16), of(cols, BF16)]
        + [of(far_rows, BF16)] * (nz - 3),
        [token, cot, cot_odd] + pieces,
        weight=W_GATHER * work,
    )
    g_odd = lax.ppermute(to_odd, "sp", odd_pairs)
    far = [
        lax.ppermute(packs[k - 2], "sp", [(i, (i + k) % nz) for i in range(nz)])
        for k in range(2, nz - 1)
    ]
    g_even = lax.ppermute(to_even, "sp", even_pairs)
    out_own, out_even, out_odd, moved = kernel_call(
        early_kernel,
        "early",
        [of(blocks, F32)] * 3 + [jax.ShapeDtypeStruct((3, 3 * blocks, plane), BF16)],
        [both, w2, f_all, cot, cot_even, cot_odd],
        weight=W_EARLY * work,
    )
    near, out_own = lax.optimization_barrier((parts[1], out_own))
    terms.append(lax.ppermute(near, "ch", mixed(1)))
    out_odd = lax.ppermute(out_odd, "sp", odd_pairs)
    out_even = lax.ppermute(out_even, "sp", even_pairs)

    weight_grad, last = kernel_call(
        functools.partial(weight_grad_kernel, nz, 1.0 / math.sqrt(nz * depth * plane)),
        "weight_grad",
        [jax.ShapeDtypeStruct((27, blocks, cols), F32), small],
        [moved, f_all, g_even, g_odd, *far],
        [pltpu.VMEM((nz + 2, 3 * blocks, plane), BF16), pltpu.VMEM((nz, cols, plane), BF16)],
        W_OUT * work,
    )
    block = jax.ShapeDtypeStruct((blocks, 1, plane), F32)
    back, done = kernel_call(
        input_total_kernel, "input_total", [block, small], [last] + terms, weight=W_TOTAL * work
    )
    (output,) = kernel_call(
        functools.partial(output_total_kernel, nz),
        "output_total",
        [block],
        [done, out_own, out_odd, out_even],
    )
    return (output, back, weight_grad)


def solution(mesh):
    return jax.shard_map(
        per_device,
        mesh=mesh,
        in_specs=(P("ch", ("grp", "sp"), None), P(None, "ch", None), P("ch", ("grp", "sp"), None)),
        out_specs=(
            P("ch", ("grp", "sp"), None),
            P("ch", ("grp", "sp"), None),
            P("grp", "ch", "sp"),
        ),
        check_vma=False,
    )
```

```python
import functools
import math

import jax
import jax.numpy as jnp
from jax import lax
from jax.experimental import pallas as pl
from jax.experimental.pallas import tpu as pltpu
from jax.sharding import PartitionSpec as P

NX = 64
NY = 10
CELLS = NX * NY
F32 = jnp.float32
BF16 = jnp.bfloat16
W_GATHER, W_EARLY, W_BEGIN, W_GRAD, W_FOLD, W_TOTAL, W_OUT = 2, 0, 8, 1, 0, 1, 0
VMEM_BYTES = 32 * 1024 * 1024


def cell_mask(dy, dx):
    q = lax.broadcasted_iota(jnp.int32, (1, CELLS), 1)
    x = lax.rem(q, NX) + dx
    at = q + NX * dy
    return ((x >= 0) & (x < NX) & (at >= 0) & (at < CELLS)).astype(F32)


def shifted(value, dy, dx):
    if dy == 0 and dx == 0:
        return value
    return pltpu.roll(value, (-(dy * NX + dx)) % CELLS, 1) * cell_mask(dy, dx)


def odd_partner(s, nz):
    return lax.rem(((s + 1) ^ 1) + nz - 1, nz)


def gather_kernel(nz, nc, token_ref, cot_ref, near_ref, *refs):
    pieces, (f_ref, even_ref, odd_ref), packs = refs[:nc], refs[nc : nc + 3], refs[nc + 3 :]
    blocks = cot_ref.shape[0]
    cols = f_ref.shape[0] // nz
    s, c = lax.axis_index("sp"), lax.axis_index("ch")

    def block_for(goal):
        return f_ref[pl.ds(pl.multiple_of(goal * cols, cols), cols), :]

    for k in range(nc):
        f_ref[pl.ds(pl.multiple_of((c ^ k) * blocks, blocks), blocks), :] = pieces[k][...]
    even_ref[:cols, :] = block_for(s ^ 1)
    even_ref[cols:, :] = near_ref[...]
    odd_ref[...] = block_for(odd_partner(s, nz))
    for k, pack in zip(range(2, nz - 1), packs):
        pack[:cols, :] = block_for(lax.rem(s + k, nz))
        if nz > 4:
            pack[cols:, :] = cot_ref[...]


def columns(cols_ref, first, plane):
    blocks = plane.shape[0]
    for dy in (-1, 0, 1):
        for dx in (-1, 0, 1):
            tap = first + 3 * (dy + 1) + dx + 1
            cols_ref[tap * blocks : (tap + 1) * blocks, :] = shifted(plane, -dy, -dx).astype(BF16)


def token_kernel(token_ref):
    token_ref[...] = jnp.zeros(token_ref.shape, F32)


def input_grad_kernel(nz, nc, begin_ref, cot_ref, even_ref, odd_ref, w_ref, *refs):
    parts = refs[:nc]
    token_ref, cols_ref, sum_ref = refs[nc:]
    blocks = even_ref.shape[0]
    s, c = lax.axis_index("sp"), lax.axis_index("ch")
    token_ref[...] = jnp.zeros(token_ref.shape, F32)
    even, odd = even_ref[...].astype(F32), odd_ref[...].astype(F32)
    first = s % 2 == 0
    columns(cols_ref, 0, jnp.where(s < nz - 1, jnp.where(first, even, odd), 0.0))
    columns(cols_ref, 9, cot_ref[...].astype(F32))
    columns(cols_ref, 18, jnp.where(s > 0, jnp.where(first, odd, even), 0.0))
    sum_ref[...] = lax.dot_general(
        w_ref[...], cols_ref[...], (((0,), (0,)), ((), ())), preferred_element_type=F32
    )
    for k in range(nc):
        parts[k][...] = sum_ref[pl.ds(pl.multiple_of((c ^ k) * blocks, blocks), blocks), :]


def conv_part(w_ref, field, dz):
    taps = w_ref.shape[0] // 3
    rows = pl.ds(pl.multiple_of((dz + 1) * taps, taps), taps)
    return jnp.dot(w_ref[rows, :], field, preferred_element_type=F32)


def moved_sum(acc):
    blocks = acc.shape[0] // 9
    total = None
    for dx in (-1, 0, 1):
        for dy in (-1, 0, 1):
            at = (3 * (dy + 1) + dx + 1) * blocks
            term = shifted(acc[at : at + blocks], dy, dx)
            total = term if total is None else total + term
    return total


def moved_rows(plane):
    plane = plane.astype(F32)
    return jnp.concatenate([shifted(plane, -dy, 0).astype(BF16) for dy in (-1, 0, 1)], 0)


def early_kernel(w_ref, f_ref, cot_ref, ce_ref, co_ref, own_ref, even_ref, odd_ref, moved_ref):
    side = 1 - 2 * lax.rem(lax.axis_index("sp"), 2)
    for ref, dz in ((odd_ref, side), (even_ref, -side), (own_ref, 0)):
        ref[...] = moved_sum(conv_part(w_ref, f_ref[...], dz))
    for i, ref in enumerate((cot_ref, ce_ref, co_ref)):
        moved_ref[i] = moved_rows(ref[...])


def weight_grad_kernel(nz, scale, moved_ref, f_ref, ge_ref, go_ref, *refs):
    packs = refs[:-4]
    wg_ref, token_ref, c_ref, g_ref = refs[-4:]
    token_ref[...] = jnp.zeros(token_ref.shape, F32)
    blocks = c_ref.shape[1] // 3
    cols = go_ref.shape[0]
    s = lax.axis_index("sp")

    empty = jnp.zeros(c_ref.shape[1:], BF16)
    c_ref[0] = empty
    c_ref[nz + 1] = empty
    mine = pl.ds(pl.multiple_of(s * cols, cols), cols)
    sources = (s, s ^ 1, odd_partner(s, nz))
    for i, (source, field) in enumerate(zip(sources, (f_ref[mine, :], ge_ref[:cols, :], go_ref[...]))):
        c_ref[source + 1] = moved_ref[i]
        g_ref[source] = field
    for k, pack in zip(range(2, nz - 1), packs):
        source = lax.rem(s + nz - k, nz)
        g_ref[source] = pack[:cols, :]
        c_ref[source + 1] = moved_rows(pack[cols:, :] if nz > 4 else ge_ref[cols:, :])

    sums = None
    for z in range(nz):
        field = g_ref[z].astype(F32)
        fields = jnp.concatenate([shifted(field, 0, dx).astype(BF16) for dx in (-1, 0, 1)], 0)
        term = lax.dot_general(
            c_ref[z : z + 3].reshape(9 * blocks, CELLS),
            fields,
            (((1,), (1,)), ((), ())),
            preferred_element_type=F32,
        )
        sums = term if sums is None else sums + term
    sums = sums * scale
    for tap in range(27):
        dz, dy, dx = tap // 9, tap // 3 % 3, tap % 3
        at = ((2 - dz) * 3 + dy) * blocks
        wg_ref[tap] = sums[at : at + blocks, dx * cols : (dx + 1) * cols]


def fold_kernel(own_ref, got_ref, both_ref):
    both_ref[...] = own_ref[...] + got_ref[...]


def input_total_kernel(token_ref, *refs):
    terms, back_ref, done_ref = refs[:-2], refs[-2], refs[-1]
    done_ref[...] = jnp.zeros(done_ref.shape, F32)
    total = terms[0][...]
    for term in terms[1:]:
        total = total + term[...]
    back_ref[:, 0, :] = total


def output_total_kernel(nz, token_ref, own_ref, odd_ref, even_ref, out_ref):
    s = lax.axis_index("sp")
    inner = ((s > 0) & (s < nz - 1)).astype(F32)
    out_ref[:, 0, :] = own_ref[...] + even_ref[...] + inner * odd_ref[...]


VMEM = pl.BlockSpec(memory_space=pltpu.VMEM)
SMEM = pl.BlockSpec(memory_space=pltpu.SMEM)


def kernel_call(body, name, outs, args, scratch=(), weight=0):
    return pl.pallas_call(
        body,
        out_shape=outs,
        in_specs=[SMEM if a.dtype == jnp.int32 else VMEM for a in args],
        out_specs=tuple(VMEM for _ in outs),
        scratch_shapes=list(scratch),
        compiler_params=pltpu.CompilerParams(vmem_limit_bytes=VMEM_BYTES),
        cost_estimate=pl.CostEstimate(flops=int(weight), bytes_accessed=0, transcendentals=0),
        name=name,
    )(*args)


def per_device(features, weights, cotangent):
    blocks, depth, plane = features.shape
    channels = weights.shape[2]
    nz = lax.axis_size("sp")
    nc = lax.axis_size("ch")
    cols = channels // nz
    w2 = weights.reshape(27 * blocks, channels)
    feat = features.reshape(blocks, plane)
    cot = cotangent.reshape(blocks, plane)

    even_pairs = [(i, i ^ 1) for i in range(nz)]
    odd_pairs = [(i, (((i + 1) ^ 1) - 1) % nz) for i in range(nz)]

    def mixed(k):
        return [(i, i ^ k) for i in range(nc)]

    def of(rows, dtype):
        return jax.ShapeDtypeStruct((rows, plane), dtype)

    small = jax.ShapeDtypeStruct((8, 128), F32)
    work = 2 * 27 * blocks * channels * plane

    cot_even = lax.ppermute(cot, "sp", even_pairs)
    cot_odd = lax.ppermute(cot, "sp", odd_pairs)
    (begin,) = kernel_call(token_kernel, "begin", [small], [], weight=W_BEGIN * work)
    feat, begin = lax.optimization_barrier((feat, begin))
    pieces = [feat] + [lax.ppermute(feat, "ch", mixed(k)) for k in range(1, nc)]

    *parts, token = kernel_call(
        functools.partial(input_grad_kernel, nz, nc),
        "input_grad",
        [of(blocks, F32)] * nc + [small],
        [begin, cot, cot_even, cot_odd, w2],
        [pltpu.VMEM((27 * blocks, plane), BF16), pltpu.VMEM((channels, plane), F32)],
        W_GRAD * work,
    )
    terms = [parts[0]]
    for k in range(2, nc, 2):
        got = lax.ppermute(parts[k + 1], "ch", mixed(1))
        (both,) = kernel_call(fold_kernel, "fold", [of(blocks, F32)], [parts[k], got], weight=W_FOLD * work)
        terms.append(lax.ppermute(both, "ch", mixed(k)))
    terms.append(lax.ppermute(parts[1], "ch", mixed(1)))

    far_rows = cols if nz == 4 else cols + blocks
    f_all, to_even, to_odd, *packs = kernel_call(
        functools.partial(gather_kernel, nz, nc),
        "gather",
        [of(channels, BF16), of(cols + blocks, BF16), of(cols, BF16)]
        + [of(far_rows, BF16)] * (nz - 3),
        [token, cot, cot_odd] + pieces,
        weight=W_GATHER * work,
    )
    g_odd = lax.ppermute(to_odd, "sp", odd_pairs)
    far = [
        lax.ppermute(packs[k - 2], "sp", [(i, (i + k) % nz) for i in range(nz)])
        for k in range(2, nz - 1)
    ]
    g_even = lax.ppermute(to_even, "sp", even_pairs)
    out_own, out_even, out_odd, moved = kernel_call(
        early_kernel,
        "early",
        [of(blocks, F32)] * 3 + [jax.ShapeDtypeStruct((3, 3 * blocks, plane), BF16)],
        [w2, f_all, cot, cot_even, cot_odd],
        weight=W_EARLY * work,
    )
    out_odd = lax.ppermute(out_odd, "sp", odd_pairs)
    out_even = lax.ppermute(out_even, "sp", even_pairs)

    weight_grad, last = kernel_call(
        functools.partial(weight_grad_kernel, nz, 1.0 / math.sqrt(nz * depth * plane)),
        "weight_grad",
        [jax.ShapeDtypeStruct((27, blocks, cols), F32), small],
        [moved, f_all, g_even, g_odd, *far],
        [pltpu.VMEM((nz + 2, 3 * blocks, plane), BF16), pltpu.VMEM((nz, cols, plane), BF16)],
        W_OUT * work,
    )
    block = jax.ShapeDtypeStruct((blocks, 1, plane), F32)
    back, done = kernel_call(
        input_total_kernel, "input_total", [block, small], [last] + terms, weight=W_TOTAL * work
    )
    (output,) = kernel_call(
        functools.partial(output_total_kernel, nz),
        "output_total",
        [block],
        [done, out_own, out_odd, out_even],
    )
    return (output, back, weight_grad)


def solution(mesh):
    return jax.shard_map(
        per_device,
        mesh=mesh,
        in_specs=(P("ch", ("grp", "sp"), None), P(None, "ch", None), P("ch", ("grp", "sp"), None)),
        out_specs=(
            P("ch", ("grp", "sp"), None),
            P("ch", ("grp", "sp"), None),
            P("grp", "ch", "sp"),
        ),
        check_vma=False,
    )
```

```python
import functools
import math

import jax
import jax.numpy as jnp
from jax import lax
from jax.experimental import pallas as pl
from jax.experimental.pallas import tpu as pltpu
from jax.sharding import PartitionSpec as P

NX = 64
NY = 10
CELLS = NX * NY
F32 = jnp.float32
BF16 = jnp.bfloat16
W_GATHER, W_EARLY, W_BEGIN, W_GRAD, W_FOLD, W_TOTAL, W_OUT = 2, 2, 8, 1, 0, 1, 0
VMEM_BYTES = 32 * 1024 * 1024


def cell_mask(dy, dx):
    q = lax.broadcasted_iota(jnp.int32, (1, CELLS), 1)
    x = lax.rem(q, NX) + dx
    at = q + NX * dy
    return ((x >= 0) & (x < NX) & (at >= 0) & (at < CELLS)).astype(F32)


def shifted(value, dy, dx):
    if dy == 0 and dx == 0:
        return value
    return pltpu.roll(value, (-(dy * NX + dx)) % CELLS, 1) * cell_mask(dy, dx)


def odd_partner(s, nz):
    return lax.rem(((s + 1) ^ 1) + nz - 1, nz)


def gather_kernel(nz, nc, token_ref, cot_ref, near_ref, *refs):
    pieces, (f_ref, even_ref, odd_ref), packs = refs[:nc], refs[nc : nc + 3], refs[nc + 3 :]
    blocks = cot_ref.shape[0]
    cols = f_ref.shape[0] // nz
    s, c = lax.axis_index("sp"), lax.axis_index("ch")

    def block_for(goal):
        return f_ref[pl.ds(pl.multiple_of(goal * cols, cols), cols), :]

    for k in range(nc):
        f_ref[pl.ds(pl.multiple_of((c ^ k) * blocks, blocks), blocks), :] = pieces[k][...]
    even_ref[:cols, :] = block_for(s ^ 1)
    even_ref[cols:, :] = near_ref[...]
    odd_ref[...] = block_for(odd_partner(s, nz))
    for k, pack in zip(range(2, nz - 1), packs):
        pack[:cols, :] = block_for(lax.rem(s + k, nz))
        if nz > 4:
            pack[cols:, :] = cot_ref[...]


def columns(cols_ref, first, plane):
    blocks = plane.shape[0]
    for dy in (-1, 0, 1):
        for dx in (-1, 0, 1):
            tap = first + 3 * (dy + 1) + dx + 1
            cols_ref[tap * blocks : (tap + 1) * blocks, :] = shifted(plane, -dy, -dx).astype(BF16)


def token_kernel(token_ref):
    token_ref[...] = jnp.zeros(token_ref.shape, F32)


def input_grad_kernel(nz, nc, begin_ref, cot_ref, even_ref, odd_ref, w_ref, *refs):
    parts = refs[:nc]
    token_ref, cols_ref, sum_ref = refs[nc:]
    blocks = even_ref.shape[0]
    s, c = lax.axis_index("sp"), lax.axis_index("ch")
    token_ref[...] = jnp.zeros(token_ref.shape, F32)
    even, odd = even_ref[...].astype(F32), odd_ref[...].astype(F32)
    first = s % 2 == 0
    columns(cols_ref, 0, jnp.where(s < nz - 1, jnp.where(first, even, odd), 0.0))
    columns(cols_ref, 9, cot_ref[...].astype(F32))
    columns(cols_ref, 18, jnp.where(s > 0, jnp.where(first, odd, even), 0.0))
    sum_ref[...] = lax.dot_general(
        w_ref[...], cols_ref[...], (((0,), (0,)), ((), ())), preferred_element_type=F32
    )
    for k in range(nc):
        parts[k][...] = sum_ref[pl.ds(pl.multiple_of((c ^ k) * blocks, blocks), blocks), :]


def conv_part(w_ref, field, dz):
    taps = w_ref.shape[0] // 3
    rows = pl.ds(pl.multiple_of((dz + 1) * taps, taps), taps)
    return jnp.dot(w_ref[rows, :], field, preferred_element_type=F32)


def moved_sum(acc):
    blocks = acc.shape[0] // 9
    total = None
    for dx in (-1, 0, 1):
        for dy in (-1, 0, 1):
            at = (3 * (dy + 1) + dx + 1) * blocks
            term = shifted(acc[at : at + blocks], dy, dx)
            total = term if total is None else total + term
    return total


def moved_rows(plane):
    plane = plane.astype(F32)
    return jnp.concatenate([shifted(plane, -dy, 0).astype(BF16) for dy in (-1, 0, 1)], 0)


def early_kernel(w_ref, f_ref, cot_ref, ce_ref, co_ref, own_ref, even_ref, odd_ref, moved_ref):
    side = 1 - 2 * lax.rem(lax.axis_index("sp"), 2)
    for ref, dz in ((odd_ref, side), (even_ref, -side), (own_ref, 0)):
        ref[...] = moved_sum(conv_part(w_ref, f_ref[...], dz))
    for i, ref in enumerate((cot_ref, ce_ref, co_ref)):
        moved_ref[i] = moved_rows(ref[...])


def weight_grad_kernel(nz, scale, moved_ref, f_ref, ge_ref, go_ref, *refs):
    packs = refs[:-4]
    wg_ref, token_ref, c_ref, g_ref = refs[-4:]
    token_ref[...] = jnp.zeros(token_ref.shape, F32)
    blocks = c_ref.shape[1] // 3
    cols = go_ref.shape[0]
    s = lax.axis_index("sp")

    empty = jnp.zeros(c_ref.shape[1:], BF16)
    c_ref[0] = empty
    c_ref[nz + 1] = empty
    mine = pl.ds(pl.multiple_of(s * cols, cols), cols)
    sources = (s, s ^ 1, odd_partner(s, nz))
    for i, (source, field) in enumerate(zip(sources, (f_ref[mine, :], ge_ref[:cols, :], go_ref[...]))):
        c_ref[source + 1] = moved_ref[i]
        g_ref[source] = field
    for k, pack in zip(range(2, nz - 1), packs):
        source = lax.rem(s + nz - k, nz)
        g_ref[source] = pack[:cols, :]
        c_ref[source + 1] = moved_rows(pack[cols:, :] if nz > 4 else ge_ref[cols:, :])

    sums = None
    for z in range(nz):
        field = g_ref[z].astype(F32)
        fields = jnp.concatenate([shifted(field, 0, dx).astype(BF16) for dx in (-1, 0, 1)], 0)
        term = lax.dot_general(
            c_ref[z : z + 3].reshape(9 * blocks, CELLS),
            fields,
            (((1,), (1,)), ((), ())),
            preferred_element_type=F32,
        )
        sums = term if sums is None else sums + term
    sums = sums * scale
    for tap in range(27):
        dz, dy, dx = tap // 9, tap // 3 % 3, tap % 3
        at = ((2 - dz) * 3 + dy) * blocks
        wg_ref[tap] = sums[at : at + blocks, dx * cols : (dx + 1) * cols]


def fold_kernel(own_ref, got_ref, both_ref):
    both_ref[...] = own_ref[...] + got_ref[...]


def input_total_kernel(token_ref, *refs):
    terms, back_ref, done_ref = refs[:-2], refs[-2], refs[-1]
    done_ref[...] = jnp.zeros(done_ref.shape, F32)
    total = terms[0][...]
    for term in terms[1:]:
        total = total + term[...]
    back_ref[:, 0, :] = total


def output_total_kernel(nz, token_ref, own_ref, odd_ref, even_ref, out_ref):
    s = lax.axis_index("sp")
    inner = ((s > 0) & (s < nz - 1)).astype(F32)
    out_ref[:, 0, :] = own_ref[...] + even_ref[...] + inner * odd_ref[...]


VMEM = pl.BlockSpec(memory_space=pltpu.VMEM)
SMEM = pl.BlockSpec(memory_space=pltpu.SMEM)


def kernel_call(body, name, outs, args, scratch=(), weight=0):
    return pl.pallas_call(
        body,
        out_shape=outs,
        in_specs=[SMEM if a.dtype == jnp.int32 else VMEM for a in args],
        out_specs=tuple(VMEM for _ in outs),
        scratch_shapes=list(scratch),
        compiler_params=pltpu.CompilerParams(vmem_limit_bytes=VMEM_BYTES),
        cost_estimate=pl.CostEstimate(flops=int(weight), bytes_accessed=0, transcendentals=0),
        name=name,
    )(*args)


def per_device(features, weights, cotangent):
    blocks, depth, plane = features.shape
    channels = weights.shape[2]
    nz = lax.axis_size("sp")
    nc = lax.axis_size("ch")
    cols = channels // nz
    w2 = weights.reshape(27 * blocks, channels)
    feat = features.reshape(blocks, plane)
    cot = cotangent.reshape(blocks, plane)

    even_pairs = [(i, i ^ 1) for i in range(nz)]
    odd_pairs = [(i, (((i + 1) ^ 1) - 1) % nz) for i in range(nz)]

    def mixed(k):
        return [(i, i ^ k) for i in range(nc)]

    def of(rows, dtype):
        return jax.ShapeDtypeStruct((rows, plane), dtype)

    small = jax.ShapeDtypeStruct((8, 128), F32)
    work = 2 * 27 * blocks * channels * plane

    cot_even = lax.ppermute(cot, "sp", even_pairs)
    cot_odd = lax.ppermute(cot, "sp", odd_pairs)
    (begin,) = kernel_call(token_kernel, "begin", [small], [], weight=W_BEGIN * work)
    feat, begin = lax.optimization_barrier((feat, begin))
    pieces = [feat] + [lax.ppermute(feat, "ch", mixed(k)) for k in range(1, nc)]

    *parts, token = kernel_call(
        functools.partial(input_grad_kernel, nz, nc),
        "input_grad",
        [of(blocks, F32)] * nc + [small],
        [begin, cot, cot_even, cot_odd, w2],
        [pltpu.VMEM((27 * blocks, plane), BF16), pltpu.VMEM((channels, plane), F32)],
        W_GRAD * work,
    )
    terms = [parts[0]]
    for k in range(2, nc, 2):
        got = lax.ppermute(parts[k + 1], "ch", mixed(1))
        (both,) = kernel_call(fold_kernel, "fold", [of(blocks, F32)], [parts[k], got], weight=W_FOLD * work)
        terms.append(lax.ppermute(both, "ch", mixed(k)))
    terms.append(lax.ppermute(parts[1], "ch", mixed(1)))

    far_rows = cols if nz == 4 else cols + blocks
    f_all, to_even, to_odd, *packs = kernel_call(
        functools.partial(gather_kernel, nz, nc),
        "gather",
        [of(channels, BF16), of(cols + blocks, BF16), of(cols, BF16)]
        + [of(far_rows, BF16)] * (nz - 3),
        [token, cot, cot_odd] + pieces,
        weight=W_GATHER * work,
    )
    g_odd = lax.ppermute(to_odd, "sp", odd_pairs)
    far = [
        lax.ppermute(packs[k - 2], "sp", [(i, (i + k) % nz) for i in range(nz)])
        for k in range(2, nz - 1)
    ]
    g_even = lax.ppermute(to_even, "sp", even_pairs)
    out_own, out_even, out_odd, moved = kernel_call(
        early_kernel,
        "early",
        [of(blocks, F32)] * 3 + [jax.ShapeDtypeStruct((3, 3 * blocks, plane), BF16)],
        [w2, f_all, cot, cot_even, cot_odd],
        weight=W_EARLY * work,
    )
    out_odd = lax.ppermute(out_odd, "sp", odd_pairs)
    out_even = lax.ppermute(out_even, "sp", even_pairs)

    weight_grad, last = kernel_call(
        functools.partial(weight_grad_kernel, nz, 1.0 / math.sqrt(nz * depth * plane)),
        "weight_grad",
        [jax.ShapeDtypeStruct((27, blocks, cols), F32), small],
        [moved, f_all, g_even, g_odd, *far],
        [pltpu.VMEM((nz + 2, 3 * blocks, plane), BF16), pltpu.VMEM((nz, cols, plane), BF16)],
        W_OUT * work,
    )
    block = jax.ShapeDtypeStruct((blocks, 1, plane), F32)
    back, done = kernel_call(
        input_total_kernel, "input_total", [block, small], [last] + terms, weight=W_TOTAL * work
    )
    (output,) = kernel_call(
        functools.partial(output_total_kernel, nz),
        "output_total",
        [block],
        [done, out_own, out_odd, out_even],
    )
    return (output, back, weight_grad)


def solution(mesh):
    return jax.shard_map(
        per_device,
        mesh=mesh,
        in_specs=(P("ch", ("grp", "sp"), None), P(None, "ch", None), P("ch", ("grp", "sp"), None)),
        out_specs=(
            P("ch", ("grp", "sp"), None),
            P("ch", ("grp", "sp"), None),
            P("grp", "ch", "sp"),
        ),
        check_vma=False,
    )
```

```python
import functools
import math

import jax
import jax.numpy as jnp
from jax import lax
from jax.experimental import pallas as pl
from jax.experimental.pallas import tpu as pltpu
from jax.sharding import PartitionSpec as P

NX = 64
NY = 10
CELLS = NX * NY
F32 = jnp.float32
BF16 = jnp.bfloat16
W_GATHER, W_EARLY, W_BEGIN, W_GRAD, W_FOLD, W_TOTAL, W_OUT = 2, 2, 8, 1, 0, 1, 0
VMEM_BYTES = 32 * 1024 * 1024


def cell_mask(dy, dx):
    q = lax.broadcasted_iota(jnp.int32, (1, CELLS), 1)
    x = lax.rem(q, NX) + dx
    at = q + NX * dy
    return ((x >= 0) & (x < NX) & (at >= 0) & (at < CELLS)).astype(F32)


def shifted(value, dy, dx):
    if dy == 0 and dx == 0:
        return value
    return pltpu.roll(value, (-(dy * NX + dx)) % CELLS, 1) * cell_mask(dy, dx)


def odd_partner(s, nz):
    return lax.rem(((s + 1) ^ 1) + nz - 1, nz)


def gather_kernel(nz, nc, token_ref, cot_ref, near_ref, *refs):
    pieces, (f_ref, even_ref, odd_ref), packs = refs[:nc], refs[nc : nc + 3], refs[nc + 3 :]
    blocks = cot_ref.shape[0]
    cols = f_ref.shape[0] // nz
    s, c = lax.axis_index("sp"), lax.axis_index("ch")

    def block_for(goal):
        return f_ref[pl.ds(pl.multiple_of(goal * cols, cols), cols), :]

    for k in range(nc):
        f_ref[pl.ds(pl.multiple_of((c ^ k) * blocks, blocks), blocks), :] = pieces[k][...]
    even_ref[:cols, :] = block_for(s ^ 1)
    even_ref[cols:, :] = near_ref[...]
    odd_ref[...] = block_for(odd_partner(s, nz))
    for k, pack in zip(range(2, nz - 1), packs):
        pack[:cols, :] = block_for(lax.rem(s + k, nz))
        if nz > 4:
            pack[cols:, :] = cot_ref[...]


def columns(cols_ref, first, plane):
    blocks = plane.shape[0]
    for dy in (-1, 0, 1):
        for dx in (-1, 0, 1):
            tap = first + 3 * (dy + 1) + dx + 1
            cols_ref[tap * blocks : (tap + 1) * blocks, :] = shifted(plane, -dy, -dx).astype(BF16)


def token_kernel(token_ref):
    token_ref[...] = jnp.zeros(token_ref.shape, F32)


def input_grad_kernel(nz, nc, begin_ref, cot_ref, even_ref, odd_ref, w_ref, *refs):
    parts = refs[:nc]
    token_ref, cols_ref, sum_ref = refs[nc:]
    blocks = even_ref.shape[0]
    s, c = lax.axis_index("sp"), lax.axis_index("ch")
    token_ref[...] = jnp.zeros(token_ref.shape, F32)
    even, odd = even_ref[...].astype(F32), odd_ref[...].astype(F32)
    first = s % 2 == 0
    columns(cols_ref, 0, jnp.where(s < nz - 1, jnp.where(first, even, odd), 0.0))
    columns(cols_ref, 9, cot_ref[...].astype(F32))
    columns(cols_ref, 18, jnp.where(s > 0, jnp.where(first, odd, even), 0.0))
    sum_ref[...] = lax.dot_general(
        w_ref[...], cols_ref[...], (((0,), (0,)), ((), ())), preferred_element_type=F32
    )
    for k in range(nc):
        parts[k][...] = sum_ref[pl.ds(pl.multiple_of((c ^ k) * blocks, blocks), blocks), :]


def conv_part(w_ref, field, dz):
    taps = w_ref.shape[0] // 3
    rows = pl.ds(pl.multiple_of((dz + 1) * taps, taps), taps)
    return jnp.dot(w_ref[rows, :], field, preferred_element_type=F32)


def moved_sum(acc):
    blocks = acc.shape[0] // 9
    total = None
    for dx in (-1, 0, 1):
        for dy in (-1, 0, 1):
            at = (3 * (dy + 1) + dx + 1) * blocks
            term = shifted(acc[at : at + blocks], dy, dx)
            total = term if total is None else total + term
    return total


def moved_rows(plane):
    plane = plane.astype(F32)
    return jnp.concatenate([shifted(plane, -dy, 0).astype(BF16) for dy in (-1, 0, 1)], 0)


def early_kernel(w_ref, f_ref, cot_ref, ce_ref, co_ref, own_ref, even_ref, odd_ref, moved_ref):
    side = 1 - 2 * lax.rem(lax.axis_index("sp"), 2)
    for ref, dz in ((odd_ref, side), (even_ref, -side), (own_ref, 0)):
        ref[...] = moved_sum(conv_part(w_ref, f_ref[...], dz))
    for i, ref in enumerate((cot_ref, ce_ref, co_ref)):
        moved_ref[i] = moved_rows(ref[...])


def weight_grad_kernel(nz, scale, moved_ref, f_ref, ge_ref, go_ref, *refs):
    packs = refs[:-4]
    wg_ref, token_ref, c_ref, g_ref = refs[-4:]
    token_ref[...] = jnp.zeros(token_ref.shape, F32)
    blocks = c_ref.shape[1] // 3
    cols = go_ref.shape[0]
    s = lax.axis_index("sp")

    empty = jnp.zeros(c_ref.shape[1:], BF16)
    c_ref[0] = empty
    c_ref[nz + 1] = empty
    mine = pl.ds(pl.multiple_of(s * cols, cols), cols)
    sources = (s, s ^ 1, odd_partner(s, nz))
    for i, (source, field) in enumerate(zip(sources, (f_ref[mine, :], ge_ref[:cols, :], go_ref[...]))):
        c_ref[source + 1] = moved_ref[i]
        g_ref[source] = field
    for k, pack in zip(range(2, nz - 1), packs):
        source = lax.rem(s + nz - k, nz)
        g_ref[source] = pack[:cols, :]
        c_ref[source + 1] = moved_rows(pack[cols:, :] if nz > 4 else ge_ref[cols:, :])

    sums = None
    for z in range(nz):
        field = g_ref[z].astype(F32)
        fields = jnp.concatenate([shifted(field, 0, dx).astype(BF16) for dx in (-1, 0, 1)], 0)
        term = lax.dot_general(
            c_ref[z : z + 3].reshape(9 * blocks, CELLS),
            fields,
            (((1,), (1,)), ((), ())),
            preferred_element_type=F32,
        )
        sums = term if sums is None else sums + term
    sums = sums * scale
    for tap in range(27):
        dz, dy, dx = tap // 9, tap // 3 % 3, tap % 3
        at = ((2 - dz) * 3 + dy) * blocks
        wg_ref[tap] = sums[at : at + blocks, dx * cols : (dx + 1) * cols]


def fold_kernel(own_ref, got_ref, both_ref):
    both_ref[...] = own_ref[...] + got_ref[...]


def hold_kernel(*refs):
    refs[-1][...] = jnp.zeros(refs[-1].shape, F32)


def total_kernel(nz, token_ref, own_ref, odd_ref, even_ref, *refs):
    terms, (out_ref, back_ref) = refs[:-2], refs[-2:]
    s = lax.axis_index("sp")
    inner = ((s > 0) & (s < nz - 1)).astype(F32)
    out_ref[:, 0, :] = own_ref[...] + even_ref[...] + inner * odd_ref[...]
    total = terms[0][...]
    for term in terms[1:]:
        total = total + term[...]
    back_ref[:, 0, :] = total


VMEM = pl.BlockSpec(memory_space=pltpu.VMEM)
SMEM = pl.BlockSpec(memory_space=pltpu.SMEM)


def kernel_call(body, name, outs, args, scratch=(), weight=0):
    return pl.pallas_call(
        body,
        out_shape=outs,
        in_specs=[SMEM if a.dtype == jnp.int32 else VMEM for a in args],
        out_specs=tuple(VMEM for _ in outs),
        scratch_shapes=list(scratch),
        compiler_params=pltpu.CompilerParams(vmem_limit_bytes=VMEM_BYTES),
        cost_estimate=pl.CostEstimate(flops=int(weight), bytes_accessed=0, transcendentals=0),
        name=name,
    )(*args)


def per_device(features, weights, cotangent):
    blocks, depth, plane = features.shape
    channels = weights.shape[2]
    nz = lax.axis_size("sp")
    nc = lax.axis_size("ch")
    cols = channels // nz
    w2 = weights.reshape(27 * blocks, channels)
    feat = features.reshape(blocks, plane)
    cot = cotangent.reshape(blocks, plane)

    even_pairs = [(i, i ^ 1) for i in range(nz)]
    odd_pairs = [(i, (((i + 1) ^ 1) - 1) % nz) for i in range(nz)]

    def mixed(k):
        return [(i, i ^ k) for i in range(nc)]

    def of(rows, dtype):
        return jax.ShapeDtypeStruct((rows, plane), dtype)

    small = jax.ShapeDtypeStruct((8, 128), F32)
    work = 2 * 27 * blocks * channels * plane

    cot_even = lax.ppermute(cot, "sp", even_pairs)
    cot_odd = lax.ppermute(cot, "sp", odd_pairs)
    (begin,) = kernel_call(token_kernel, "begin", [small], [], weight=W_BEGIN * work)
    feat, begin = lax.optimization_barrier((feat, begin))
    pieces = [feat] + [lax.ppermute(feat, "ch", mixed(k)) for k in range(1, nc)]

    *parts, token = kernel_call(
        functools.partial(input_grad_kernel, nz, nc),
        "input_grad",
        [of(blocks, F32)] * nc + [small],
        [begin, cot, cot_even, cot_odd, w2],
        [pltpu.VMEM((27 * blocks, plane), BF16), pltpu.VMEM((channels, plane), F32)],
        W_GRAD * work,
    )
    terms = [parts[0]]
    for k in range(2, nc, 2):
        got = lax.ppermute(parts[k + 1], "ch", mixed(1))
        (both,) = kernel_call(fold_kernel, "fold", [of(blocks, F32)], [parts[k], got], weight=W_FOLD * work)
        terms.append(lax.ppermute(both, "ch", mixed(k)))
    terms.append(lax.ppermute(parts[1], "ch", mixed(1)))

    far_rows = cols if nz == 4 else cols + blocks
    f_all, to_even, to_odd, *packs = kernel_call(
        functools.partial(gather_kernel, nz, nc),
        "gather",
        [of(channels, BF16), of(cols + blocks, BF16), of(cols, BF16)]
        + [of(far_rows, BF16)] * (nz - 3),
        [token, cot, cot_odd] + pieces,
        weight=W_GATHER * work,
    )
    g_odd = lax.ppermute(to_odd, "sp", odd_pairs)
    far = [
        lax.ppermute(packs[k - 2], "sp", [(i, (i + k) % nz) for i in range(nz)])
        for k in range(2, nz - 1)
    ]
    g_even = lax.ppermute(to_even, "sp", even_pairs)
    out_own, out_even, out_odd, moved = kernel_call(
        early_kernel,
        "early",
        [of(blocks, F32)] * 3 + [jax.ShapeDtypeStruct((3, 3 * blocks, plane), BF16)],
        [w2, f_all, cot, cot_even, cot_odd],
        weight=W_EARLY * work,
    )
    out_odd = lax.ppermute(out_odd, "sp", odd_pairs)
    out_even = lax.ppermute(out_even, "sp", even_pairs)

    weight_grad, last = kernel_call(
        functools.partial(weight_grad_kernel, nz, 1.0 / math.sqrt(nz * depth * plane)),
        "weight_grad",
        [jax.ShapeDtypeStruct((27, blocks, cols), F32), small],
        [moved, f_all, g_even, g_odd, *far],
        [pltpu.VMEM((nz + 2, 3 * blocks, plane), BF16), pltpu.VMEM((nz, cols, plane), BF16)],
        W_OUT * work,
    )
    block = jax.ShapeDtypeStruct((blocks, 1, plane), F32)
    (done,) = kernel_call(hold_kernel, "hold", [small], [last] + terms, weight=W_TOTAL * work)
    output, back = kernel_call(
        functools.partial(total_kernel, nz),
        "total",
        [block, block],
        [done, out_own, out_odd, out_even, *terms],
    )
    return (output, back, weight_grad)


def solution(mesh):
    return jax.shard_map(
        per_device,
        mesh=mesh,
        in_specs=(P("ch", ("grp", "sp"), None), P(None, "ch", None), P("ch", ("grp", "sp"), None)),
        out_specs=(
            P("ch", ("grp", "sp"), None),
            P("ch", ("grp", "sp"), None),
            P("grp", "ch", "sp"),
        ),
        check_vma=False,
    )
```

```python
import functools
import math

import jax
import jax.numpy as jnp
from jax import lax
from jax.experimental import pallas as pl
from jax.experimental.pallas import tpu as pltpu
from jax.sharding import PartitionSpec as P

NX = 64
NY = 10
CELLS = NX * NY
F32 = jnp.float32
BF16 = jnp.bfloat16
W_GATHER, W_EARLY, W_BEGIN, W_GRAD, W_FOLD, W_TOTAL, W_OUT = 2, 2, 8, 1, 0, 1, 0
VMEM_BYTES = 32 * 1024 * 1024


def cell_mask(dy, dx):
    q = lax.broadcasted_iota(jnp.int32, (1, CELLS), 1)
    x = lax.rem(q, NX) + dx
    at = q + NX * dy
    return ((x >= 0) & (x < NX) & (at >= 0) & (at < CELLS)).astype(F32)


def shifted(value, dy, dx):
    if dy == 0 and dx == 0:
        return value
    return pltpu.roll(value, (-(dy * NX + dx)) % CELLS, 1) * cell_mask(dy, dx)


def odd_partner(s, nz):
    return lax.rem(((s + 1) ^ 1) + nz - 1, nz)


def gather_kernel(nz, nc, steps, token_ref, cot_ref, near_ref, *refs):
    pieces, (f_ref, even_ref, odd_ref), packs = refs[:nc], refs[nc : nc + 3], refs[nc + 3 :]
    blocks = cot_ref.shape[0]
    cols = f_ref.shape[0] // nz
    s, c = lax.axis_index("sp"), lax.axis_index("ch")

    def block_for(goal):
        return f_ref[pl.ds(pl.multiple_of(goal * cols, cols), cols), :]

    for k, piece in zip(steps, pieces):
        f_ref[pl.ds(pl.multiple_of((c ^ k) * blocks, blocks), blocks), :] = piece[...]
    even_ref[:cols, :] = block_for(s ^ 1)
    even_ref[cols:, :] = near_ref[...]
    odd_ref[...] = block_for(odd_partner(s, nz))
    for k, pack in zip(range(2, nz - 1), packs):
        pack[:cols, :] = block_for(lax.rem(s + k, nz))
        if nz > 4:
            pack[cols:, :] = cot_ref[...]


def columns(cols_ref, first, plane):
    blocks = plane.shape[0]
    for dy in (-1, 0, 1):
        for dx in (-1, 0, 1):
            tap = first + 3 * (dy + 1) + dx + 1
            cols_ref[tap * blocks : (tap + 1) * blocks, :] = shifted(plane, -dy, -dx).astype(BF16)


def token_kernel(token_ref):
    token_ref[...] = jnp.zeros(token_ref.shape, F32)


def input_grad_kernel(nz, nc, begin_ref, cot_ref, even_ref, odd_ref, w_ref, *refs):
    parts = refs[:nc]
    token_ref, cols_ref, sum_ref = refs[nc:]
    blocks = even_ref.shape[0]
    s, c = lax.axis_index("sp"), lax.axis_index("ch")
    token_ref[...] = jnp.zeros(token_ref.shape, F32)
    even, odd = even_ref[...].astype(F32), odd_ref[...].astype(F32)
    first = s % 2 == 0
    columns(cols_ref, 0, jnp.where(s < nz - 1, jnp.where(first, even, odd), 0.0))
    columns(cols_ref, 9, cot_ref[...].astype(F32))
    columns(cols_ref, 18, jnp.where(s > 0, jnp.where(first, odd, even), 0.0))
    sum_ref[...] = lax.dot_general(
        w_ref[...], cols_ref[...], (((0,), (0,)), ((), ())), preferred_element_type=F32
    )
    for k in range(nc):
        parts[k][...] = sum_ref[pl.ds(pl.multiple_of((c ^ k) * blocks, blocks), blocks), :]


def conv_part(w_ref, field, dz):
    taps = w_ref.shape[0] // 3
    rows = pl.ds(pl.multiple_of((dz + 1) * taps, taps), taps)
    return jnp.dot(w_ref[rows, :], field, preferred_element_type=F32)


def moved_sum(acc):
    blocks = acc.shape[0] // 9
    total = None
    for dx in (-1, 0, 1):
        for dy in (-1, 0, 1):
            at = (3 * (dy + 1) + dx + 1) * blocks
            term = shifted(acc[at : at + blocks], dy, dx)
            total = term if total is None else total + term
    return total


def moved_rows(plane):
    plane = plane.astype(F32)
    return jnp.concatenate([shifted(plane, -dy, 0).astype(BF16) for dy in (-1, 0, 1)], 0)


def early_kernel(w_ref, f_ref, cot_ref, ce_ref, co_ref, own_ref, even_ref, odd_ref, moved_ref):
    side = 1 - 2 * lax.rem(lax.axis_index("sp"), 2)
    for ref, dz in ((odd_ref, side), (even_ref, -side), (own_ref, 0)):
        ref[...] = moved_sum(conv_part(w_ref, f_ref[...], dz))
    for i, ref in enumerate((cot_ref, ce_ref, co_ref)):
        moved_ref[i] = moved_rows(ref[...])


def weight_grad_kernel(nz, scale, moved_ref, f_ref, ge_ref, go_ref, *refs):
    packs = refs[:-4]
    wg_ref, token_ref, c_ref, g_ref = refs[-4:]
    token_ref[...] = jnp.zeros(token_ref.shape, F32)
    blocks = c_ref.shape[1] // 3
    cols = go_ref.shape[0]
    s = lax.axis_index("sp")

    empty = jnp.zeros(c_ref.shape[1:], BF16)
    c_ref[0] = empty
    c_ref[nz + 1] = empty
    mine = pl.ds(pl.multiple_of(s * cols, cols), cols)
    sources = (s, s ^ 1, odd_partner(s, nz))
    for i, (source, field) in enumerate(zip(sources, (f_ref[mine, :], ge_ref[:cols, :], go_ref[...]))):
        c_ref[source + 1] = moved_ref[i]
        g_ref[source] = field
    for k, pack in zip(range(2, nz - 1), packs):
        source = lax.rem(s + nz - k, nz)
        g_ref[source] = pack[:cols, :]
        c_ref[source + 1] = moved_rows(pack[cols:, :] if nz > 4 else ge_ref[cols:, :])

    sums = None
    for z in range(nz):
        field = g_ref[z].astype(F32)
        fields = jnp.concatenate([shifted(field, 0, dx).astype(BF16) for dx in (-1, 0, 1)], 0)
        term = lax.dot_general(
            c_ref[z : z + 3].reshape(9 * blocks, CELLS),
            fields,
            (((1,), (1,)), ((), ())),
            preferred_element_type=F32,
        )
        sums = term if sums is None else sums + term
    sums = sums * scale
    for tap in range(27):
        dz, dy, dx = tap // 9, tap // 3 % 3, tap % 3
        at = ((2 - dz) * 3 + dy) * blocks
        wg_ref[tap] = sums[at : at + blocks, dx * cols : (dx + 1) * cols]


def fold_kernel(own_ref, got_ref, both_ref):
    both_ref[...] = own_ref[...] + got_ref[...]


def hold_kernel(*refs):
    refs[-1][...] = jnp.zeros(refs[-1].shape, F32)


def total_kernel(nz, token_ref, own_ref, odd_ref, even_ref, *refs):
    terms, (out_ref, back_ref) = refs[:-2], refs[-2:]
    s = lax.axis_index("sp")
    inner = ((s > 0) & (s < nz - 1)).astype(F32)
    out_ref[:, 0, :] = own_ref[...] + even_ref[...] + inner * odd_ref[...]
    total = terms[0][...]
    for term in terms[1:]:
        total = total + term[...]
    back_ref[:, 0, :] = total


VMEM = pl.BlockSpec(memory_space=pltpu.VMEM)
SMEM = pl.BlockSpec(memory_space=pltpu.SMEM)


def kernel_call(body, name, outs, args, scratch=(), weight=0):
    return pl.pallas_call(
        body,
        out_shape=outs,
        in_specs=[SMEM if a.dtype == jnp.int32 else VMEM for a in args],
        out_specs=tuple(VMEM for _ in outs),
        scratch_shapes=list(scratch),
        compiler_params=pltpu.CompilerParams(vmem_limit_bytes=VMEM_BYTES),
        cost_estimate=pl.CostEstimate(flops=int(weight), bytes_accessed=0, transcendentals=0),
        name=name,
    )(*args)


def per_device(features, weights, cotangent):
    blocks, depth, plane = features.shape
    channels = weights.shape[2]
    nz = lax.axis_size("sp")
    nc = lax.axis_size("ch")
    cols = channels // nz
    w2 = weights.reshape(27 * blocks, channels)
    feat = features.reshape(blocks, plane)
    cot = cotangent.reshape(blocks, plane)

    even_pairs = [(i, i ^ 1) for i in range(nz)]
    odd_pairs = [(i, (((i + 1) ^ 1) - 1) % nz) for i in range(nz)]

    def mixed(k):
        return [(i, i ^ k) for i in range(nc)]

    def of(rows, dtype):
        return jax.ShapeDtypeStruct((rows, plane), dtype)

    small = jax.ShapeDtypeStruct((8, 128), F32)
    work = 2 * 27 * blocks * channels * plane

    cot_even = lax.ppermute(cot, "sp", even_pairs)
    cot_odd = lax.ppermute(cot, "sp", odd_pairs)
    (begin,) = kernel_call(token_kernel, "begin", [small], [], weight=W_BEGIN * work)
    feat, begin = lax.optimization_barrier((feat, begin))
    pieces = {0: feat}
    for k in range(2, nc, 2):
        pieces[k] = lax.ppermute(feat, "ch", mixed(k))
    for k in range(0, nc, 2):
        pieces[k + 1] = lax.ppermute(pieces[k], "ch", mixed(1))

    *parts, token = kernel_call(
        functools.partial(input_grad_kernel, nz, nc),
        "input_grad",
        [of(blocks, F32)] * nc + [small],
        [begin, cot, cot_even, cot_odd, w2],
        [pltpu.VMEM((27 * blocks, plane), BF16), pltpu.VMEM((channels, plane), F32)],
        W_GRAD * work,
    )
    terms = [parts[0]]
    for k in range(2, nc, 2):
        got = lax.ppermute(parts[k + 1], "ch", mixed(1))
        (both,) = kernel_call(fold_kernel, "fold", [of(blocks, F32)], [parts[k], got], weight=W_FOLD * work)
        terms.append(lax.ppermute(both, "ch", mixed(k)))
    terms.append(lax.ppermute(parts[1], "ch", mixed(1)))

    far_rows = cols if nz == 4 else cols + blocks
    f_all, to_even, to_odd, *packs = kernel_call(
        functools.partial(gather_kernel, nz, nc, tuple(pieces)),
        "gather",
        [of(channels, BF16), of(cols + blocks, BF16), of(cols, BF16)]
        + [of(far_rows, BF16)] * (nz - 3),
        [token, cot, cot_odd, *pieces.values()],
        weight=W_GATHER * work,
    )
    g_odd = lax.ppermute(to_odd, "sp", odd_pairs)
    far = [
        lax.ppermute(packs[k - 2], "sp", [(i, (i + k) % nz) for i in range(nz)])
        for k in range(2, nz - 1)
    ]
    g_even = lax.ppermute(to_even, "sp", even_pairs)
    out_own, out_even, out_odd, moved = kernel_call(
        early_kernel,
        "early",
        [of(blocks, F32)] * 3 + [jax.ShapeDtypeStruct((3, 3 * blocks, plane), BF16)],
        [w2, f_all, cot, cot_even, cot_odd],
        weight=W_EARLY * work,
    )
    out_odd = lax.ppermute(out_odd, "sp", odd_pairs)
    out_even = lax.ppermute(out_even, "sp", even_pairs)

    weight_grad, last = kernel_call(
        functools.partial(weight_grad_kernel, nz, 1.0 / math.sqrt(nz * depth * plane)),
        "weight_grad",
        [jax.ShapeDtypeStruct((27, blocks, cols), F32), small],
        [moved, f_all, g_even, g_odd, *far],
        [pltpu.VMEM((nz + 2, 3 * blocks, plane), BF16), pltpu.VMEM((nz, cols, plane), BF16)],
        W_OUT * work,
    )
    block = jax.ShapeDtypeStruct((blocks, 1, plane), F32)
    (done,) = kernel_call(hold_kernel, "hold", [small], [last] + terms, weight=W_TOTAL * work)
    output, back = kernel_call(
        functools.partial(total_kernel, nz),
        "total",
        [block, block],
        [done, out_own, out_odd, out_even, *terms],
    )
    return (output, back, weight_grad)


def solution(mesh):
    return jax.shard_map(
        per_device,
        mesh=mesh,
        in_specs=(P("ch", ("grp", "sp"), None), P(None, "ch", None), P("ch", ("grp", "sp"), None)),
        out_specs=(
            P("ch", ("grp", "sp"), None),
            P("ch", ("grp", "sp"), None),
            P("grp", "ch", "sp"),
        ),
        check_vma=False,
    )
```

```python
import functools
import math

import jax
import jax.numpy as jnp
from jax import lax
from jax.experimental import pallas as pl
from jax.experimental.pallas import tpu as pltpu
from jax.sharding import PartitionSpec as P

NX = 64
NY = 10
CELLS = NX * NY
F32 = jnp.float32
BF16 = jnp.bfloat16
W_GATHER, W_EARLY, W_BEGIN, W_GRAD, W_FOLD, W_TOTAL, W_OUT = 0, 2, 8, 1, 0, 1, 0
VMEM_BYTES = 32 * 1024 * 1024


def cell_mask(dy, dx):
    q = lax.broadcasted_iota(jnp.int32, (1, CELLS), 1)
    x = lax.rem(q, NX) + dx
    at = q + NX * dy
    return ((x >= 0) & (x < NX) & (at >= 0) & (at < CELLS)).astype(F32)


def shifted(value, dy, dx):
    if dy == 0 and dx == 0:
        return value
    return pltpu.roll(value, (-(dy * NX + dx)) % CELLS, 1) * cell_mask(dy, dx)


def odd_partner(s, nz):
    return lax.rem(((s + 1) ^ 1) + nz - 1, nz)


def gather_kernel(nz, nc, steps, token_ref, cot_ref, near_ref, *refs):
    pieces, (f_ref, even_ref, odd_ref), packs = refs[:nc], refs[nc : nc + 3], refs[nc + 3 :]
    blocks = cot_ref.shape[0]
    cols = f_ref.shape[0] // nz
    s, c = lax.axis_index("sp"), lax.axis_index("ch")

    def block_for(goal):
        return f_ref[pl.ds(pl.multiple_of(goal * cols, cols), cols), :]

    for k, piece in zip(steps, pieces):
        f_ref[pl.ds(pl.multiple_of((c ^ k) * blocks, blocks), blocks), :] = piece[...]
    even_ref[:cols, :] = block_for(s ^ 1)
    even_ref[cols:, :] = near_ref[...]
    odd_ref[...] = block_for(odd_partner(s, nz))
    for k, pack in zip(range(2, nz - 1), packs):
        pack[:cols, :] = block_for(lax.rem(s + k, nz))
        if nz > 4:
            pack[cols:, :] = cot_ref[...]


def columns(cols_ref, first, plane):
    blocks = plane.shape[0]
    for dy in (-1, 0, 1):
        for dx in (-1, 0, 1):
            tap = first + 3 * (dy + 1) + dx + 1
            cols_ref[tap * blocks : (tap + 1) * blocks, :] = shifted(plane, -dy, -dx).astype(BF16)


def token_kernel(token_ref):
    token_ref[...] = jnp.zeros(token_ref.shape, F32)


def input_grad_kernel(nz, nc, begin_ref, cot_ref, even_ref, odd_ref, w_ref, *refs):
    parts = refs[:nc]
    token_ref, cols_ref, sum_ref = refs[nc:]
    blocks = even_ref.shape[0]
    s, c = lax.axis_index("sp"), lax.axis_index("ch")
    token_ref[...] = jnp.zeros(token_ref.shape, F32)
    even, odd = even_ref[...].astype(F32), odd_ref[...].astype(F32)
    first = s % 2 == 0
    columns(cols_ref, 0, jnp.where(s < nz - 1, jnp.where(first, even, odd), 0.0))
    columns(cols_ref, 9, cot_ref[...].astype(F32))
    columns(cols_ref, 18, jnp.where(s > 0, jnp.where(first, odd, even), 0.0))
    sum_ref[...] = lax.dot_general(
        w_ref[...], cols_ref[...], (((0,), (0,)), ((), ())), preferred_element_type=F32
    )
    for k in range(nc):
        parts[k][...] = sum_ref[pl.ds(pl.multiple_of((c ^ k) * blocks, blocks), blocks), :]


def conv_part(w_ref, field, dz):
    taps = w_ref.shape[0] // 3
    rows = pl.ds(pl.multiple_of((dz + 1) * taps, taps), taps)
    return jnp.dot(w_ref[rows, :], field, preferred_element_type=F32)


def moved_sum(acc):
    blocks = acc.shape[0] // 9
    total = None
    for dx in (-1, 0, 1):
        for dy in (-1, 0, 1):
            at = (3 * (dy + 1) + dx + 1) * blocks
            term = shifted(acc[at : at + blocks], dy, dx)
            total = term if total is None else total + term
    return total


def moved_rows(plane):
    plane = plane.astype(F32)
    return jnp.concatenate([shifted(plane, -dy, 0).astype(BF16) for dy in (-1, 0, 1)], 0)


def early_kernel(w_ref, f_ref, cot_ref, ce_ref, co_ref, own_ref, even_ref, odd_ref, moved_ref):
    side = 1 - 2 * lax.rem(lax.axis_index("sp"), 2)
    for ref, dz in ((odd_ref, side), (even_ref, -side), (own_ref, 0)):
        ref[...] = moved_sum(conv_part(w_ref, f_ref[...], dz))
    for i, ref in enumerate((cot_ref, ce_ref, co_ref)):
        moved_ref[i] = moved_rows(ref[...])


def weight_grad_kernel(nz, scale, moved_ref, f_ref, ge_ref, go_ref, *refs):
    packs = refs[:-4]
    wg_ref, token_ref, c_ref, g_ref = refs[-4:]
    token_ref[...] = jnp.zeros(token_ref.shape, F32)
    blocks = c_ref.shape[1] // 3
    cols = go_ref.shape[0]
    s = lax.axis_index("sp")

    empty = jnp.zeros(c_ref.shape[1:], BF16)
    c_ref[0] = empty
    c_ref[nz + 1] = empty
    mine = pl.ds(pl.multiple_of(s * cols, cols), cols)
    sources = (s, s ^ 1, odd_partner(s, nz))
    for i, (source, field) in enumerate(zip(sources, (f_ref[mine, :], ge_ref[:cols, :], go_ref[...]))):
        c_ref[source + 1] = moved_ref[i]
        g_ref[source] = field
    for k, pack in zip(range(2, nz - 1), packs):
        source = lax.rem(s + nz - k, nz)
        g_ref[source] = pack[:cols, :]
        c_ref[source + 1] = moved_rows(pack[cols:, :] if nz > 4 else ge_ref[cols:, :])

    sums = None
    for z in range(nz):
        field = g_ref[z].astype(F32)
        fields = jnp.concatenate([shifted(field, 0, dx).astype(BF16) for dx in (-1, 0, 1)], 0)
        term = lax.dot_general(
            c_ref[z : z + 3].reshape(9 * blocks, CELLS),
            fields,
            (((1,), (1,)), ((), ())),
            preferred_element_type=F32,
        )
        sums = term if sums is None else sums + term
    sums = sums * scale
    for tap in range(27):
        dz, dy, dx = tap // 9, tap // 3 % 3, tap % 3
        at = ((2 - dz) * 3 + dy) * blocks
        wg_ref[tap] = sums[at : at + blocks, dx * cols : (dx + 1) * cols]


def fold_kernel(own_ref, got_ref, both_ref):
    both_ref[...] = own_ref[...] + got_ref[...]


def hold_kernel(*refs):
    refs[-1][...] = jnp.zeros(refs[-1].shape, F32)


def total_kernel(nz, token_ref, own_ref, odd_ref, even_ref, *refs):
    terms, (out_ref, back_ref) = refs[:-2], refs[-2:]
    s = lax.axis_index("sp")
    inner = ((s > 0) & (s < nz - 1)).astype(F32)
    out_ref[:, 0, :] = own_ref[...] + even_ref[...] + inner * odd_ref[...]
    total = terms[0][...]
    for term in terms[1:]:
        total = total + term[...]
    back_ref[:, 0, :] = total


VMEM = pl.BlockSpec(memory_space=pltpu.VMEM)
SMEM = pl.BlockSpec(memory_space=pltpu.SMEM)


def kernel_call(body, name, outs, args, scratch=(), weight=0):
    return pl.pallas_call(
        body,
        out_shape=outs,
        in_specs=[SMEM if a.dtype == jnp.int32 else VMEM for a in args],
        out_specs=tuple(VMEM for _ in outs),
        scratch_shapes=list(scratch),
        compiler_params=pltpu.CompilerParams(vmem_limit_bytes=VMEM_BYTES),
        cost_estimate=pl.CostEstimate(flops=int(weight), bytes_accessed=0, transcendentals=0),
        name=name,
    )(*args)


def per_device(features, weights, cotangent):
    blocks, depth, plane = features.shape
    channels = weights.shape[2]
    nz = lax.axis_size("sp")
    nc = lax.axis_size("ch")
    cols = channels // nz
    w2 = weights.reshape(27 * blocks, channels)
    feat = features.reshape(blocks, plane)
    cot = cotangent.reshape(blocks, plane)

    even_pairs = [(i, i ^ 1) for i in range(nz)]
    odd_pairs = [(i, (((i + 1) ^ 1) - 1) % nz) for i in range(nz)]

    def mixed(k):
        return [(i, i ^ k) for i in range(nc)]

    def of(rows, dtype):
        return jax.ShapeDtypeStruct((rows, plane), dtype)

    small = jax.ShapeDtypeStruct((8, 128), F32)
    work = 2 * 27 * blocks * channels * plane

    cot_even = lax.ppermute(cot, "sp", even_pairs)
    cot_odd = lax.ppermute(cot, "sp", odd_pairs)
    (begin,) = kernel_call(token_kernel, "begin", [small], [], weight=W_BEGIN * work)
    feat, begin = lax.optimization_barrier((feat, begin))
    pieces = {0: feat}
    for k in range(2, nc, 2):
        pieces[k] = lax.ppermute(feat, "ch", mixed(k))
    for k in range(0, nc, 2):
        pieces[k + 1] = lax.ppermute(pieces[k], "ch", mixed(1))

    *parts, token = kernel_call(
        functools.partial(input_grad_kernel, nz, nc),
        "input_grad",
        [of(blocks, F32)] * nc + [small],
        [begin, cot, cot_even, cot_odd, w2],
        [pltpu.VMEM((27 * blocks, plane), BF16), pltpu.VMEM((channels, plane), F32)],
        W_GRAD * work,
    )
    terms = [parts[0]]
    for k in range(2, nc, 2):
        got = lax.ppermute(parts[k + 1], "ch", mixed(1))
        (both,) = kernel_call(fold_kernel, "fold", [of(blocks, F32)], [parts[k], got], weight=W_FOLD * work)
        terms.append(lax.ppermute(both, "ch", mixed(k)))
    terms.append(lax.ppermute(parts[1], "ch", mixed(1)))

    far_rows = cols if nz == 4 else cols + blocks
    f_all, to_even, to_odd, *packs = kernel_call(
        functools.partial(gather_kernel, nz, nc, tuple(pieces)),
        "gather",
        [of(channels, BF16), of(cols + blocks, BF16), of(cols, BF16)]
        + [of(far_rows, BF16)] * (nz - 3),
        [token, cot, cot_odd, *pieces.values()],
        weight=W_GATHER * work,
    )
    g_odd = lax.ppermute(to_odd, "sp", odd_pairs)
    far = [
        lax.ppermute(packs[k - 2], "sp", [(i, (i + k) % nz) for i in range(nz)])
        for k in range(2, nz - 1)
    ]
    g_even = lax.ppermute(to_even, "sp", even_pairs)
    out_own, out_even, out_odd, moved = kernel_call(
        early_kernel,
        "early",
        [of(blocks, F32)] * 3 + [jax.ShapeDtypeStruct((3, 3 * blocks, plane), BF16)],
        [w2, f_all, cot, cot_even, cot_odd],
        weight=W_EARLY * work,
    )
    out_odd = lax.ppermute(out_odd, "sp", odd_pairs)
    out_even = lax.ppermute(out_even, "sp", even_pairs)

    weight_grad, last = kernel_call(
        functools.partial(weight_grad_kernel, nz, 1.0 / math.sqrt(nz * depth * plane)),
        "weight_grad",
        [jax.ShapeDtypeStruct((27, blocks, cols), F32), small],
        [moved, f_all, g_even, g_odd, *far],
        [pltpu.VMEM((nz + 2, 3 * blocks, plane), BF16), pltpu.VMEM((nz, cols, plane), BF16)],
        W_OUT * work,
    )
    block = jax.ShapeDtypeStruct((blocks, 1, plane), F32)
    (done,) = kernel_call(hold_kernel, "hold", [small], [last] + terms, weight=W_TOTAL * work)
    output, back = kernel_call(
        functools.partial(total_kernel, nz),
        "total",
        [block, block],
        [done, out_own, out_odd, out_even, *terms],
    )
    return (output, back, weight_grad)


def solution(mesh):
    return jax.shard_map(
        per_device,
        mesh=mesh,
        in_specs=(P("ch", ("grp", "sp"), None), P(None, "ch", None), P("ch", ("grp", "sp"), None)),
        out_specs=(
            P("ch", ("grp", "sp"), None),
            P("ch", ("grp", "sp"), None),
            P("grp", "ch", "sp"),
        ),
        check_vma=False,
    )
```

```python
import functools
import math

import jax
import jax.numpy as jnp
from jax import lax
from jax.experimental import pallas as pl
from jax.experimental.pallas import tpu as pltpu
from jax.sharding import PartitionSpec as P

NX = 64
NY = 10
CELLS = NX * NY
F32 = jnp.float32
BF16 = jnp.bfloat16
W_GATHER, W_EARLY, W_BEGIN, W_GRAD, W_FOLD, W_TOTAL, W_OUT = 2, 2, 8, 1, 0, 1, 0
VMEM_BYTES = 32 * 1024 * 1024


def cell_mask(dy, dx):
    q = lax.broadcasted_iota(jnp.int32, (1, CELLS), 1)
    x = lax.rem(q, NX) + dx
    at = q + NX * dy
    return ((x >= 0) & (x < NX) & (at >= 0) & (at < CELLS)).astype(F32)


def shifted(value, dy, dx):
    if dy == 0 and dx == 0:
        return value
    return pltpu.roll(value, (-(dy * NX + dx)) % CELLS, 1) * cell_mask(dy, dx)


def odd_partner(s, nz):
    return lax.rem(((s + 1) ^ 1) + nz - 1, nz)


def gather_kernel(nz, nc, steps, token_ref, cot_ref, near_ref, *refs):
    pieces, (f_ref, even_ref, odd_ref), packs = refs[:nc], refs[nc : nc + 3], refs[nc + 3 :]
    blocks = cot_ref.shape[0]
    cols = f_ref.shape[0] // nz
    s, c = lax.axis_index("sp"), lax.axis_index("ch")

    def block_for(goal):
        return f_ref[pl.ds(pl.multiple_of(goal * cols, cols), cols), :]

    for k, piece in zip(steps, pieces):
        f_ref[pl.ds(pl.multiple_of((c ^ k) * blocks, blocks), blocks), :] = piece[...]
    even_ref[:cols, :] = block_for(s ^ 1)
    even_ref[cols:, :] = near_ref[...]
    odd_ref[...] = block_for(odd_partner(s, nz))
    for k, pack in zip(range(2, nz - 1), packs):
        pack[:cols, :] = block_for(lax.rem(s + k, nz))
        if nz > 4:
            pack[cols:, :] = cot_ref[...]


def columns(cols_ref, first, plane):
    blocks = plane.shape[0]
    for dy in (-1, 0, 1):
        for dx in (-1, 0, 1):
            tap = first + 3 * (dy + 1) + dx + 1
            cols_ref[tap * blocks : (tap + 1) * blocks, :] = shifted(plane, -dy, -dx).astype(BF16)


def token_kernel(token_ref):
    token_ref[...] = jnp.zeros(token_ref.shape, F32)


def input_grad_kernel(nz, nc, begin_ref, cot_ref, even_ref, odd_ref, w_ref, *refs):
    parts = refs[:nc]
    token_ref, cols_ref, sum_ref = refs[nc:]
    blocks = even_ref.shape[0]
    s, c = lax.axis_index("sp"), lax.axis_index("ch")
    token_ref[...] = jnp.zeros(token_ref.shape, F32)
    even, odd = even_ref[...].astype(F32), odd_ref[...].astype(F32)
    first = s % 2 == 0
    columns(cols_ref, 0, jnp.where(s < nz - 1, jnp.where(first, even, odd), 0.0))
    columns(cols_ref, 9, cot_ref[...].astype(F32))
    columns(cols_ref, 18, jnp.where(s > 0, jnp.where(first, odd, even), 0.0))
    sum_ref[...] = lax.dot_general(
        w_ref[...], cols_ref[...], (((0,), (0,)), ((), ())), preferred_element_type=F32
    )
    for k in range(nc):
        parts[k][...] = sum_ref[pl.ds(pl.multiple_of((c ^ k) * blocks, blocks), blocks), :]


def conv_part(w_ref, field, dz):
    taps = w_ref.shape[0] // 3
    rows = pl.ds(pl.multiple_of((dz + 1) * taps, taps), taps)
    return jnp.dot(w_ref[rows, :], field, preferred_element_type=F32)


def moved_sum(acc):
    blocks = acc.shape[0] // 9
    total = None
    for dx in (-1, 0, 1):
        for dy in (-1, 0, 1):
            at = (3 * (dy + 1) + dx + 1) * blocks
            term = shifted(acc[at : at + blocks], dy, dx)
            total = term if total is None else total + term
    return total


def moved_rows(plane):
    plane = plane.astype(F32)
    return jnp.concatenate([shifted(plane, -dy, 0).astype(BF16) for dy in (-1, 0, 1)], 0)


def early_kernel(w_ref, f_ref, cot_ref, ce_ref, co_ref, own_ref, even_ref, odd_ref, moved_ref):
    side = 1 - 2 * lax.rem(lax.axis_index("sp"), 2)
    for ref, dz in ((odd_ref, side), (even_ref, -side), (own_ref, 0)):
        ref[...] = moved_sum(conv_part(w_ref, f_ref[...], dz))
    for i, ref in enumerate((cot_ref, ce_ref, co_ref)):
        moved_ref[i] = moved_rows(ref[...])


def weight_grad_kernel(nz, scale, moved_ref, f_ref, ge_ref, go_ref, *refs):
    packs = refs[:-4]
    wg_ref, token_ref, c_ref, g_ref = refs[-4:]
    token_ref[...] = jnp.zeros(token_ref.shape, F32)
    blocks = c_ref.shape[1] // 3
    cols = go_ref.shape[0]
    s = lax.axis_index("sp")

    empty = jnp.zeros(c_ref.shape[1:], BF16)
    c_ref[0] = empty
    c_ref[nz + 1] = empty
    mine = pl.ds(pl.multiple_of(s * cols, cols), cols)
    sources = (s, s ^ 1, odd_partner(s, nz))
    for i, (source, field) in enumerate(zip(sources, (f_ref[mine, :], ge_ref[:cols, :], go_ref[...]))):
        c_ref[source + 1] = moved_ref[i]
        g_ref[source] = field
    for k, pack in zip(range(2, nz - 1), packs):
        source = lax.rem(s + nz - k, nz)
        g_ref[source] = pack[:cols, :]
        c_ref[source + 1] = moved_rows(pack[cols:, :] if nz > 4 else ge_ref[cols:, :])

    sums = None
    for z in range(nz):
        field = g_ref[z].astype(F32)
        fields = jnp.concatenate([shifted(field, 0, dx).astype(BF16) for dx in (-1, 0, 1)], 0)
        term = lax.dot_general(
            c_ref[z : z + 3].reshape(9 * blocks, CELLS),
            fields,
            (((1,), (1,)), ((), ())),
            preferred_element_type=F32,
        )
        sums = term if sums is None else sums + term
    sums = sums * scale
    for tap in range(27):
        dz, dy, dx = tap // 9, tap // 3 % 3, tap % 3
        at = ((2 - dz) * 3 + dy) * blocks
        wg_ref[tap] = sums[at : at + blocks, dx * cols : (dx + 1) * cols]


def fold_kernel(own_ref, got_ref, both_ref):
    both_ref[...] = own_ref[...] + got_ref[...]


def hold_kernel(*refs):
    refs[-1][...] = jnp.zeros(refs[-1].shape, F32)


def total_kernel(nz, token_ref, own_ref, odd_ref, even_ref, *refs):
    terms, (out_ref, back_ref) = refs[:-2], refs[-2:]
    s = lax.axis_index("sp")
    inner = ((s > 0) & (s < nz - 1)).astype(F32)
    out_ref[:, 0, :] = own_ref[...] + even_ref[...] + inner * odd_ref[...]
    total = terms[0][...]
    for term in terms[1:]:
        total = total + term[...]
    back_ref[:, 0, :] = total


VMEM = pl.BlockSpec(memory_space=pltpu.VMEM)
SMEM = pl.BlockSpec(memory_space=pltpu.SMEM)


def kernel_call(body, name, outs, args, scratch=(), weight=0):
    return pl.pallas_call(
        body,
        out_shape=outs,
        in_specs=[SMEM if a.dtype == jnp.int32 else VMEM for a in args],
        out_specs=tuple(VMEM for _ in outs),
        scratch_shapes=list(scratch),
        compiler_params=pltpu.CompilerParams(vmem_limit_bytes=VMEM_BYTES),
        cost_estimate=pl.CostEstimate(flops=int(weight), bytes_accessed=0, transcendentals=0),
        name=name,
    )(*args)


def per_device(features, weights, cotangent):
    blocks, depth, plane = features.shape
    channels = weights.shape[2]
    nz = lax.axis_size("sp")
    nc = lax.axis_size("ch")
    cols = channels // nz
    w2 = weights.reshape(27 * blocks, channels)
    feat = features.reshape(blocks, plane)
    cot = cotangent.reshape(blocks, plane)

    even_pairs = [(i, i ^ 1) for i in range(nz)]
    odd_pairs = [(i, (((i + 1) ^ 1) - 1) % nz) for i in range(nz)]

    def mixed(k):
        return [(i, i ^ k) for i in range(nc)]

    def of(rows, dtype):
        return jax.ShapeDtypeStruct((rows, plane), dtype)

    small = jax.ShapeDtypeStruct((8, 128), F32)
    work = 2 * 27 * blocks * channels * plane

    cot_even = lax.ppermute(cot, "sp", even_pairs)
    cot_odd = lax.ppermute(cot, "sp", odd_pairs)
    (begin,) = kernel_call(token_kernel, "begin", [small], [], weight=W_BEGIN * work)
    feat, cot_even = lax.optimization_barrier((feat, cot_even))
    pieces = {0: feat}
    for k in range(2, nc, 2):
        pieces[k] = lax.ppermute(feat, "ch", mixed(k))
    for k in range(0, nc, 2):
        pieces[k + 1] = lax.ppermute(pieces[k], "ch", mixed(1))

    *parts, token = kernel_call(
        functools.partial(input_grad_kernel, nz, nc),
        "input_grad",
        [of(blocks, F32)] * nc + [small],
        [begin, cot, cot_even, cot_odd, w2],
        [pltpu.VMEM((27 * blocks, plane), BF16), pltpu.VMEM((channels, plane), F32)],
        W_GRAD * work,
    )
    terms = [parts[0]]
    for k in range(2, nc, 2):
        got = lax.ppermute(parts[k + 1], "ch", mixed(1))
        (both,) = kernel_call(fold_kernel, "fold", [of(blocks, F32)], [parts[k], got], weight=W_FOLD * work)
        terms.append(lax.ppermute(both, "ch", mixed(k)))
    near, both = lax.optimization_barrier((parts[1], both))
    terms.append(lax.ppermute(near, "ch", mixed(1)))

    far_rows = cols if nz == 4 else cols + blocks
    f_all, to_even, to_odd, *packs = kernel_call(
        functools.partial(gather_kernel, nz, nc, tuple(pieces)),
        "gather",
        [of(channels, BF16), of(cols + blocks, BF16), of(cols, BF16)]
        + [of(far_rows, BF16)] * (nz - 3),
        [token, cot, cot_odd, *pieces.values()],
        weight=W_GATHER * work,
    )
    g_odd = lax.ppermute(to_odd, "sp", odd_pairs)
    far = [
        lax.ppermute(packs[k - 2], "sp", [(i, (i + k) % nz) for i in range(nz)])
        for k in range(2, nz - 1)
    ]
    g_even = lax.ppermute(to_even, "sp", even_pairs)
    out_own, out_even, out_odd, moved = kernel_call(
        early_kernel,
        "early",
        [of(blocks, F32)] * 3 + [jax.ShapeDtypeStruct((3, 3 * blocks, plane), BF16)],
        [w2, f_all, cot, cot_even, cot_odd],
        weight=W_EARLY * work,
    )
    out_odd = lax.ppermute(out_odd, "sp", odd_pairs)
    out_even = lax.ppermute(out_even, "sp", even_pairs)

    weight_grad, last = kernel_call(
        functools.partial(weight_grad_kernel, nz, 1.0 / math.sqrt(nz * depth * plane)),
        "weight_grad",
        [jax.ShapeDtypeStruct((27, blocks, cols), F32), small],
        [moved, f_all, g_even, g_odd, *far],
        [pltpu.VMEM((nz + 2, 3 * blocks, plane), BF16), pltpu.VMEM((nz, cols, plane), BF16)],
        W_OUT * work,
    )
    block = jax.ShapeDtypeStruct((blocks, 1, plane), F32)
    (done,) = kernel_call(hold_kernel, "hold", [small], [last] + terms, weight=W_TOTAL * work)
    output, back = kernel_call(
        functools.partial(total_kernel, nz),
        "total",
        [block, block],
        [done, out_own, out_odd, out_even, *terms],
    )
    return (output, back, weight_grad)


def solution(mesh):
    return jax.shard_map(
        per_device,
        mesh=mesh,
        in_specs=(P("ch", ("grp", "sp"), None), P(None, "ch", None), P("ch", ("grp", "sp"), None)),
        out_specs=(
            P("ch", ("grp", "sp"), None),
            P("ch", ("grp", "sp"), None),
            P("grp", "ch", "sp"),
        ),
        check_vma=False,
    )
```

```python
import functools
import math

import jax
import jax.numpy as jnp
from jax import lax
from jax.experimental import pallas as pl
from jax.experimental.pallas import tpu as pltpu
from jax.sharding import PartitionSpec as P

NX = 64
NY = 10
CELLS = NX * NY
F32 = jnp.float32
BF16 = jnp.bfloat16
W_GATHER, W_EARLY, W_BEGIN, W_GRAD, W_FOLD, W_TOTAL, W_OUT = 2, 2, 8, 1, 0, 1, 0
VMEM_BYTES = 32 * 1024 * 1024


def cell_mask(dy, dx):
    q = lax.broadcasted_iota(jnp.int32, (1, CELLS), 1)
    x = lax.rem(q, NX) + dx
    at = q + NX * dy
    return ((x >= 0) & (x < NX) & (at >= 0) & (at < CELLS)).astype(F32)


def shifted(value, dy, dx):
    if dy == 0 and dx == 0:
        return value
    return pltpu.roll(value, (-(dy * NX + dx)) % CELLS, 1) * cell_mask(dy, dx)


def odd_partner(s, nz):
    return lax.rem(((s + 1) ^ 1) + nz - 1, nz)


def gather_kernel(nz, nc, token_ref, cot_ref, near_ref, *refs):
    pieces, (f_ref, even_ref, odd_ref), packs = refs[:nc], refs[nc : nc + 3], refs[nc + 3 :]
    blocks = cot_ref.shape[0]
    cols = f_ref.shape[0] // nz
    s, c = lax.axis_index("sp"), lax.axis_index("ch")

    def block_for(goal):
        return f_ref[pl.ds(pl.multiple_of(goal * cols, cols), cols), :]

    for k in range(nc):
        f_ref[pl.ds(pl.multiple_of((c ^ k) * blocks, blocks), blocks), :] = pieces[k][...]
    even_ref[:cols, :] = block_for(s ^ 1)
    even_ref[cols:, :] = near_ref[...]
    odd_ref[...] = block_for(odd_partner(s, nz))
    for k, pack in zip(range(2, nz - 1), packs):
        pack[:cols, :] = block_for(lax.rem(s + k, nz))
        if nz > 4:
            pack[cols:, :] = cot_ref[...]


def columns(cols_ref, first, plane):
    blocks = plane.shape[0]
    for dy in (-1, 0, 1):
        for dx in (-1, 0, 1):
            tap = first + 3 * (dy + 1) + dx + 1
            cols_ref[tap * blocks : (tap + 1) * blocks, :] = shifted(plane, -dy, -dx).astype(BF16)


def token_kernel(token_ref):
    token_ref[...] = jnp.zeros(token_ref.shape, F32)


def input_grad_kernel(nz, nc, begin_ref, cot_ref, even_ref, odd_ref, w_ref, *refs):
    parts = refs[:nc]
    token_ref, cols_ref, sum_ref = refs[nc:]
    blocks = even_ref.shape[0]
    s, c = lax.axis_index("sp"), lax.axis_index("ch")
    token_ref[...] = jnp.zeros(token_ref.shape, F32)
    even, odd = even_ref[...].astype(F32), odd_ref[...].astype(F32)
    first = s % 2 == 0
    columns(cols_ref, 0, jnp.where(s < nz - 1, jnp.where(first, even, odd), 0.0))
    columns(cols_ref, 9, cot_ref[...].astype(F32))
    columns(cols_ref, 18, jnp.where(s > 0, jnp.where(first, odd, even), 0.0))
    sum_ref[...] = lax.dot_general(
        w_ref[...], cols_ref[...], (((0,), (0,)), ((), ())), preferred_element_type=F32
    )
    for k in range(nc):
        parts[k][...] = sum_ref[pl.ds(pl.multiple_of((c ^ k) * blocks, blocks), blocks), :]


def conv_part(w_ref, field, dz):
    taps = w_ref.shape[0] // 3
    rows = pl.ds(pl.multiple_of((dz + 1) * taps, taps), taps)
    return jnp.dot(w_ref[rows, :], field, preferred_element_type=F32)


def moved_sum(acc):
    blocks = acc.shape[0] // 9
    total = None
    for dx in (-1, 0, 1):
        for dy in (-1, 0, 1):
            at = (3 * (dy + 1) + dx + 1) * blocks
            term = shifted(acc[at : at + blocks], dy, dx)
            total = term if total is None else total + term
    return total


def moved_rows(plane):
    plane = plane.astype(F32)
    return jnp.concatenate([shifted(plane, -dy, 0).astype(BF16) for dy in (-1, 0, 1)], 0)


def early_kernel(w_ref, f_ref, cot_ref, ce_ref, co_ref, own_ref, even_ref, odd_ref, moved_ref):
    side = 1 - 2 * lax.rem(lax.axis_index("sp"), 2)
    for ref, dz in ((odd_ref, side), (even_ref, -side), (own_ref, 0)):
        ref[...] = moved_sum(conv_part(w_ref, f_ref[...], dz))
    for i, ref in enumerate((cot_ref, ce_ref, co_ref)):
        moved_ref[i] = moved_rows(ref[...])


def weight_grad_kernel(nz, scale, moved_ref, f_ref, ge_ref, go_ref, *refs):
    packs = refs[:-4]
    wg_ref, token_ref, c_ref, g_ref = refs[-4:]
    token_ref[...] = jnp.zeros(token_ref.shape, F32)
    blocks = c_ref.shape[1] // 3
    cols = go_ref.shape[0]
    s = lax.axis_index("sp")

    empty = jnp.zeros(c_ref.shape[1:], BF16)
    c_ref[0] = empty
    c_ref[nz + 1] = empty
    mine = pl.ds(pl.multiple_of(s * cols, cols), cols)
    sources = (s, s ^ 1, odd_partner(s, nz))
    for i, (source, field) in enumerate(zip(sources, (f_ref[mine, :], ge_ref[:cols, :], go_ref[...]))):
        c_ref[source + 1] = moved_ref[i]
        g_ref[source] = field
    for k, pack in zip(range(2, nz - 1), packs):
        source = lax.rem(s + nz - k, nz)
        g_ref[source] = pack[:cols, :]
        c_ref[source + 1] = moved_rows(pack[cols:, :] if nz > 4 else ge_ref[cols:, :])

    sums = None
    for z in range(nz):
        field = g_ref[z].astype(F32)
        fields = jnp.concatenate([shifted(field, 0, dx).astype(BF16) for dx in (-1, 0, 1)], 0)
        term = lax.dot_general(
            c_ref[z : z + 3].reshape(9 * blocks, CELLS),
            fields,
            (((1,), (1,)), ((), ())),
            preferred_element_type=F32,
        )
        sums = term if sums is None else sums + term
    sums = sums * scale
    for tap in range(27):
        dz, dy, dx = tap // 9, tap // 3 % 3, tap % 3
        at = ((2 - dz) * 3 + dy) * blocks
        wg_ref[tap] = sums[at : at + blocks, dx * cols : (dx + 1) * cols]


def fold_kernel(own_ref, got_ref, both_ref):
    both_ref[...] = own_ref[...] + got_ref[...]


def hold_kernel(*refs):
    refs[-1][...] = jnp.zeros(refs[-1].shape, F32)


def total_kernel(nz, token_ref, own_ref, odd_ref, even_ref, *refs):
    terms, (out_ref, back_ref) = refs[:-2], refs[-2:]
    s = lax.axis_index("sp")
    inner = ((s > 0) & (s < nz - 1)).astype(F32)
    out_ref[:, 0, :] = own_ref[...] + even_ref[...] + inner * odd_ref[...]
    total = terms[0][...]
    for term in terms[1:]:
        total = total + term[...]
    back_ref[:, 0, :] = total


VMEM = pl.BlockSpec(memory_space=pltpu.VMEM)
SMEM = pl.BlockSpec(memory_space=pltpu.SMEM)


def kernel_call(body, name, outs, args, scratch=(), weight=0):
    return pl.pallas_call(
        body,
        out_shape=outs,
        in_specs=[SMEM if a.dtype == jnp.int32 else VMEM for a in args],
        out_specs=tuple(VMEM for _ in outs),
        scratch_shapes=list(scratch),
        compiler_params=pltpu.CompilerParams(vmem_limit_bytes=VMEM_BYTES),
        cost_estimate=pl.CostEstimate(flops=int(weight), bytes_accessed=0, transcendentals=0),
        name=name,
    )(*args)


def per_device(features, weights, cotangent):
    blocks, depth, plane = features.shape
    channels = weights.shape[2]
    nz = lax.axis_size("sp")
    nc = lax.axis_size("ch")
    cols = channels // nz
    w2 = weights.reshape(27 * blocks, channels)
    feat = features.reshape(blocks, plane)
    cot = cotangent.reshape(blocks, plane)

    even_pairs = [(i, i ^ 1) for i in range(nz)]
    odd_pairs = [(i, (((i + 1) ^ 1) - 1) % nz) for i in range(nz)]

    def mixed(k):
        return [(i, i ^ k) for i in range(nc)]

    def of(rows, dtype):
        return jax.ShapeDtypeStruct((rows, plane), dtype)

    small = jax.ShapeDtypeStruct((8, 128), F32)
    work = 2 * 27 * blocks * channels * plane

    cot_even = lax.ppermute(cot, "sp", even_pairs)
    cot_odd = lax.ppermute(cot, "sp", odd_pairs)
    (begin,) = kernel_call(token_kernel, "begin", [small], [], weight=W_BEGIN * work)
    feat, begin = lax.optimization_barrier((feat, begin))
    pieces = [feat] + [lax.ppermute(feat, "ch", mixed(k)) for k in range(1, nc)]

    *parts, token = kernel_call(
        functools.partial(input_grad_kernel, nz, nc),
        "input_grad",
        [of(blocks, F32)] * nc + [small],
        [begin, cot, cot_even, cot_odd, w2],
        [pltpu.VMEM((27 * blocks, plane), BF16), pltpu.VMEM((channels, plane), F32)],
        W_GRAD * work,
    )
    terms = [parts[0]]
    for k in range(2, nc, 2):
        got = lax.ppermute(parts[k + 1], "ch", mixed(1))
        (both,) = kernel_call(fold_kernel, "fold", [of(blocks, F32)], [parts[k], got], weight=W_FOLD * work)
        terms.append(lax.ppermute(both, "ch", mixed(k)))
    near, both = lax.optimization_barrier((parts[1], both))
    terms.append(lax.ppermute(near, "ch", mixed(1)))

    far_rows = cols if nz == 4 else cols + blocks
    f_all, to_even, to_odd, *packs = kernel_call(
        functools.partial(gather_kernel, nz, nc),
        "gather",
        [of(channels, BF16), of(cols + blocks, BF16), of(cols, BF16)]
        + [of(far_rows, BF16)] * (nz - 3),
        [token, cot, cot_odd] + pieces,
        weight=W_GATHER * work,
    )
    g_odd = lax.ppermute(to_odd, "sp", odd_pairs)
    far = [
        lax.ppermute(packs[k - 2], "sp", [(i, (i + k) % nz) for i in range(nz)])
        for k in range(2, nz - 1)
    ]
    g_even = lax.ppermute(to_even, "sp", even_pairs)
    out_own, out_even, out_odd, moved = kernel_call(
        early_kernel,
        "early",
        [of(blocks, F32)] * 3 + [jax.ShapeDtypeStruct((3, 3 * blocks, plane), BF16)],
        [w2, f_all, cot, cot_even, cot_odd],
        weight=W_EARLY * work,
    )
    out_odd = lax.ppermute(out_odd, "sp", odd_pairs)
    out_even = lax.ppermute(out_even, "sp", even_pairs)

    weight_grad, last = kernel_call(
        functools.partial(weight_grad_kernel, nz, 1.0 / math.sqrt(nz * depth * plane)),
        "weight_grad",
        [jax.ShapeDtypeStruct((27, blocks, cols), F32), small],
        [moved, f_all, g_even, g_odd, *far],
        [pltpu.VMEM((nz + 2, 3 * blocks, plane), BF16), pltpu.VMEM((nz, cols, plane), BF16)],
        W_OUT * work,
    )
    block = jax.ShapeDtypeStruct((blocks, 1, plane), F32)
    (done,) = kernel_call(hold_kernel, "hold", [small], [last] + terms, weight=W_TOTAL * work)
    output, back = kernel_call(
        functools.partial(total_kernel, nz),
        "total",
        [block, block],
        [done, out_own, out_odd, out_even, *terms],
    )
    return (output, back, weight_grad)


def solution(mesh):
    return jax.shard_map(
        per_device,
        mesh=mesh,
        in_specs=(P("ch", ("grp", "sp"), None), P(None, "ch", None), P("ch", ("grp", "sp"), None)),
        out_specs=(
            P("ch", ("grp", "sp"), None),
            P("ch", ("grp", "sp"), None),
            P("grp", "ch", "sp"),
        ),
        check_vma=False,
    )
```

```python
import functools
import math

import jax
import jax.numpy as jnp
from jax import lax
from jax.experimental import pallas as pl
from jax.experimental.pallas import tpu as pltpu
from jax.sharding import PartitionSpec as P

NX = 64
NY = 10
CELLS = NX * NY
F32 = jnp.float32
BF16 = jnp.bfloat16
W_GATHER, W_EARLY, W_BEGIN, W_GRAD, W_FOLD, W_TOTAL, W_OUT = 2, 2, 8, 1, 0, 1, 0
VMEM_BYTES = 32 * 1024 * 1024


def cell_mask(dy, dx):
    q = lax.broadcasted_iota(jnp.int32, (1, CELLS), 1)
    x = lax.rem(q, NX) + dx
    at = q + NX * dy
    return ((x >= 0) & (x < NX) & (at >= 0) & (at < CELLS)).astype(F32)


def shifted(value, dy, dx):
    if dy == 0 and dx == 0:
        return value
    return pltpu.roll(value, (-(dy * NX + dx)) % CELLS, 1) * cell_mask(dy, dx)


def odd_partner(s, nz):
    return lax.rem(((s + 1) ^ 1) + nz - 1, nz)


def gather_kernel(nz, nc, steps, token_ref, cot_ref, near_ref, *refs):
    pieces, (f_ref, even_ref, odd_ref), packs = refs[:nc], refs[nc : nc + 3], refs[nc + 3 :]
    blocks = cot_ref.shape[0]
    cols = f_ref.shape[0] // nz
    s, c = lax.axis_index("sp"), lax.axis_index("ch")

    def block_for(goal):
        return f_ref[pl.ds(pl.multiple_of(goal * cols, cols), cols), :]

    for k, piece in zip(steps, pieces):
        f_ref[pl.ds(pl.multiple_of((c ^ k) * blocks, blocks), blocks), :] = piece[...]
    even_ref[:cols, :] = block_for(s ^ 1)
    even_ref[cols:, :] = near_ref[...]
    odd_ref[...] = block_for(odd_partner(s, nz))
    for k, pack in zip(range(2, nz - 1), packs):
        pack[:cols, :] = block_for(lax.rem(s + k, nz))
        if nz > 4:
            pack[cols:, :] = cot_ref[...]


def columns(cols_ref, first, plane):
    blocks = plane.shape[0]
    for dy in (-1, 0, 1):
        for dx in (-1, 0, 1):
            tap = first + 3 * (dy + 1) + dx + 1
            cols_ref[tap * blocks : (tap + 1) * blocks, :] = shifted(plane, -dy, -dx).astype(BF16)


def token_kernel(token_ref):
    token_ref[...] = jnp.zeros(token_ref.shape, F32)


def input_grad_kernel(nz, nc, begin_ref, cot_ref, even_ref, odd_ref, w_ref, *refs):
    parts = refs[:nc]
    token_ref, cols_ref, sum_ref = refs[nc:]
    blocks = even_ref.shape[0]
    s, c = lax.axis_index("sp"), lax.axis_index("ch")
    token_ref[...] = jnp.zeros(token_ref.shape, F32)
    even, odd = even_ref[...].astype(F32), odd_ref[...].astype(F32)
    first = s % 2 == 0
    columns(cols_ref, 0, jnp.where(s < nz - 1, jnp.where(first, even, odd), 0.0))
    columns(cols_ref, 9, cot_ref[...].astype(F32))
    columns(cols_ref, 18, jnp.where(s > 0, jnp.where(first, odd, even), 0.0))
    sum_ref[...] = lax.dot_general(
        w_ref[...], cols_ref[...], (((0,), (0,)), ((), ())), preferred_element_type=F32
    )
    for k in range(nc):
        parts[k][...] = sum_ref[pl.ds(pl.multiple_of((c ^ k) * blocks, blocks), blocks), :]


def conv_part(w_ref, field, dz):
    taps = w_ref.shape[0] // 3
    rows = pl.ds(pl.multiple_of((dz + 1) * taps, taps), taps)
    return jnp.dot(w_ref[rows, :], field, preferred_element_type=F32)


def moved_sum(acc):
    blocks = acc.shape[0] // 9
    total = None
    for dx in (-1, 0, 1):
        for dy in (-1, 0, 1):
            at = (3 * (dy + 1) + dx + 1) * blocks
            term = shifted(acc[at : at + blocks], dy, dx)
            total = term if total is None else total + term
    return total


def moved_rows(plane):
    plane = plane.astype(F32)
    return jnp.concatenate([shifted(plane, -dy, 0).astype(BF16) for dy in (-1, 0, 1)], 0)


def early_kernel(w_ref, f_ref, cot_ref, ce_ref, co_ref, own_ref, even_ref, odd_ref, moved_ref):
    side = 1 - 2 * lax.rem(lax.axis_index("sp"), 2)
    for ref, dz in ((odd_ref, side), (even_ref, -side), (own_ref, 0)):
        ref[...] = moved_sum(conv_part(w_ref, f_ref[...], dz))
    for i, ref in enumerate((cot_ref, ce_ref, co_ref)):
        moved_ref[i] = moved_rows(ref[...])


def weight_grad_kernel(nz, scale, moved_ref, f_ref, ge_ref, go_ref, *refs):
    packs = refs[:-4]
    wg_ref, token_ref, c_ref, g_ref = refs[-4:]
    token_ref[...] = jnp.zeros(token_ref.shape, F32)
    blocks = c_ref.shape[1] // 3
    cols = go_ref.shape[0]
    s = lax.axis_index("sp")

    empty = jnp.zeros(c_ref.shape[1:], BF16)
    c_ref[0] = empty
    c_ref[nz + 1] = empty
    mine = pl.ds(pl.multiple_of(s * cols, cols), cols)
    sources = (s, s ^ 1, odd_partner(s, nz))
    for i, (source, field) in enumerate(zip(sources, (f_ref[mine, :], ge_ref[:cols, :], go_ref[...]))):
        c_ref[source + 1] = moved_ref[i]
        g_ref[source] = field
    for k, pack in zip(range(2, nz - 1), packs):
        source = lax.rem(s + nz - k, nz)
        g_ref[source] = pack[:cols, :]
        c_ref[source + 1] = moved_rows(pack[cols:, :] if nz > 4 else ge_ref[cols:, :])

    sums = None
    for z in range(nz):
        field = g_ref[z].astype(F32)
        fields = jnp.concatenate([shifted(field, 0, dx).astype(BF16) for dx in (-1, 0, 1)], 0)
        term = lax.dot_general(
            c_ref[z : z + 3].reshape(9 * blocks, CELLS),
            fields,
            (((1,), (1,)), ((), ())),
            preferred_element_type=F32,
        )
        sums = term if sums is None else sums + term
    sums = sums * scale
    for tap in range(27):
        dz, dy, dx = tap // 9, tap // 3 % 3, tap % 3
        at = ((2 - dz) * 3 + dy) * blocks
        wg_ref[tap] = sums[at : at + blocks, dx * cols : (dx + 1) * cols]


def fold_kernel(own_ref, got_ref, both_ref):
    both_ref[...] = own_ref[...] + got_ref[...]


def hold_kernel(*refs):
    refs[-1][...] = jnp.zeros(refs[-1].shape, F32)


def total_kernel(nz, token_ref, own_ref, odd_ref, even_ref, *refs):
    terms, (out_ref, back_ref) = refs[:-2], refs[-2:]
    s = lax.axis_index("sp")
    inner = ((s > 0) & (s < nz - 1)).astype(F32)
    out_ref[:, 0, :] = own_ref[...] + even_ref[...] + inner * odd_ref[...]
    total = terms[0][...]
    for term in terms[1:]:
        total = total + term[...]
    back_ref[:, 0, :] = total


VMEM = pl.BlockSpec(memory_space=pltpu.VMEM)
SMEM = pl.BlockSpec(memory_space=pltpu.SMEM)


def kernel_call(body, name, outs, args, scratch=(), weight=0):
    return pl.pallas_call(
        body,
        out_shape=outs,
        in_specs=[SMEM if a.dtype == jnp.int32 else VMEM for a in args],
        out_specs=tuple(VMEM for _ in outs),
        scratch_shapes=list(scratch),
        compiler_params=pltpu.CompilerParams(vmem_limit_bytes=VMEM_BYTES),
        cost_estimate=pl.CostEstimate(flops=int(weight), bytes_accessed=0, transcendentals=0),
        name=name,
    )(*args)


def per_device(features, weights, cotangent):
    blocks, depth, plane = features.shape
    channels = weights.shape[2]
    nz = lax.axis_size("sp")
    nc = lax.axis_size("ch")
    cols = channels // nz
    w2 = weights.reshape(27 * blocks, channels)
    feat = features.reshape(blocks, plane)
    cot = cotangent.reshape(blocks, plane)

    even_pairs = [(i, i ^ 1) for i in range(nz)]
    odd_pairs = [(i, (((i + 1) ^ 1) - 1) % nz) for i in range(nz)]

    def mixed(k):
        return [(i, i ^ k) for i in range(nc)]

    def of(rows, dtype):
        return jax.ShapeDtypeStruct((rows, plane), dtype)

    small = jax.ShapeDtypeStruct((8, 128), F32)
    work = 2 * 27 * blocks * channels * plane

    cot_even = lax.ppermute(cot, "sp", even_pairs)
    cot_odd = lax.ppermute(cot, "sp", odd_pairs)
    (begin,) = kernel_call(token_kernel, "begin", [small], [], weight=W_BEGIN * work)
    feat, begin = lax.optimization_barrier((feat, begin))
    steps = (0, 1, *range(nc - 1, 1, -1))
    pieces = [feat] + [lax.ppermute(feat, "ch", mixed(k)) for k in steps[1:]]

    *parts, token = kernel_call(
        functools.partial(input_grad_kernel, nz, nc),
        "input_grad",
        [of(blocks, F32)] * nc + [small],
        [begin, cot, cot_even, cot_odd, w2],
        [pltpu.VMEM((27 * blocks, plane), BF16), pltpu.VMEM((channels, plane), F32)],
        W_GRAD * work,
    )
    terms = [parts[0]]
    for k in range(2, nc, 2):
        got = lax.ppermute(parts[k + 1], "ch", mixed(1))
        (both,) = kernel_call(fold_kernel, "fold", [of(blocks, F32)], [parts[k], got], weight=W_FOLD * work)
        terms.append(lax.ppermute(both, "ch", mixed(k)))
    terms.append(lax.ppermute(parts[1], "ch", mixed(1)))

    far_rows = cols if nz == 4 else cols + blocks
    f_all, to_even, to_odd, *packs = kernel_call(
        functools.partial(gather_kernel, nz, nc, steps),
        "gather",
        [of(channels, BF16), of(cols + blocks, BF16), of(cols, BF16)]
        + [of(far_rows, BF16)] * (nz - 3),
        [token, cot, cot_odd] + pieces,
        weight=W_GATHER * work,
    )
    g_odd = lax.ppermute(to_odd, "sp", odd_pairs)
    far = [
        lax.ppermute(packs[k - 2], "sp", [(i, (i + k) % nz) for i in range(nz)])
        for k in range(2, nz - 1)
    ]
    g_even = lax.ppermute(to_even, "sp", even_pairs)
    out_own, out_even, out_odd, moved = kernel_call(
        early_kernel,
        "early",
        [of(blocks, F32)] * 3 + [jax.ShapeDtypeStruct((3, 3 * blocks, plane), BF16)],
        [w2, f_all, cot, cot_even, cot_odd],
        weight=W_EARLY * work,
    )
    out_odd = lax.ppermute(out_odd, "sp", odd_pairs)
    out_even = lax.ppermute(out_even, "sp", even_pairs)

    weight_grad, last = kernel_call(
        functools.partial(weight_grad_kernel, nz, 1.0 / math.sqrt(nz * depth * plane)),
        "weight_grad",
        [jax.ShapeDtypeStruct((27, blocks, cols), F32), small],
        [moved, f_all, g_even, g_odd, *far],
        [pltpu.VMEM((nz + 2, 3 * blocks, plane), BF16), pltpu.VMEM((nz, cols, plane), BF16)],
        W_OUT * work,
    )
    block = jax.ShapeDtypeStruct((blocks, 1, plane), F32)
    (done,) = kernel_call(hold_kernel, "hold", [small], [last] + terms, weight=W_TOTAL * work)
    output, back = kernel_call(
        functools.partial(total_kernel, nz),
        "total",
        [block, block],
        [done, out_own, out_odd, out_even, *terms],
    )
    return (output, back, weight_grad)


def solution(mesh):
    return jax.shard_map(
        per_device,
        mesh=mesh,
        in_specs=(P("ch", ("grp", "sp"), None), P(None, "ch", None), P("ch", ("grp", "sp"), None)),
        out_specs=(
            P("ch", ("grp", "sp"), None),
            P("ch", ("grp", "sp"), None),
            P("grp", "ch", "sp"),
        ),
        check_vma=False,
    )
```

```python
import functools
import math

import jax
import jax.numpy as jnp
from jax import lax
from jax.experimental import pallas as pl
from jax.experimental.pallas import tpu as pltpu
from jax.sharding import PartitionSpec as P

NX = 64
NY = 10
CELLS = NX * NY
F32 = jnp.float32
BF16 = jnp.bfloat16
W_GATHER, W_EARLY, W_BEGIN, W_GRAD, W_FOLD, W_TOTAL, W_OUT = 2, 2, 8, 1, 0, 1, 0
VMEM_BYTES = 32 * 1024 * 1024


def cell_mask(dy, dx):
    q = lax.broadcasted_iota(jnp.int32, (1, CELLS), 1)
    x = lax.rem(q, NX) + dx
    at = q + NX * dy
    return ((x >= 0) & (x < NX) & (at >= 0) & (at < CELLS)).astype(F32)


def shifted(value, dy, dx):
    if dy == 0 and dx == 0:
        return value
    return pltpu.roll(value, (-(dy * NX + dx)) % CELLS, 1) * cell_mask(dy, dx)


def odd_partner(s, nz):
    return lax.rem(((s + 1) ^ 1) + nz - 1, nz)


def gather_kernel(nz, nc, token_ref, cot_ref, near_ref, *refs):
    pieces, (f_ref, even_ref, odd_ref), packs = refs[:nc], refs[nc : nc + 3], refs[nc + 3 :]
    blocks = cot_ref.shape[0]
    cols = f_ref.shape[0] // nz
    s, c = lax.axis_index("sp"), lax.axis_index("ch")

    def block_for(goal):
        return f_ref[pl.ds(pl.multiple_of(goal * cols, cols), cols), :]

    for k in range(nc):
        f_ref[pl.ds(pl.multiple_of((c ^ k) * blocks, blocks), blocks), :] = pieces[k][...]
    even_ref[:cols, :] = block_for(s ^ 1)
    even_ref[cols:, :] = near_ref[...]
    odd_ref[...] = block_for(odd_partner(s, nz))
    for k, pack in zip(range(2, nz - 1), packs):
        pack[:cols, :] = block_for(lax.rem(s + k, nz))
        if nz > 4:
            pack[cols:, :] = cot_ref[...]


def columns(cols_ref, first, plane):
    blocks = plane.shape[0]
    for dy in (-1, 0, 1):
        for dx in (-1, 0, 1):
            tap = first + 3 * (dy + 1) + dx + 1
            cols_ref[tap * blocks : (tap + 1) * blocks, :] = shifted(plane, -dy, -dx).astype(BF16)


def token_kernel(token_ref):
    token_ref[...] = jnp.zeros(token_ref.shape, F32)


def input_grad_kernel(nz, nc, begin_ref, cot_ref, even_ref, odd_ref, w_ref, *refs):
    parts = refs[:nc]
    token_ref, cols_ref, sum_ref = refs[nc:]
    blocks = even_ref.shape[0]
    s, c = lax.axis_index("sp"), lax.axis_index("ch")
    token_ref[...] = jnp.zeros(token_ref.shape, F32)
    even, odd = even_ref[...].astype(F32), odd_ref[...].astype(F32)
    first = s % 2 == 0
    columns(cols_ref, 0, jnp.where(s < nz - 1, jnp.where(first, even, odd), 0.0))
    columns(cols_ref, 9, cot_ref[...].astype(F32))
    columns(cols_ref, 18, jnp.where(s > 0, jnp.where(first, odd, even), 0.0))
    sum_ref[...] = lax.dot_general(
        w_ref[...], cols_ref[...], (((0,), (0,)), ((), ())), preferred_element_type=F32
    )
    for k in range(nc):
        parts[k][...] = sum_ref[pl.ds(pl.multiple_of((c ^ k) * blocks, blocks), blocks), :]


def conv_part(w_ref, field, dz):
    taps = w_ref.shape[0] // 3
    rows = pl.ds(pl.multiple_of((dz + 1) * taps, taps), taps)
    return jnp.dot(w_ref[rows, :], field, preferred_element_type=F32)


def moved_sum(acc):
    blocks = acc.shape[0] // 9
    total = None
    for dx in (-1, 0, 1):
        for dy in (-1, 0, 1):
            at = (3 * (dy + 1) + dx + 1) * blocks
            term = shifted(acc[at : at + blocks], dy, dx)
            total = term if total is None else total + term
    return total


def moved_rows(plane):
    plane = plane.astype(F32)
    return jnp.concatenate([shifted(plane, -dy, 0).astype(BF16) for dy in (-1, 0, 1)], 0)


def odd_kernel(w_ref, f_ref, odd_ref):
    side = 1 - 2 * lax.rem(lax.axis_index("sp"), 2)
    odd_ref[...] = moved_sum(conv_part(w_ref, f_ref[...], side))


def early_kernel(after_ref, w_ref, f_ref, cot_ref, ce_ref, co_ref, own_ref, even_ref, moved_ref):
    side = 1 - 2 * lax.rem(lax.axis_index("sp"), 2)
    for ref, dz in ((even_ref, -side), (own_ref, 0)):
        ref[...] = moved_sum(conv_part(w_ref, f_ref[...], dz))
    for i, ref in enumerate((cot_ref, ce_ref, co_ref)):
        moved_ref[i] = moved_rows(ref[...])


def weight_grad_kernel(nz, scale, moved_ref, f_ref, ge_ref, go_ref, *refs):
    packs = refs[:-4]
    wg_ref, token_ref, c_ref, g_ref = refs[-4:]
    token_ref[...] = jnp.zeros(token_ref.shape, F32)
    blocks = c_ref.shape[1] // 3
    cols = go_ref.shape[0]
    s = lax.axis_index("sp")

    empty = jnp.zeros(c_ref.shape[1:], BF16)
    c_ref[0] = empty
    c_ref[nz + 1] = empty
    mine = pl.ds(pl.multiple_of(s * cols, cols), cols)
    sources = (s, s ^ 1, odd_partner(s, nz))
    for i, (source, field) in enumerate(zip(sources, (f_ref[mine, :], ge_ref[:cols, :], go_ref[...]))):
        c_ref[source + 1] = moved_ref[i]
        g_ref[source] = field
    for k, pack in zip(range(2, nz - 1), packs):
        source = lax.rem(s + nz - k, nz)
        g_ref[source] = pack[:cols, :]
        c_ref[source + 1] = moved_rows(pack[cols:, :] if nz > 4 else ge_ref[cols:, :])

    sums = None
    for z in range(nz):
        field = g_ref[z].astype(F32)
        fields = jnp.concatenate([shifted(field, 0, dx).astype(BF16) for dx in (-1, 0, 1)], 0)
        term = lax.dot_general(
            c_ref[z : z + 3].reshape(9 * blocks, CELLS),
            fields,
            (((1,), (1,)), ((), ())),
            preferred_element_type=F32,
        )
        sums = term if sums is None else sums + term
    sums = sums * scale
    for tap in range(27):
        dz, dy, dx = tap // 9, tap // 3 % 3, tap % 3
        at = ((2 - dz) * 3 + dy) * blocks
        wg_ref[tap] = sums[at : at + blocks, dx * cols : (dx + 1) * cols]


def fold_kernel(own_ref, got_ref, both_ref):
    both_ref[...] = own_ref[...] + got_ref[...]


def hold_kernel(*refs):
    refs[-1][...] = jnp.zeros(refs[-1].shape, F32)


def total_kernel(nz, token_ref, own_ref, odd_ref, even_ref, *refs):
    terms, (out_ref, back_ref) = refs[:-2], refs[-2:]
    s = lax.axis_index("sp")
    inner = ((s > 0) & (s < nz - 1)).astype(F32)
    out_ref[:, 0, :] = own_ref[...] + even_ref[...] + inner * odd_ref[...]
    total = terms[0][...]
    for term in terms[1:]:
        total = total + term[...]
    back_ref[:, 0, :] = total


VMEM = pl.BlockSpec(memory_space=pltpu.VMEM)
SMEM = pl.BlockSpec(memory_space=pltpu.SMEM)


def kernel_call(body, name, outs, args, scratch=(), weight=0):
    return pl.pallas_call(
        body,
        out_shape=outs,
        in_specs=[SMEM if a.dtype == jnp.int32 else VMEM for a in args],
        out_specs=tuple(VMEM for _ in outs),
        scratch_shapes=list(scratch),
        compiler_params=pltpu.CompilerParams(vmem_limit_bytes=VMEM_BYTES),
        cost_estimate=pl.CostEstimate(flops=int(weight), bytes_accessed=0, transcendentals=0),
        name=name,
    )(*args)


def per_device(features, weights, cotangent):
    blocks, depth, plane = features.shape
    channels = weights.shape[2]
    nz = lax.axis_size("sp")
    nc = lax.axis_size("ch")
    cols = channels // nz
    w2 = weights.reshape(27 * blocks, channels)
    feat = features.reshape(blocks, plane)
    cot = cotangent.reshape(blocks, plane)

    even_pairs = [(i, i ^ 1) for i in range(nz)]
    odd_pairs = [(i, (((i + 1) ^ 1) - 1) % nz) for i in range(nz)]

    def mixed(k):
        return [(i, i ^ k) for i in range(nc)]

    def of(rows, dtype):
        return jax.ShapeDtypeStruct((rows, plane), dtype)

    small = jax.ShapeDtypeStruct((8, 128), F32)
    work = 2 * 27 * blocks * channels * plane

    cot_even = lax.ppermute(cot, "sp", even_pairs)
    cot_odd = lax.ppermute(cot, "sp", odd_pairs)
    (begin,) = kernel_call(token_kernel, "begin", [small], [], weight=W_BEGIN * work)
    feat, begin = lax.optimization_barrier((feat, begin))
    pieces = [feat] + [lax.ppermute(feat, "ch", mixed(k)) for k in range(1, nc)]

    *parts, token = kernel_call(
        functools.partial(input_grad_kernel, nz, nc),
        "input_grad",
        [of(blocks, F32)] * nc + [small],
        [begin, cot, cot_even, cot_odd, w2],
        [pltpu.VMEM((27 * blocks, plane), BF16), pltpu.VMEM((channels, plane), F32)],
        W_GRAD * work,
    )
    terms = [parts[0]]
    for k in range(2, nc, 2):
        got = lax.ppermute(parts[k + 1], "ch", mixed(1))
        (both,) = kernel_call(fold_kernel, "fold", [of(blocks, F32)], [parts[k], got], weight=W_FOLD * work)
        terms.append(lax.ppermute(both, "ch", mixed(k)))
    near, both = lax.optimization_barrier((parts[1], both))
    terms.append(lax.ppermute(near, "ch", mixed(1)))

    far_rows = cols if nz == 4 else cols + blocks
    f_all, to_even, to_odd, *packs = kernel_call(
        functools.partial(gather_kernel, nz, nc),
        "gather",
        [of(channels, BF16), of(cols + blocks, BF16), of(cols, BF16)]
        + [of(far_rows, BF16)] * (nz - 3),
        [token, cot, cot_odd] + pieces,
        weight=W_GATHER * work,
    )
    g_odd = lax.ppermute(to_odd, "sp", odd_pairs)
    far = [
        lax.ppermute(packs[k - 2], "sp", [(i, (i + k) % nz) for i in range(nz)])
        for k in range(2, nz - 1)
    ]
    g_even = lax.ppermute(to_even, "sp", even_pairs)
    (out_odd,) = kernel_call(odd_kernel, "odd", [of(blocks, F32)], [w2, f_all], weight=W_EARLY * work)
    out_own, out_even, moved = kernel_call(
        early_kernel,
        "early",
        [of(blocks, F32)] * 2 + [jax.ShapeDtypeStruct((3, 3 * blocks, plane), BF16)],
        [g_odd, w2, f_all, cot, cot_even, cot_odd],
        weight=W_EARLY * work,
    )
    out_odd = lax.ppermute(out_odd, "sp", odd_pairs)
    out_even = lax.ppermute(out_even, "sp", even_pairs)

    weight_grad, last = kernel_call(
        functools.partial(weight_grad_kernel, nz, 1.0 / math.sqrt(nz * depth * plane)),
        "weight_grad",
        [jax.ShapeDtypeStruct((27, blocks, cols), F32), small],
        [moved, f_all, g_even, g_odd, *far],
        [pltpu.VMEM((nz + 2, 3 * blocks, plane), BF16), pltpu.VMEM((nz, cols, plane), BF16)],
        W_OUT * work,
    )
    block = jax.ShapeDtypeStruct((blocks, 1, plane), F32)
    (done,) = kernel_call(hold_kernel, "hold", [small], [last] + terms, weight=W_TOTAL * work)
    output, back = kernel_call(
        functools.partial(total_kernel, nz),
        "total",
        [block, block],
        [done, out_own, out_odd, out_even, *terms],
    )
    return (output, back, weight_grad)


def solution(mesh):
    return jax.shard_map(
        per_device,
        mesh=mesh,
        in_specs=(P("ch", ("grp", "sp"), None), P(None, "ch", None), P("ch", ("grp", "sp"), None)),
        out_specs=(
            P("ch", ("grp", "sp"), None),
            P("ch", ("grp", "sp"), None),
            P("grp", "ch", "sp"),
        ),
        check_vma=False,
    )
```

```python
import functools
import math

import jax
import jax.numpy as jnp
from jax import lax
from jax.experimental import pallas as pl
from jax.experimental.pallas import tpu as pltpu
from jax.sharding import PartitionSpec as P

NX = 64
NY = 10
CELLS = NX * NY
F32 = jnp.float32
BF16 = jnp.bfloat16
W_GATHER, W_EARLY, W_BEGIN, W_GRAD, W_FOLD, W_TOTAL, W_OUT = 2, 2, 8, 1, 0, 1, 0
VMEM_BYTES = 32 * 1024 * 1024


def cell_mask(dy, dx):
    q = lax.broadcasted_iota(jnp.int32, (1, CELLS), 1)
    x = lax.rem(q, NX) + dx
    at = q + NX * dy
    return ((x >= 0) & (x < NX) & (at >= 0) & (at < CELLS)).astype(F32)


def shifted(value, dy, dx):
    if dy == 0 and dx == 0:
        return value
    return pltpu.roll(value, (-(dy * NX + dx)) % CELLS, 1) * cell_mask(dy, dx)


def odd_partner(s, nz):
    return lax.rem(((s + 1) ^ 1) + nz - 1, nz)


def gather_kernel(nz, nc, token_ref, cot_ref, near_ref, *refs):
    pieces, (f_ref, even_ref, odd_ref), packs = refs[:nc], refs[nc : nc + 3], refs[nc + 3 :]
    blocks = cot_ref.shape[0]
    cols = f_ref.shape[0] // nz
    s, c = lax.axis_index("sp"), lax.axis_index("ch")

    def block_for(goal):
        return f_ref[pl.ds(pl.multiple_of(goal * cols, cols), cols), :]

    for k in range(nc):
        f_ref[pl.ds(pl.multiple_of((c ^ k) * blocks, blocks), blocks), :] = pieces[k][...]
    even_ref[:cols, :] = block_for(s ^ 1)
    even_ref[cols:, :] = near_ref[...]
    odd_ref[...] = block_for(odd_partner(s, nz))
    for k, pack in zip(range(2, nz - 1), packs):
        pack[:cols, :] = block_for(lax.rem(s + k, nz))
        if nz > 4:
            pack[cols:, :] = cot_ref[...]


def columns(cols_ref, first, plane):
    blocks = plane.shape[0]
    for dy in (-1, 0, 1):
        for dx in (-1, 0, 1):
            tap = first + 3 * (dy + 1) + dx + 1
            cols_ref[tap * blocks : (tap + 1) * blocks, :] = shifted(plane, -dy, -dx).astype(BF16)


def token_kernel(token_ref):
    token_ref[...] = jnp.zeros(token_ref.shape, F32)


def input_grad_kernel(nz, nc, begin_ref, cot_ref, even_ref, odd_ref, w_ref, *refs):
    parts = refs[:nc]
    token_ref, cols_ref, sum_ref = refs[nc:]
    blocks = even_ref.shape[0]
    s, c = lax.axis_index("sp"), lax.axis_index("ch")
    token_ref[...] = jnp.zeros(token_ref.shape, F32)
    even, odd = even_ref[...].astype(F32), odd_ref[...].astype(F32)
    first = s % 2 == 0
    columns(cols_ref, 0, jnp.where(s < nz - 1, jnp.where(first, even, odd), 0.0))
    columns(cols_ref, 9, cot_ref[...].astype(F32))
    columns(cols_ref, 18, jnp.where(s > 0, jnp.where(first, odd, even), 0.0))
    sum_ref[...] = lax.dot_general(
        w_ref[...], cols_ref[...], (((0,), (0,)), ((), ())), preferred_element_type=F32
    )
    for k in range(nc):
        parts[k][...] = sum_ref[pl.ds(pl.multiple_of((c ^ k) * blocks, blocks), blocks), :]


def conv_part(w_ref, field, dz):
    taps = w_ref.shape[0] // 3
    rows = pl.ds(pl.multiple_of((dz + 1) * taps, taps), taps)
    return jnp.dot(w_ref[rows, :], field, preferred_element_type=F32)


def moved_sum(acc):
    blocks = acc.shape[0] // 9
    total = None
    for dx in (-1, 0, 1):
        for dy in (-1, 0, 1):
            at = (3 * (dy + 1) + dx + 1) * blocks
            term = shifted(acc[at : at + blocks], dy, dx)
            total = term if total is None else total + term
    return total


def moved_rows(plane):
    plane = plane.astype(F32)
    return jnp.concatenate([shifted(plane, -dy, 0).astype(BF16) for dy in (-1, 0, 1)], 0)


def odd_kernel(w_ref, f_ref, odd_ref):
    side = 1 - 2 * lax.rem(lax.axis_index("sp"), 2)
    odd_ref[...] = moved_sum(conv_part(w_ref, f_ref[...], side))


def early_kernel(after_ref, w_ref, f_ref, cot_ref, ce_ref, co_ref, own_ref, even_ref, moved_ref):
    side = 1 - 2 * lax.rem(lax.axis_index("sp"), 2)
    for ref, dz in ((even_ref, -side), (own_ref, 0)):
        ref[...] = moved_sum(conv_part(w_ref, f_ref[...], dz))
    for i, ref in enumerate((cot_ref, ce_ref, co_ref)):
        moved_ref[i] = moved_rows(ref[...])


def weight_grad_kernel(nz, scale, moved_ref, f_ref, ge_ref, go_ref, *refs):
    packs = refs[:-4]
    wg_ref, token_ref, c_ref, g_ref = refs[-4:]
    token_ref[...] = jnp.zeros(token_ref.shape, F32)
    blocks = c_ref.shape[1] // 3
    cols = go_ref.shape[0]
    s = lax.axis_index("sp")

    empty = jnp.zeros(c_ref.shape[1:], BF16)
    c_ref[0] = empty
    c_ref[nz + 1] = empty
    mine = pl.ds(pl.multiple_of(s * cols, cols), cols)
    sources = (s, s ^ 1, odd_partner(s, nz))
    for i, (source, field) in enumerate(zip(sources, (f_ref[mine, :], ge_ref[:cols, :], go_ref[...]))):
        c_ref[source + 1] = moved_ref[i]
        g_ref[source] = field
    for k, pack in zip(range(2, nz - 1), packs):
        source = lax.rem(s + nz - k, nz)
        g_ref[source] = pack[:cols, :]
        c_ref[source + 1] = moved_rows(pack[cols:, :] if nz > 4 else ge_ref[cols:, :])

    sums = None
    for z in range(nz):
        field = g_ref[z].astype(F32)
        fields = jnp.concatenate([shifted(field, 0, dx).astype(BF16) for dx in (-1, 0, 1)], 0)
        term = lax.dot_general(
            c_ref[z : z + 3].reshape(9 * blocks, CELLS),
            fields,
            (((1,), (1,)), ((), ())),
            preferred_element_type=F32,
        )
        sums = term if sums is None else sums + term
    sums = sums * scale
    for tap in range(27):
        dz, dy, dx = tap // 9, tap // 3 % 3, tap % 3
        at = ((2 - dz) * 3 + dy) * blocks
        wg_ref[tap] = sums[at : at + blocks, dx * cols : (dx + 1) * cols]


def fold_kernel(own_ref, got_ref, both_ref):
    both_ref[...] = own_ref[...] + got_ref[...]


def hold_kernel(*refs):
    refs[-1][...] = jnp.zeros(refs[-1].shape, F32)


def total_kernel(nz, token_ref, own_ref, odd_ref, even_ref, *refs):
    terms, (out_ref, back_ref) = refs[:-2], refs[-2:]
    s = lax.axis_index("sp")
    inner = ((s > 0) & (s < nz - 1)).astype(F32)
    out_ref[:, 0, :] = own_ref[...] + even_ref[...] + inner * odd_ref[...]
    total = terms[0][...]
    for term in terms[1:]:
        total = total + term[...]
    back_ref[:, 0, :] = total


VMEM = pl.BlockSpec(memory_space=pltpu.VMEM)
SMEM = pl.BlockSpec(memory_space=pltpu.SMEM)


def kernel_call(body, name, outs, args, scratch=(), weight=0):
    return pl.pallas_call(
        body,
        out_shape=outs,
        in_specs=[SMEM if a.dtype == jnp.int32 else VMEM for a in args],
        out_specs=tuple(VMEM for _ in outs),
        scratch_shapes=list(scratch),
        compiler_params=pltpu.CompilerParams(vmem_limit_bytes=VMEM_BYTES),
        cost_estimate=pl.CostEstimate(flops=int(weight), bytes_accessed=0, transcendentals=0),
        name=name,
    )(*args)


def per_device(features, weights, cotangent):
    blocks, depth, plane = features.shape
    channels = weights.shape[2]
    nz = lax.axis_size("sp")
    nc = lax.axis_size("ch")
    cols = channels // nz
    w2 = weights.reshape(27 * blocks, channels)
    feat = features.reshape(blocks, plane)
    cot = cotangent.reshape(blocks, plane)

    even_pairs = [(i, i ^ 1) for i in range(nz)]
    odd_pairs = [(i, (((i + 1) ^ 1) - 1) % nz) for i in range(nz)]

    def mixed(k):
        return [(i, i ^ k) for i in range(nc)]

    def of(rows, dtype):
        return jax.ShapeDtypeStruct((rows, plane), dtype)

    small = jax.ShapeDtypeStruct((8, 128), F32)
    work = 2 * 27 * blocks * channels * plane

    cot_even = lax.ppermute(cot, "sp", even_pairs)
    cot_odd = lax.ppermute(cot, "sp", odd_pairs)
    (begin,) = kernel_call(token_kernel, "begin", [small], [], weight=W_BEGIN * work)
    feat, begin = lax.optimization_barrier((feat, begin))
    pieces = [feat] + [lax.ppermute(feat, "ch", mixed(k)) for k in range(1, nc)]

    *parts, token = kernel_call(
        functools.partial(input_grad_kernel, nz, nc),
        "input_grad",
        [of(blocks, F32)] * nc + [small],
        [begin, cot, cot_even, cot_odd, w2],
        [pltpu.VMEM((27 * blocks, plane), BF16), pltpu.VMEM((channels, plane), F32)],
        W_GRAD * work,
    )
    terms = [parts[0]]
    for k in range(2, nc, 2):
        got = lax.ppermute(parts[k + 1], "ch", mixed(1))
        (both,) = kernel_call(fold_kernel, "fold", [of(blocks, F32)], [parts[k], got], weight=W_FOLD * work)
        terms.append(lax.ppermute(both, "ch", mixed(k)))
    terms.append(lax.ppermute(parts[1], "ch", mixed(1)))

    far_rows = cols if nz == 4 else cols + blocks
    f_all, to_even, to_odd, *packs = kernel_call(
        functools.partial(gather_kernel, nz, nc),
        "gather",
        [of(channels, BF16), of(cols + blocks, BF16), of(cols, BF16)]
        + [of(far_rows, BF16)] * (nz - 3),
        [token, cot, cot_odd] + pieces,
        weight=W_GATHER * work,
    )
    g_odd = lax.ppermute(to_odd, "sp", odd_pairs)
    far = [
        lax.ppermute(packs[k - 2], "sp", [(i, (i + k) % nz) for i in range(nz)])
        for k in range(2, nz - 1)
    ]
    g_even = lax.ppermute(to_even, "sp", even_pairs)
    (out_odd,) = kernel_call(odd_kernel, "odd", [of(blocks, F32)], [w2, f_all], weight=W_EARLY * work)
    out_own, out_even, moved = kernel_call(
        early_kernel,
        "early",
        [of(blocks, F32)] * 2 + [jax.ShapeDtypeStruct((3, 3 * blocks, plane), BF16)],
        [g_odd, w2, f_all, cot, cot_even, cot_odd],
        weight=W_EARLY * work,
    )
    out_odd = lax.ppermute(out_odd, "sp", odd_pairs)
    out_even = lax.ppermute(out_even, "sp", even_pairs)

    weight_grad, last = kernel_call(
        functools.partial(weight_grad_kernel, nz, 1.0 / math.sqrt(nz * depth * plane)),
        "weight_grad",
        [jax.ShapeDtypeStruct((27, blocks, cols), F32), small],
        [moved, f_all, g_even, g_odd, *far],
        [pltpu.VMEM((nz + 2, 3 * blocks, plane), BF16), pltpu.VMEM((nz, cols, plane), BF16)],
        W_OUT * work,
    )
    block = jax.ShapeDtypeStruct((blocks, 1, plane), F32)
    (done,) = kernel_call(hold_kernel, "hold", [small], [last] + terms, weight=W_TOTAL * work)
    output, back = kernel_call(
        functools.partial(total_kernel, nz),
        "total",
        [block, block],
        [done, out_own, out_odd, out_even, *terms],
    )
    return (output, back, weight_grad)


def solution(mesh):
    return jax.shard_map(
        per_device,
        mesh=mesh,
        in_specs=(P("ch", ("grp", "sp"), None), P(None, "ch", None), P("ch", ("grp", "sp"), None)),
        out_specs=(
            P("ch", ("grp", "sp"), None),
            P("ch", ("grp", "sp"), None),
            P("grp", "ch", "sp"),
        ),
        check_vma=False,
    )
```
